32 devices in a mesh: dp: 8 (over z, y), tensor: 4 (over x, core).
Axes of the slice: x: 2, y: 2, z: 4, core: 2. Of those that a mesh axis runs over, the one named last changes fastest.
Arguments:
- tokens: bfloat16 [8, 2048, 768], P('dp', 'tensor'), may hold values from -6 to 6
- picture_ids: int32 [8, 2048], P('dp'), may hold values from -1 to 19, as said below
- ln1_gain: float32 [768], replicated, may hold values from 0.1 to 1.9
- ln1_bias: float32 [768], replicated, may hold values from -3 to 3
- w_qkv: bfloat16 [768, 3, 768], P('dp', None, 'tensor'), may hold values from -0.21875 to 0.21875
- q_gain: float32 [64], replicated, may hold values from 0.1 to 1.9
- k_gain: float32 [64], replicated, may hold values from 0.1 to 1.9
- w_out: bfloat16 [768, 768], P('tensor', 'dp'), may hold values from -1.75 to 1.75
- ln2_gain: float32 [768], replicated, may hold values from 0.1 to 1.9
- ln2_bias: float32 [768], replicated, may hold values from -3 to 3
- w_up: bfloat16 [768, 3072], P('dp', 'tensor'), may hold values from -0.21875 to 0.21875
- w_down: bfloat16 [3072, 768], P('tensor', 'dp'), may hold values from -0.109375 to 0.109375
- cotangent: bfloat16 [8, 2048, 768], P('dp', 'tensor'), may hold values from -6 to 6
Outputs:
- result: bfloat16 [8, 2048, 768], P('dp', 'tensor')
- grad_tokens: bfloat16 [8, 2048, 768], P('dp', 'tensor')
- grad_ln1_gain: float32 [768], replicated
- grad_ln1_bias: float32 [768], replicated
- grad_w_qkv: float32 [768, 3, 768], P('dp', None, 'tensor')
- grad_q_gain: float32 [64], replicated
- grad_k_gain: float32 [64], replicated
- grad_w_out: float32 [768, 768], P('tensor', 'dp')
- grad_ln2_gain: float32 [768], replicated
- grad_ln2_bias: float32 [768], replicated
- grad_w_up: float32 [768, 3072], P('dp', 'tensor')
- grad_w_down: float32 [3072, 768], P('tensor', 'dp')
The draws below stay inside these ranges and needn't reach their ends.
Inputs may be any that keep to these rules, and one draw needn't show every extreme that they name: `picture_ids`: each row holds whole pictures of 100 to 1024 consecutive slots numbered 0, 1, 2, ... from the row's start, then padding slots marked -1; some picture of every draw has exactly 1024 slots, and some row of every draw holds only pictures of 100 slots, as many as fit.
All inputs are finite; a program needn't handle non-finite values.
Results may differ from the reference program's by a relative error of at most 0.018.
Values may be sent and summed in bfloat16 or wider, within the bound.
No kernel may reach another device: no remote copies, remote signals or barrier semaphores. Data moves between devices by JAX's collectives and lax.ppermute only.
A program may use at most 128 MiB of HBM per device.

```python
import jax
import jax.numpy as jnp
from jax import lax

D = 768
HEADS = 12
HD = 64
FF = 3072
ROW = 2048
PIC_MIN = 100
PIC_MAX = 1024
BATCH = 8


def draw_picture_ids(key, part):
    cand_count = ROW // PIC_MIN + 1
    key_lengths, key_row = jax.random.split(key)
    lengths = jax.random.randint(key_lengths, (BATCH, cand_count), PIC_MIN, PIC_MAX + 1, dtype=jnp.int32)
    chosen = jax.random.randint(key_row, (), 0, BATCH, dtype=jnp.int32)
    packed_row = (chosen + 1) % BATCH
    row_index = jnp.arange(BATCH, dtype=jnp.int32)[:, None]
    lengths = jnp.where(row_index == packed_row, PIC_MIN, lengths)
    first_col = (row_index == chosen) & (jnp.arange(cand_count, dtype=jnp.int32)[None, :] == 0)
    lengths = jnp.where(first_col, PIC_MAX, lengths)
    end_slots = jnp.cumsum(lengths, axis=1)
    slot_index = jnp.arange(ROW, dtype=jnp.int32)
    picture = jnp.sum((end_slots[:, None, :] <= slot_index[None, :, None]).astype(jnp.int32), axis=2)
    complete = jnp.sum((end_slots <= ROW).astype(jnp.int32), axis=1)
    return jnp.where(picture < complete[:, None], picture, -1).astype(jnp.int32)


def with_spikes(result, key, source, target, shards_of, factor):
    owner, partner = [(jnp.arange(result.shape[axis_at]) // (result.shape[axis_at] // shards_of)).reshape([-1 if axis == axis_at else 1 for axis in range(result.ndim)]) for axis_at in (source, target)]
    chosen = jax.random.permutation(key, shards_of)[partner]
    strong = (owner == chosen) | (owner == (partner + shards_of // 2) % shards_of)
    return jnp.where(strong, factor * result, result)


def shard_levels(own_key, dims, pieces, low, high):
    factor_of, own = 1.0, jax.random.fold_in(own_key, 6)
    for position, blocks in pieces:
        draws = jnp.exp(jax.random.uniform(jax.random.fold_in(own, position), (blocks,), jnp.float32, low / len(pieces), high / len(pieces)))
        factor_of = factor_of * jnp.repeat(draws, dims[position] // blocks).reshape([-1 if axis == position else 1 for axis in range(len(dims))])
    return factor_of


def bell_draw(stream_key, shape, width, bound, cuts=(), kind=jnp.bfloat16):
    gain = shard_levels(stream_key, shape, cuts, -0.22, 0.18) if cuts else 1.0
    result = jax.random.normal(stream_key, shape, jnp.float32) * width * gain
    return jnp.minimum(jnp.maximum(result, -bound), bound).astype(kind)


def bell_draw_with(key, dims, width, limit, pieces, heavy, kind=jnp.bfloat16):
    array = width * jax.random.normal(key, dims, jnp.float32)
    if pieces:
        array = array * shard_levels(key, dims, pieces, -0.22, 0.18)
    return jnp.clip(with_spikes(array, jax.random.fold_in(key, 3), *heavy), -limit, limit).astype(kind)


def setup_inputs(seed: int = 0) -> dict:
    splits = jax.random.split(jax.random.key(seed), 14)
    tokens = bell_draw(splits[0], (BATCH, ROW, D), 1.0, 6.0, ((0, 8), (1, 4)))
    picture_ids = draw_picture_ids(jax.random.fold_in(splits[13], 71), 0)
    ln1_gain = jnp.clip(1.0 + 0.18 * jax.random.normal(splits[2], (D,), jnp.float32), 0.1, 1.9)
    ln1_bias = bell_draw(splits[3], (D,), 0.5, 3.0, (), jnp.float32)
    w_qkv = bell_draw(splits[4], (D, 3, D), D ** -0.5, 0.21875, ((0, 8), (2, 4)))
    q_gain = jnp.clip(1.0 + 0.18 * jax.random.normal(splits[5], (HD,), jnp.float32), 0.1, 1.9)
    k_gain = jnp.clip(1.0 + 0.18 * jax.random.normal(splits[6], (HD,), jnp.float32), 0.1, 1.9)
    w_out = bell_draw(splits[7], (D, D), (D * 16 // PIC_MAX) ** -0.5, 1.75, ((0, 4), (1, 8)))
    ln2_gain = jnp.clip(1.0 + 0.18 * jax.random.normal(splits[8], (D,), jnp.float32), 0.1, 1.9)
    ln2_bias = bell_draw(splits[9], (D,), 0.5, 3.0, (), jnp.float32)
    w_up = bell_draw(splits[10], (D, FF), D ** -0.5, 0.21875, ((0, 8), (1, 4)))
    w_down = bell_draw(splits[11], (FF, D), FF ** -0.5, 0.109375, ((0, 4), (1, 8)))
    cotangent = bell_draw_with(splits[12], (BATCH, ROW, D), 1.0, 6.0, ((0, 8), (1, 4)), (0, 2, 8, 2.0))
    return dict(tokens=tokens, picture_ids=picture_ids, ln1_gain=ln1_gain, ln1_bias=ln1_bias, w_qkv=w_qkv, q_gain=q_gain, k_gain=k_gain, w_out=w_out, ln2_gain=ln2_gain, ln2_bias=ln2_bias, w_up=w_up, w_down=w_down, cotangent=cotangent)


EPSILON = 1e-06
HIGHEST = lax.Precision.HIGHEST

@jax.custom_vjp
def low(v):
    return lax.optimization_barrier(v.astype(jnp.bfloat16)).astype(jnp.float32)

@jax.custom_vjp
def low_back(v):
    return v

def low_keep(v):
    return (low(v), None)

def low_pass(kept, grad):
    return (grad,)

def back_keep(v):
    return (v, None)

def back_low(kept, grad):
    return (low(grad),)
low.defvjp(low_keep, low_pass)
low_back.defvjp(back_keep, back_low)

def layer_norm(values, gain_vec, bias_vec):
    center = values - lax.optimization_barrier(jnp.mean(values, axis=-1, keepdims=True))
    spread = lax.optimization_barrier(jnp.mean(center * center, axis=-1, keepdims=True))
    return center * lax.rsqrt(spread + EPSILON) * gain_vec + bias_vec

def head_norm(values, gain_vec):
    center = values - lax.optimization_barrier(jnp.mean(values, axis=-1, keepdims=True))
    spread = lax.optimization_barrier(jnp.mean(center * center, axis=-1, keepdims=True))
    return center * lax.rsqrt(spread + EPSILON) * gain_vec

def row_forward(tokens_row, ids_row, params):
    ln1_gain, ln1_bias, w_qkv, q_gain, k_gain, w_out, ln2_gain, ln2_bias, w_up, w_down = params
    slot_count = tokens_row.shape[0]
    normed = low(layer_norm(tokens_row, ln1_gain, ln1_bias))
    project = jnp.einsum('sd,dic->sic', normed, w_qkv, precision=HIGHEST)
    query_raw = low_back(project[:, 0]).reshape(slot_count, HEADS, HD)
    key_raw = low_back(project[:, 1]).reshape(slot_count, HEADS, HD)
    value_rows = low(low_back(project[:, 2])).reshape(slot_count, HEADS, HD)
    query_norm = low(head_norm(query_raw, q_gain))
    key_norm = low(head_norm(key_raw, k_gain))
    scores = low_back(jnp.einsum('qhe,khe->hqk', query_norm, key_norm, precision=HIGHEST) * HD ** (-0.5))
    allowed = ids_row[:, None] == ids_row[None, :]
    scores = jnp.where(allowed[None], scores, -1e+30)
    top_score = lax.optimization_barrier(jnp.max(scores, axis=-1, keepdims=True))
    exponent = jnp.exp(scores - top_score)
    probs = exponent / lax.optimization_barrier(jnp.sum(exponent, axis=-1, keepdims=True))
    attended = jnp.einsum('hqk,khe->qhe', low(probs), value_rows, precision=HIGHEST).reshape(slot_count, HEADS * HD)
    attended = low(low_back(attended))
    middle = tokens_row + low_back(jnp.dot(attended, w_out, precision=HIGHEST))
    normed_two = low(layer_norm(middle, ln2_gain, ln2_bias))
    up_proj = low_back(jnp.dot(normed_two, w_up, precision=HIGHEST))
    hidden = low(jax.nn.gelu(up_proj, approximate=False))
    return middle + low_back(jnp.dot(hidden, w_down, precision=HIGHEST))

def reference(tokens, picture_ids, ln1_gain, ln1_bias, w_qkv, q_gain, k_gain, w_out, ln2_gain, ln2_bias, w_up, w_down, cotangent):
    params = tuple((item.astype(jnp.float32) for item in (ln1_gain, ln1_bias, w_qkv, q_gain, k_gain, w_out, ln2_gain, ln2_bias, w_up, w_down)))
    tokens_float = tokens.astype(jnp.float32)
    row_step = jax.checkpoint(row_forward)

    def whole(inputs, weights):
        return lax.map(lambda row_pair: row_step(row_pair[0], row_pair[1], weights), (inputs, picture_ids))
    outputs, pullback = jax.vjp(whole, tokens_float, params)
    grad_input, grads = pullback(cotangent.astype(jnp.float32))
    return (outputs.astype(jnp.bfloat16), grad_input.astype(jnp.bfloat16), grads[0], grads[1], grads[2], grads[3], grads[4], grads[5], grads[6], grads[7], grads[8], grads[9])
```

```python
import functools

import jax
import jax.numpy as jnp
from jax import lax
from jax.experimental import pallas as pl
from jax.experimental.pallas import tpu as pltpu
from jax.sharding import PartitionSpec as P

HD=64; EPSILON=1e-6
LOG2E=1.4426950408889634
QSCALE=LOG2E/8.0
BIG=256.0
F32=jnp.float32; BF=jnp.bfloat16

def nn(a,b): return lax.dot_general(a,b,(((1,),(0,)),((),())),preferred_element_type=F32)

def norm_T(x):
    c = x - jnp.mean(x,axis=0,keepdims=True)
    inv = lax.rsqrt(jnp.mean(c*c,axis=0,keepdims=True)+EPSILON)
    return c*inv, inv

def split3(v):
    hi=v.astype(BF).astype(F32); r=v-hi
    mid=r.astype(BF).astype(F32); lo=r-mid
    return hi,mid,lo

def fwd_kernel(n_ref,l_ref, q_ref,k_ref,v_ref,fq_ref,fk_ref,qg_ref,kg_ref,o_ref,lse_ref,KT,QN,VN,*,HG,Q,K,BQ,BK,CH):
    ones_row = jnp.where(lax.broadcasted_iota(jnp.int32,(64,CH),0)==0,1.0,0.0).astype(F32)
    for h in range(HG):
        for c in range(K//CH):
            s=slice(c*CH,(c+1)*CH)
            kn,_=norm_T(k_ref[h,:,s])
            KT[h,:64,s]=(kn*kg_ref[...]).astype(BF)
            KT[h,64:,s]=fk_ref[:,s]
            VN[h,s,:]=jnp.concatenate([v_ref[h,:,s].astype(F32),ones_row],axis=0).T.astype(BF)
        for c in range(Q//CH):
            s=slice(c*CH,(c+1)*CH)
            qn,_=norm_T(q_ref[h,:,s])
            qa=jnp.concatenate([qn*(qg_ref[...]*QSCALE),fq_ref[:,s].astype(F32)],axis=0)
            QN[h,s,:]=qa.T.astype(BF)
    NK=K//BK
    for qb in range(Q//BQ):
        def body(i,accs):
            kb=pl.multiple_of(l_ref[qb*NK+i]*BK,BK)
            out=[]
            for h in range(HG):
                S=nn(QN[h,qb*BQ:(qb+1)*BQ,:],KT[h,:,pl.ds(kb,BK)])
                P=jnp.exp2(S).astype(BF)
                out.append(accs[h]+nn(P,VN[h,pl.ds(kb,BK),:]))
            return tuple(out)
        accs=lax.fori_loop(0,n_ref[qb],body,tuple(jnp.zeros((BQ,128),F32) for _ in range(HG)))
        for h in range(HG):
            t=accs[h].T
            tot=t[64:65]
            s=slice(qb*BQ,(qb+1)*BQ)
            o_ref[h,:,s]=(t[:64]/tot).astype(BF)
            lse_ref[h,:,s]=jnp.log2(tot)

def attn_fwd(n,l,q,kv,fq,fk,qg,kg,*,HG=3,BQ=256,BK=256,CH=512):
    R,_,Q=q.shape; K=kv.shape[-1]
    q=q.reshape(R,3,64,Q); kv=kv.reshape(R,2,3,64,K)
    G=3//HG
    kern=functools.partial(fwd_kernel,HG=HG,Q=Q,K=K,BQ=BQ,BK=BK,CH=CH)
    full=lambda shp: pl.BlockSpec(shp,lambda r,g,*_:(0,)*len(shp))
    o,lse=pl.pallas_call(kern,
      out_shape=(jax.ShapeDtypeStruct((R,3,64,Q),BF),jax.ShapeDtypeStruct((R,3,1,Q),F32)),
      grid_spec=pltpu.PrefetchScalarGridSpec(num_scalar_prefetch=2,grid=(R,G),
        in_specs=[pl.BlockSpec((None,HG,64,Q),lambda r,g,*_:(r,g,0,0)),
                  pl.BlockSpec((None,None,HG,64,K),lambda r,g,*_:(r,0,g,0,0)),
                  pl.BlockSpec((None,None,HG,64,K),lambda r,g,*_:(r,1,g,0,0)),
                  full((64,Q)),full((64,K)),full((64,1)),full((64,1))],
        out_specs=(pl.BlockSpec((None,HG,64,Q),lambda r,g,*_:(r,g,0,0)),pl.BlockSpec((None,HG,1,Q),lambda r,g,*_:(r,g,0,0))),
        scratch_shapes=[pltpu.VMEM((HG,128,K),BF),pltpu.VMEM((HG,Q,128),BF),pltpu.VMEM((HG,K,128),BF)]),
      compiler_params=pltpu.CompilerParams(vmem_limit_bytes=50*2**20),
      name="attn_fwd")(n,l,q,kv,kv,fq,fk,qg.reshape(64,1),kg.reshape(64,1))
    return o,lse

def bwd_kernel(n_ref,l_ref, q_ref,k_ref,v_ref,do_ref,o_ref,lse_ref,fq_ref,fk_ref,qg_ref,kg_ref,
               gq_ref,gkv_ref,gqg_ref,gkg_ref, KT,KN,VN,QT,QN,DOT,DON,DQT,DK,DV,*,HG,Q,K,BQ,BK,CH):
    first=(pl.program_id(0)==0)&(pl.program_id(1)==0)
    @pl.when(first)
    def _():
        gqg_ref[...]=jnp.zeros_like(gqg_ref); gkg_ref[...]=jnp.zeros_like(gkg_ref)
    row=lax.broadcasted_iota(jnp.int32,(64,CH),0)
    three=jnp.where(row<3,1.0,0.0).astype(F32)
    for h in range(HG):
        for c in range(K//CH):
            s=slice(c*CH,(c+1)*CH)
            kn,_=norm_T(k_ref[h,:,s])
            kt=jnp.concatenate([kn*kg_ref[...],fk_ref[:,s].astype(F32)],axis=0)
            KT[h,:,s]=kt[:64].astype(BF)
            KN[h,s,:]=kt.T.astype(BF)
            VN[h,s,:]=jnp.concatenate([v_ref[h,:,s].astype(F32),three],axis=0).T.astype(BF)
            DK[h,s,:]=jnp.zeros((CH,128),F32); DV[h,s,:]=jnp.zeros((CH,128),F32)
        for c in range(Q//CH):
            s=slice(c*CH,(c+1)*CH)
            qn,_=norm_T(q_ref[h,:,s])
            a,b,d=split3(-lse_ref[h,:,s])
            f=fq_ref[:,s].astype(F32)
            f=jnp.where(row==33,a,jnp.where(row==34,b,jnp.where(row==35,d,f)))
            qt=jnp.concatenate([qn*(qg_ref[...]*QSCALE),f],axis=0)
            QT[h,:,s]=qt.astype(BF)
            QN[h,s,:]=qt.T.astype(BF)
            do=do_ref[h,:,s].astype(F32)
            D=-jnp.sum(do*o_ref[h,:,s].astype(F32),axis=0,keepdims=True)
            a,b,d=split3(D)
            g=jnp.where(row==0,a,jnp.where(row==1,b,jnp.where(row==2,d,0.0)))
            dt=jnp.concatenate([do,g],axis=0)
            DOT[h,:,s]=dt.astype(BF)
            DON[h,s,:]=dt.T.astype(BF)
    NK=K//BK
    for qb in range(Q//BQ):
        qs=slice(qb*BQ,(qb+1)*BQ)
        def body(i,accs):
            kb=pl.multiple_of(l_ref[qb*NK+i]*BK,BK)
            ks=pl.ds(kb,BK)
            out=[]
            for h in range(HG):
                ST=nn(KN[h,ks,:],QT[h,:,qs])
                P=jnp.exp2(ST)
                DP=nn(VN[h,ks,:],DOT[h,:,qs])
                dS=(P*DP).astype(BF)
                DV[h,ks,:]+=nn(P.astype(BF),DON[h,qs,:])
                DK[h,ks,:]+=nn(dS,QN[h,qs,:])
                out.append(accs[h]+nn(KT[h,:,ks],dS))
            return tuple(out)
        accs=lax.fori_loop(0,n_ref[qb],body,tuple(jnp.zeros((64,BQ),F32) for _ in range(HG)))
        for h in range(HG): DQT[h,:,qs]=accs[h]
    def ln_back(dx,gain,raw):
        hat,inv=norm_T(raw)
        u=dx*gain
        g=inv*(u-jnp.mean(u,axis=0,keepdims=True)-hat*jnp.mean(u*hat,axis=0,keepdims=True))
        return g, jnp.sum(dx*hat,axis=1,keepdims=True)
    for h in range(HG):
        for c in range(K//CH):
            s=slice(c*CH,(c+1)*CH)
            g,gg=ln_back(DK[h,s,:].T[:64]*(1.0/LOG2E),kg_ref[...],k_ref[h,:,s])
            gkv_ref[0,h,:,s]=g.astype(BF)
            gkg_ref[...]+=gg
            gkv_ref[1,h,:,s]=DV[h,s,:].T[:64].astype(BF)
        for c in range(Q//CH):
            s=slice(c*CH,(c+1)*CH)
            g,gg=ln_back(DQT[h,:,s]*0.125,qg_ref[...],q_ref[h,:,s])
            gq_ref[h,:,s]=g.astype(BF)
            gqg_ref[...]+=gg

def attn_bwd(n,l,q,kv,do,o,lse,fq,fk,qg,kg,*,HG=3,BQ=256,BK=256,CH=512):
    R,_,Q=q.shape; K=kv.shape[-1]
    q=q.reshape(R,3,64,Q); kv=kv.reshape(R,2,3,64,K); do=do.reshape(R,3,64,Q)
    G=3//HG
    kern=functools.partial(bwd_kernel,HG=HG,Q=Q,K=K,BQ=BQ,BK=BK,CH=CH)
    full=lambda shp: pl.BlockSpec(shp,lambda r,g,*_:(0,)*len(shp))
    qsp=lambda: pl.BlockSpec((None,HG,64,Q),lambda r,g,*_:(r,g,0,0))
    return pl.pallas_call(kern,
      out_shape=(jax.ShapeDtypeStruct((R,3,64,Q),BF),jax.ShapeDtypeStruct((R,2,3,64,K),BF),jax.ShapeDtypeStruct((64,1),F32),jax.ShapeDtypeStruct((64,1),F32)),
      grid_spec=pltpu.PrefetchScalarGridSpec(num_scalar_prefetch=2,grid=(R,G),
        in_specs=[qsp(),
                  pl.BlockSpec((None,None,HG,64,K),lambda r,g,*_:(r,0,g,0,0)),
                  pl.BlockSpec((None,None,HG,64,K),lambda r,g,*_:(r,1,g,0,0)),
                  qsp(),qsp(),pl.BlockSpec((None,HG,1,Q),lambda r,g,*_:(r,g,0,0)),
                  full((64,Q)),full((64,K)),full((64,1)),full((64,1))],
        out_specs=(qsp(),pl.BlockSpec((None,2,HG,64,K),lambda r,g,*_:(r,0,g,0,0)),full((64,1)),full((64,1))),
        scratch_shapes=[pltpu.VMEM((HG,64,K),BF),pltpu.VMEM((HG,K,128),BF),pltpu.VMEM((HG,K,128),BF),
                        pltpu.VMEM((HG,128,Q),BF),pltpu.VMEM((HG,Q,128),BF),pltpu.VMEM((HG,128,Q),BF),pltpu.VMEM((HG,Q,128),BF),
                        pltpu.VMEM((HG,64,Q),F32),pltpu.VMEM((HG,K,128),F32),pltpu.VMEM((HG,K,128),F32)]),
      compiler_params=pltpu.CompilerParams(vmem_limit_bytes=56*2**20),
      name="attn_bwd")(n,l,q,kv,kv,do,o,lse,fq,fk,qg.reshape(64,1),kg.reshape(64,1))

def features(ids, Q, BQ=256, BK=256):
    K=ids.shape[0]
    r=jnp.arange(64,dtype=jnp.int32)[:,None]
    hot=(ids[None,:]+1)==r
    hot=hot&(r<32)
    fk=jnp.where(hot,1.0,jnp.where((r>=32)&(r<36),1.0,0.0)).astype(BF)
    fq=jnp.where(hot[:,:Q],BIG,jnp.where(r==32,-BIG,0.0)).astype(BF)
    kb=hot[:32].reshape(32,K//BK,BK).any(-1)
    qb=hot[:32,:Q].reshape(32,Q//BQ,BQ).any(-1)
    act=(qb[:,:,None]&kb[:,None,:]).any(0)
    n=act.sum(-1).astype(jnp.int32)
    NK=K//BK
    before=jnp.arange(NK)[:,None]>jnp.arange(NK)[None,:]
    rank=(act[:,None,:]&before[None]).sum(-1)
    lst=((rank[:,None,:]==jnp.arange(NK)[None,:,None])&act[:,None,:])
    lst=(lst*jnp.arange(NK)[None,None,:]).sum(-1).astype(jnp.int32)
    return fq,fk,n,lst.reshape(-1)


def xor_perm(size, mask):
    return [(i, i ^ mask) for i in range(size)]


def swap(values, axis, mask):
    return lax.ppermute(values, axis, xor_perm(lax.axis_size(axis), mask))


def place(held, got, bit, axis):
    low = jnp.where(bit == 0, held, got)
    high = jnp.where(bit == 0, got, held)
    return jnp.stack([low, high], axis=axis)


def gather_weights(shard):
    rows, cols = shard.shape
    size = lax.axis_size("dp")
    me = lax.axis_index("dp")
    held = shard[None]
    for level in reversed(range(1, size.bit_length() - 1)):
        got = swap(held, "dp", 1 << level)
        held = place(held, got, (me >> level) & 1, 1).reshape(-1, rows, cols)
    count = held.shape[0]
    half = rows // 2
    part_a, part_b = held[:, :half], held[:, half:]
    bit = me & 1
    part_a = jnp.stack([part_a, swap(part_a, "tensor", 2)], axis=0)
    part_b = place(part_b, swap(part_b, "dp", 1), bit, 1)
    part_a = place(part_a, swap(part_a, "dp", 1), bit, 2)
    part_b = jnp.stack([part_b, swap(part_b, "tensor", 2)], axis=0)
    both = jnp.concatenate([part_a, part_b], axis=3)
    return both.reshape(2, count * 2 * rows, cols)


def take_half(values, bit, axis):
    return lax.dynamic_index_in_dim(values, bit, axis, keepdims=False)


def scatter_grads(grad):
    size = lax.axis_size("dp")
    me = lax.axis_index("dp")
    cols = grad.shape[2]
    rows = grad.shape[1] // size
    half = rows // 2
    bit = me & 1
    grad = grad.reshape(2, size // 2, 2, rows, cols)
    part_a, part_b = grad[:, :, :, :half], grad[:, :, :, half:]
    got = swap(take_half(part_a, 1 - bit, 2).astype(BF), "dp", 1)
    part_a = take_half(part_a, bit, 2) + got.astype(F32)
    got = swap(part_b[1].astype(BF), "tensor", 2)
    part_b = part_b[0] + got.astype(F32)
    got = swap(part_a[1].astype(BF), "tensor", 2)
    part_a = part_a[0] + got.astype(F32)
    got = swap(take_half(part_b, 1 - bit, 1).astype(BF), "dp", 1)
    part_b = take_half(part_b, bit, 1) + got.astype(F32)
    held = jnp.concatenate([part_a, part_b], axis=1)
    for level in range(1, size.bit_length() - 1):
        bit = (me >> level) & 1
        held = held.reshape(-1, 2, rows, cols)
        got = swap(take_half(held, 1 - bit, 1).astype(BF), "dp", 1 << level)
        held = take_half(held, bit, 1) + got.astype(F32)
    return held.reshape(rows, cols)


def sum_all(values):
    values = values + swap(values, "tensor", 1)
    values = values + swap(values, "tensor", 2)
    for level in range(lax.axis_size("dp").bit_length() - 1):
        values = values + swap(values, "dp", 1 << level)
    return values


def hat_of(values):
    center = values - jnp.mean(values, axis=-1, keepdims=True)
    inv = lax.rsqrt(jnp.mean(center * center, axis=-1, keepdims=True) + EPSILON)
    return center * inv, inv


def hat_back(grad, gain, hat, inv):
    u = grad * gain
    return inv * (u - jnp.mean(u, axis=-1, keepdims=True) - hat * jnp.mean(u * hat, axis=-1, keepdims=True))


def gelu_pair(v):
    x = jnp.abs(v) * (0.5**0.5)
    t = 1.0 / (1.0 + 0.3275911 * x)
    e = jnp.exp(-x * x)
    poly = ((((1.061405429 * t - 1.453152027) * t + 1.421413741) * t - 0.284496736) * t + 0.254829592) * t
    tail = 0.5 * poly * e
    phi = jnp.where(v < 0, tail, 1.0 - tail)
    return v * phi, phi + v * e * 0.3989422804014327


def own_part(share):
    half = share.shape[0] // 2
    got = swap(share[half:].astype(BF), "tensor", 1)
    return share[:half] + got.astype(F32)


def with_core(own):
    return jnp.concatenate([own, swap(own, "tensor", 1)], axis=0)


def mm(spec, *arrays):
    return jnp.einsum(spec, *arrays, preferred_element_type=F32)


def per_device(tokens, picture_ids, ln1_gain, ln1_bias, w_qkv, q_gain, k_gain, w_out, ln2_gain, ln2_bias, w_up, w_down, cotangent):
    slots, width = tokens.shape[1:]
    local = w_qkv.shape[2]
    hidden_cols = w_up.shape[1]
    tok = tokens[0]
    cot = cotangent[0]
    tensor = lax.axis_index("tensor")
    tok_x = swap(tok, "tensor", 2)
    tok_c = swap(tok, "tensor", 1)
    w_one = gather_weights(jnp.concatenate([w_qkv[:, 1], w_qkv[:, 2], w_qkv[:, 0]], axis=1))
    w_two = gather_weights(jnp.concatenate([w_up, w_down.T, w_out.T], axis=1))
    tok_xc = swap(tok_x, "tensor", 1)
    cot_all = with_core(cot)
    ids = picture_ids[0].reshape(4, slots)
    ids = jnp.concatenate([lax.dynamic_index_in_dim(ids, tensor ^ i, 0, keepdims=False) for i in range(4)])
    q_slots = 2 * slots
    fq, fk, count, blocks = features(ids, q_slots, BQ, BK)

    hats = [hat_of(block.astype(F32)) for block in (tok, tok_c, tok_x, tok_xc)]
    normed = jnp.concatenate([(hat * ln1_gain + ln1_bias).astype(BF) for hat, _ in hats], axis=0)
    kv = mm("sd,rdc->rcs", normed, w_one[:, :, : 2 * local]).reshape(2, 2, local, 4 * slots)
    q = mm("sd,rdc->rcs", normed[:q_slots], w_one[:, :, 2 * local :])
    att, lse = attn_fwd(count, blocks, q, kv, fq, fk, q_gain, k_gain, HG=HGF, BQ=BQ, BK=BK)
    att_cols = att.reshape(2, local, q_slots)

    wu = w_two[:, :, :hidden_cols]
    wd = w_two[:, :, hidden_cols : 2 * hidden_cols]
    wo = w_two[:, :, 2 * hidden_cols :]
    middle = tok.astype(F32) + own_part(mm("rcs,rdc->sd", att_cols, wo))
    hat2, inv2 = hat_of(middle)
    normed2 = with_core((hat2 * ln2_gain + ln2_bias).astype(BF))
    hid, slope = gelu_pair(mm("sd,rdf->srf", normed2, wu))
    hid = hid.astype(BF)
    slope = slope.astype(BF)
    grad_up = (mm("sd,rdf->srf", cot_all, wd) * slope.astype(F32)).astype(BF)
    grad_normed2 = own_part(mm("srf,rdf->sd", grad_up, wu))
    grad_wu = mm("sd,srf->rdf", normed2, grad_up)
    grad_wd = mm("sd,srf->rdf", cot_all, hid)
    grad_gain2 = jnp.sum(grad_normed2 * hat2, axis=0)
    grad_bias2 = jnp.sum(grad_normed2, axis=0)
    grad_mid = cot.astype(F32) + hat_back(grad_normed2, ln2_gain, hat2, inv2)
    branch = with_core(grad_mid.astype(BF))
    grad_att = mm("sd,rdc->rcs", branch, wo).astype(BF)
    grad_wo = mm("sd,rcs->rdc", branch, att_cols)
    result = (middle + own_part(mm("srf,rdf->sd", hid, wd))).astype(BF)
    grad_two = scatter_grads(jnp.concatenate([grad_wu, grad_wd, grad_wo], axis=2))

    gq, gkv, grad_qg, grad_kg = attn_bwd(
        count, blocks, q, kv, grad_att, att, lse, fq, fk, q_gain, k_gain, HG=HGB, BQ=BQ, BK=BK
    )
    gq = gq.reshape(2, local, q_slots)
    gkv = gkv.reshape(2, 2 * local, 4 * slots)
    other = mm("rcs,rdc->sd", gkv[:, :, q_slots:], w_one[:, :, : 2 * local])
    here = mm("rcs,rdc->sd", jnp.concatenate([gkv[:, :, :q_slots], gq], axis=1), w_one)
    across = own_part(other)
    grad_normed = own_part(here)
    got = swap(across.astype(BF), "tensor", 2)
    grad_wkv = mm("sd,rcs->rdc", normed, gkv)
    grad_wq = mm("sd,rcs->rdc", normed[:q_slots], gq)
    grad_one = scatter_grads(jnp.concatenate([grad_wkv, grad_wq], axis=2))
    hat1, inv1 = hats[0]
    grad_gain1 = jnp.sum(grad_normed * hat1, axis=0) + jnp.sum(across * hats[2][0], axis=0)
    grad_bias1 = jnp.sum(grad_normed, axis=0) + jnp.sum(across, axis=0)
    heads = jnp.pad(jnp.concatenate([grad_qg[:, 0], grad_kg[:, 0]]), (0, width - 2 * HD))
    small = sum_all(jnp.stack([grad_gain1, grad_bias1, grad_gain2, grad_bias2, heads]))
    grad_normed = grad_normed + got.astype(F32)
    grad_tokens = (grad_mid + hat_back(grad_normed, ln1_gain, hat1, inv1)).astype(BF)

    grad_qkv = jnp.stack([grad_one[:, 2 * local :], grad_one[:, :local], grad_one[:, local : 2 * local]], axis=1)
    return (
        result[None],
        grad_tokens[None],
        small[0],
        small[1],
        grad_qkv,
        small[4, :HD],
        small[4, HD : 2 * HD],
        grad_two[:, 2 * hidden_cols :].T,
        small[2],
        small[3],
        grad_two[:, :hidden_cols],
        grad_two[:, hidden_cols : 2 * hidden_cols].T,
    )


BQ = 512
BK = 256
HGF = 3
HGB = 3


def solution(mesh):
    rows = P("dp", "tensor", None)
    wide = P("dp", "tensor")
    tall = P("tensor", "dp")
    qkv = P("dp", None, "tensor")
    in_specs = (rows, P("dp", None), P(), P(), qkv, P(), P(), tall, P(), P(), wide, tall, rows)
    out_specs = (rows, rows, P(), P(), qkv, P(), P(), tall, P(), P(), wide, tall)
    return jax.shard_map(per_device, mesh=mesh, in_specs=in_specs, out_specs=out_specs, check_vma=False)
```

```python
import functools

import jax
import jax.numpy as jnp
from jax import lax
from jax.experimental import pallas as pl
from jax.experimental.pallas import tpu as pltpu
from jax.sharding import PartitionSpec as P

HD=64; EPSILON=1e-6
LOG2E=1.4426950408889634
QSCALE=LOG2E/8.0
BIG=256.0
F32=jnp.float32; BF=jnp.bfloat16

def nn(a,b): return lax.dot_general(a,b,(((1,),(0,)),((),())),preferred_element_type=F32)

def norm_T(x):
    c = x - jnp.mean(x,axis=0,keepdims=True)
    inv = lax.rsqrt(jnp.mean(c*c,axis=0,keepdims=True)+EPSILON)
    return c*inv, inv

def split3(v):
    hi=v.astype(BF).astype(F32); r=v-hi
    mid=r.astype(BF).astype(F32); lo=r-mid
    return hi,mid,lo

def fwd_kernel(n_ref,l_ref, q_ref,k_ref,v_ref,fq_ref,fk_ref,qg_ref,kg_ref,o_ref,lse_ref,KT,QN,VN,*,HG,Q,K,BQ,BK,CH):
    ones_row = jnp.where(lax.broadcasted_iota(jnp.int32,(64,CH),0)==0,1.0,0.0).astype(F32)
    for h in range(HG):
        for c in range(K//CH):
            s=slice(c*CH,(c+1)*CH)
            kn,_=norm_T(k_ref[h,:,s])
            KT[h,:64,s]=(kn*kg_ref[...]).astype(BF)
            KT[h,64:,s]=fk_ref[:,s]
            VN[h,s,:]=jnp.concatenate([v_ref[h,:,s].astype(F32),ones_row],axis=0).T.astype(BF)
        for c in range(Q//CH):
            s=slice(c*CH,(c+1)*CH)
            qn,_=norm_T(q_ref[h,:,s])
            qa=jnp.concatenate([qn*(qg_ref[...]*QSCALE),fq_ref[:,s].astype(F32)],axis=0)
            QN[h,s,:]=qa.T.astype(BF)
    NK=K//BK
    for qb in range(Q//BQ):
        def body(i,accs):
            kb=pl.multiple_of(l_ref[qb*NK+i]*BK,BK)
            out=[]
            for h in range(HG):
                S=nn(QN[h,qb*BQ:(qb+1)*BQ,:],KT[h,:,pl.ds(kb,BK)])
                P=jnp.exp2(S).astype(BF)
                out.append(accs[h]+nn(P,VN[h,pl.ds(kb,BK),:]))
            return tuple(out)
        accs=lax.fori_loop(0,n_ref[qb],body,tuple(jnp.zeros((BQ,128),F32) for _ in range(HG)))
        for h in range(HG):
            t=accs[h].T
            tot=t[64:65]
            s=slice(qb*BQ,(qb+1)*BQ)
            o_ref[h,:,s]=(t[:64]/tot).astype(BF)
            lse_ref[h,:,s]=jnp.log2(tot)

def attn_fwd(n,l,q,kv,fq,fk,qg,kg,*,HG=3,BQ=256,BK=256,CH=512,deps=()):
    Q=q.shape[-1]; K=kv.shape[-1]
    q=q.reshape(3,64,Q); kv=kv.reshape(2,3,64,K)
    kern=functools.partial(fwd_kernel,HG=HG,Q=Q,K=K,BQ=BQ,BK=BK,CH=CH)
    full=lambda shp: pl.BlockSpec(shp,lambda g,*_:(0,)*len(shp))
    return pl.pallas_call(drop_deps(kern,9,len(deps)),
      out_shape=(jax.ShapeDtypeStruct((3,64,Q),BF),jax.ShapeDtypeStruct((3,1,Q),F32)),
      grid_spec=pltpu.PrefetchScalarGridSpec(num_scalar_prefetch=2,grid=(3//HG,),
        in_specs=[pl.BlockSpec((HG,64,Q),lambda g,*_:(g,0,0)),
                  pl.BlockSpec((None,HG,64,K),lambda g,*_:(0,g,0,0)),
                  pl.BlockSpec((None,HG,64,K),lambda g,*_:(1,g,0,0)),
                  full((64,Q)),full((64,K)),full((64,1)),full((64,1))]+[pl.BlockSpec(memory_space=pl.ANY)]*len(deps),
        out_specs=(pl.BlockSpec((HG,64,Q),lambda g,*_:(g,0,0)),pl.BlockSpec((HG,1,Q),lambda g,*_:(g,0,0))),
        scratch_shapes=[pltpu.VMEM((HG,128,K),BF),pltpu.VMEM((HG,Q,128),BF),pltpu.VMEM((HG,K,128),BF)]),
      compiler_params=pltpu.CompilerParams(vmem_limit_bytes=48*2**20),
      cost_estimate=cost(1.2e10),name="attn_fwd")(n,l,q,kv,kv,fq,fk,qg.reshape(64,1),kg.reshape(64,1),*deps)

def bwd_kernel(n_ref,l_ref, q_ref,k_ref,v_ref,do_ref,o_ref,lse_ref,fq_ref,fk_ref,qg_ref,kg_ref,
               gq_ref,gkv_ref,gqg_ref,gkg_ref, KT,KN,VN,QT,QN,DOT,DON,DQT,DK,DV,*,HG,Q,K,BQ,BK,CH):
    first=pl.program_id(0)==0
    @pl.when(first)
    def _():
        gqg_ref[...]=jnp.zeros_like(gqg_ref); gkg_ref[...]=jnp.zeros_like(gkg_ref)
    row=lax.broadcasted_iota(jnp.int32,(64,CH),0)
    three=jnp.where(row<3,1.0,0.0).astype(F32)
    for h in range(HG):
        for c in range(K//CH):
            s=slice(c*CH,(c+1)*CH)
            kn,_=norm_T(k_ref[h,:,s])
            kt=jnp.concatenate([kn*kg_ref[...],fk_ref[:,s].astype(F32)],axis=0)
            KT[h,:,s]=kt[:64].astype(BF)
            KN[h,s,:]=kt.T.astype(BF)
            VN[h,s,:]=jnp.concatenate([v_ref[h,:,s].astype(F32),three],axis=0).T.astype(BF)
            DK[h,s,:]=jnp.zeros((CH,128),F32); DV[h,s,:]=jnp.zeros((CH,128),F32)
        for c in range(Q//CH):
            s=slice(c*CH,(c+1)*CH)
            qn,_=norm_T(q_ref[h,:,s])
            a,b,d=split3(-lse_ref[h,:,s])
            f=fq_ref[:,s].astype(F32)
            f=jnp.where(row==33,a,jnp.where(row==34,b,jnp.where(row==35,d,f)))
            qt=jnp.concatenate([qn*(qg_ref[...]*QSCALE),f],axis=0)
            QT[h,:,s]=qt.astype(BF)
            QN[h,s,:]=qt.T.astype(BF)
            do=do_ref[h,:,s].astype(F32)
            D=-jnp.sum(do*o_ref[h,:,s].astype(F32),axis=0,keepdims=True)
            a,b,d=split3(D)
            g=jnp.where(row==0,a,jnp.where(row==1,b,jnp.where(row==2,d,0.0)))
            dt=jnp.concatenate([do,g],axis=0)
            DOT[h,:,s]=dt.astype(BF)
            DON[h,s,:]=dt.T.astype(BF)
    NK=K//BK
    for qb in range(Q//BQ):
        qs=slice(qb*BQ,(qb+1)*BQ)
        def body(i,accs):
            kb=pl.multiple_of(l_ref[qb*NK+i]*BK,BK)
            ks=pl.ds(kb,BK)
            out=[]
            for h in range(HG):
                ST=nn(KN[h,ks,:],QT[h,:,qs])
                P=jnp.exp2(ST)
                DP=nn(VN[h,ks,:],DOT[h,:,qs])
                dS=(P*DP).astype(BF)
                DV[h,ks,:]+=nn(P.astype(BF),DON[h,qs,:])
                DK[h,ks,:]+=nn(dS,QN[h,qs,:])
                out.append(accs[h]+nn(KT[h,:,ks],dS))
            return tuple(out)
        accs=lax.fori_loop(0,n_ref[qb],body,tuple(jnp.zeros((64,BQ),F32) for _ in range(HG)))
        for h in range(HG): DQT[h,:,qs]=accs[h]
    def ln_back(dx,gain,raw):
        hat,inv=norm_T(raw)
        u=dx*gain
        g=inv*(u-jnp.mean(u,axis=0,keepdims=True)-hat*jnp.mean(u*hat,axis=0,keepdims=True))
        return g, jnp.sum(dx*hat,axis=1,keepdims=True)
    for h in range(HG):
        for c in range(K//CH):
            s=slice(c*CH,(c+1)*CH)
            g,gg=ln_back(DK[h,s,:].T[:64]*(1.0/LOG2E),kg_ref[...],k_ref[h,:,s])
            gkv_ref[0,h,:,s]=g.astype(BF)
            gkg_ref[...]+=gg
            gkv_ref[1,h,:,s]=DV[h,s,:].T[:64].astype(BF)
        for c in range(Q//CH):
            s=slice(c*CH,(c+1)*CH)
            g,gg=ln_back(DQT[h,:,s]*0.125,qg_ref[...],q_ref[h,:,s])
            gq_ref[h,:,s]=g.astype(BF)
            gqg_ref[...]+=gg

def attn_bwd(n,l,q,kv,do,o,lse,fq,fk,qg,kg,*,HG=3,BQ=256,BK=256,CH=512,deps=()):
    Q=q.shape[-1]; K=kv.shape[-1]
    q=q.reshape(3,64,Q); kv=kv.reshape(2,3,64,K); do=do.reshape(3,64,Q)
    kern=functools.partial(bwd_kernel,HG=HG,Q=Q,K=K,BQ=BQ,BK=BK,CH=CH)
    full=lambda shp: pl.BlockSpec(shp,lambda g,*_:(0,)*len(shp))
    qsp=lambda: pl.BlockSpec((HG,64,Q),lambda g,*_:(g,0,0))
    return pl.pallas_call(drop_deps(kern,12,len(deps)),
      out_shape=(jax.ShapeDtypeStruct((3,64,Q),BF),jax.ShapeDtypeStruct((2,3,64,K),BF),jax.ShapeDtypeStruct((64,1),F32),jax.ShapeDtypeStruct((64,1),F32)),
      grid_spec=pltpu.PrefetchScalarGridSpec(num_scalar_prefetch=2,grid=(3//HG,),
        in_specs=[qsp(),
                  pl.BlockSpec((None,HG,64,K),lambda g,*_:(0,g,0,0)),
                  pl.BlockSpec((None,HG,64,K),lambda g,*_:(1,g,0,0)),
                  qsp(),qsp(),pl.BlockSpec((HG,1,Q),lambda g,*_:(g,0,0)),
                  full((64,Q)),full((64,K)),full((64,1)),full((64,1))]+[pl.BlockSpec(memory_space=pl.ANY)]*len(deps),
        out_specs=(qsp(),pl.BlockSpec((2,HG,64,K),lambda g,*_:(0,g,0,0)),full((64,1)),full((64,1))),
        scratch_shapes=[pltpu.VMEM((HG,64,K),BF),pltpu.VMEM((HG,K,128),BF),pltpu.VMEM((HG,K,128),BF),
                        pltpu.VMEM((HG,128,Q),BF),pltpu.VMEM((HG,Q,128),BF),pltpu.VMEM((HG,128,Q),BF),pltpu.VMEM((HG,Q,128),BF),
                        pltpu.VMEM((HG,64,Q),F32),pltpu.VMEM((HG,K,128),F32),pltpu.VMEM((HG,K,128),F32)]),
      compiler_params=pltpu.CompilerParams(vmem_limit_bytes=48*2**20),
      cost_estimate=cost(2e10),name="attn_bwd")(n,l,q,kv,kv,do,o,lse,fq,fk,qg.reshape(64,1),kg.reshape(64,1),*deps)

def features(ids, Q, BQ=256, BK=256):
    K=ids.shape[0]
    r=jnp.arange(64,dtype=jnp.int32)[:,None]
    hot=(ids[None,:]+1)==r
    hot=hot&(r<32)
    fk=jnp.where(hot,1.0,jnp.where((r>=32)&(r<36),1.0,0.0)).astype(BF)
    fq=jnp.where(hot[:,:Q],BIG,jnp.where(r==32,-BIG,0.0)).astype(BF)
    kb=hot[:32].reshape(32,K//BK,BK).any(-1)
    qb=hot[:32,:Q].reshape(32,Q//BQ,BQ).any(-1)
    act=(qb[:,:,None]&kb[:,None,:]).any(0)
    n=act.sum(-1).astype(jnp.int32)
    NK=K//BK
    before=jnp.arange(NK)[:,None]>jnp.arange(NK)[None,:]
    rank=(act[:,None,:]&before[None]).sum(-1)
    lst=((rank[:,None,:]==jnp.arange(NK)[None,:,None])&act[:,None,:])
    lst=(lst*jnp.arange(NK)[None,None,:]).sum(-1).astype(jnp.int32)
    return fq,fk,n,lst.reshape(-1)


def drop_deps(kern, inputs, extra):
    if not extra:
        return kern
    return lambda *refs: kern(*refs[:inputs], *refs[inputs + extra :])


def cost(flops):
    return pl.CostEstimate(flops=int(flops * 1e-6), bytes_accessed=1024, transcendentals=0)


ANY = pl.BlockSpec(memory_space=pl.ANY)


def whole(shape):
    return pl.BlockSpec(tuple(shape), lambda *_: (0,) * len(shape))


def glue(kern, inputs, outs, bit, deps, name):
    kern = drop_deps(kern, len(inputs) + 1, len(deps))
    return pl.pallas_call(
        kern,
        out_shape=tuple(jax.ShapeDtypeStruct(s, t) for s, t in outs),
        grid_spec=pltpu.PrefetchScalarGridSpec(
            num_scalar_prefetch=1,
            grid=(1,),
            in_specs=[whole(i.shape) for i in inputs] + [ANY] * len(deps),
            out_specs=tuple(whole(s) for s, _ in outs),
        ),
        compiler_params=pltpu.CompilerParams(vmem_limit_bytes=48 * 2**20),
        cost_estimate=cost(1),
        name=name,
    )(bit.reshape(1), *inputs, *deps)


def pair_dp(held, got, bit, cuts=None, deps=()):
    m, rows, cols = held.shape
    cuts = [0, rows] if cuts is None else [0, *cuts, rows]

    def kern(bit_ref, held_ref, got_ref, *outs):
        bit = bit_ref[0]
        for i in range(m):
            for lo, hi, out in zip(cuts, cuts[1:], outs):
                out[i, bit] = held_ref[i, lo:hi]
                out[i, 1 - bit] = got_ref[i, lo:hi]

    outs = [((m, 2, hi - lo, cols), held.dtype) for lo, hi in zip(cuts, cuts[1:])]
    res = glue(kern, (held, got), outs, bit, deps, "pair_dp")
    return [r.reshape(2 * m, r.shape[2], cols) for r in res]


def pair_both(part_a, got_a, part_b, got_b, bit, deps=()):
    m, rows_a, cols = part_a.shape
    rows_b = part_b.shape[1]

    def kern(bit_ref, a, ga, b, gb, out_a, out_b):
        bit = bit_ref[0]
        out_a[0] = a[...]
        out_a[1] = ga[...]
        for i in range(m):
            out_b[i, bit] = b[i]
            out_b[i, 1 - bit] = gb[i]

    outs = [((2, m, rows_a, cols), BF), ((m, 2, rows_b, cols), BF)]
    return glue(kern, (part_a, got_a, part_b, got_b), outs, bit, deps, "pair_both")


def pair_last(part_a, got_a, part_b, got_b, bit, deps=()):
    _, m, rows_a, cols = part_a.shape
    rows_b = part_b.shape[2]

    def kern(bit_ref, a, ga, b, gb, out):
        bit = bit_ref[0]
        for i in range(m):
            for t in range(2):
                out[t, i, bit, :rows_a] = a[t, i]
                out[t, i, 1 - bit, :rows_a] = ga[t, i]
            for y in range(2):
                out[0, i, y, rows_a:] = b[i, y]
                out[1, i, y, rows_a:] = gb[i, y]

    outs = [((2, m, 2, rows_a + rows_b, cols), BF)]
    (res,) = glue(kern, (part_a, got_a, part_b, got_b), outs, bit, deps, "pair_last")
    return res.reshape(2, 2 * m * (rows_a + rows_b), cols)


def fold_dp(kept, got, bit, deps=()):
    n, rows, cols = kept.shape

    def kern(bit_ref, kept_ref, got_ref, keep, send):
        bit = bit_ref[0]
        for i in range(n // 2):
            keep[i] = kept_ref[2 * i + bit].astype(F32) + got_ref[2 * i + bit].astype(F32)
            send[i] = (kept_ref[2 * i + 1 - bit].astype(F32) + got_ref[2 * i + 1 - bit].astype(F32)).astype(BF)

    outs = [((n // 2, rows, cols), F32), ((n // 2, rows, cols), BF)]
    return glue(kern, (kept, got), outs, bit, deps, "fold_dp")


def fold_x(kept, got, bit, deps=()):
    shape = kept.shape[1:]

    def kern(bit_ref, kept_ref, got_ref, keep, send):
        keep[...] = kept_ref[0].astype(F32) + got_ref[0].astype(F32)
        send[...] = (kept_ref[1].astype(F32) + got_ref[1].astype(F32)).astype(BF)

    return glue(kern, (kept, got), [(shape, F32), (shape, BF)], bit, deps, "fold_x")


def split_store(value, bit, keep, send, blocks):
    rows = value.shape[0] // blocks
    for b in range(2):

        @pl.when(bit == b)
        def _(b=b):
            for j in range(blocks):
                part = value[j * rows : (j + 1) * rows].astype(BF)
                if j % 2 == b:
                    keep[j // 2] = part
                else:
                    send[j // 2] = part


def nt(a, b):
    return lax.dot_general(a, b, (((1,), (1,)), ((), ())), preferred_element_type=F32)


def gelu_pair(v):
    x = jnp.abs(v) * (0.5**0.5)
    t = 1.0 / (1.0 + 0.3275911 * x)
    e = jnp.exp2(v * v * (-0.5 * LOG2E))
    poly = ((((1.061405429 * t - 1.453152027) * t + 1.421413741) * t - 0.284496736) * t + 0.254829592) * t
    tail = 0.5 * poly * e
    phi = jnp.where(v < 0, tail, 1.0 - tail)
    return v * phi, phi + v * e * 0.3989422804014327


def mlp_fwd_kernel(bit_ref, n2_ref, cot_ref, wu_ref, wd_ref, slope_ref, keep_ref, part_ref, own_ref, send_ref, cott, acc, *, rows, chunk):
    step = pl.program_id(0) * pl.num_programs(1) + pl.program_id(1)
    last = pl.num_programs(0) * pl.num_programs(1) - 1

    @pl.when(step == 0)
    def _():
        for i in range(rows // chunk):
            s = slice(i * chunk, (i + 1) * chunk)
            cott[:, s] = cot_ref[s, :].T
        acc[...] = jnp.zeros_like(acc)

    total = jnp.zeros(wd_ref.shape, F32)
    for i in range(rows // chunk):
        s = slice(i * chunk, (i + 1) * chunk)
        hid, slope = gelu_pair(nn(n2_ref[s, :], wu_ref[...]))
        slope_ref[s, :] = slope.astype(BF)
        hid = hid.astype(BF)
        acc[s, :] += nt(hid, wd_ref[...])
        total += nn(cott[:, s], hid)
    split_store(total, bit_ref[0], keep_ref, part_ref, 2 * keep_ref.shape[0])

    @pl.when(step == last)
    def _():
        own_ref[...] = acc[: rows // 2]
        send_ref[...] = acc[rows // 2 :].astype(BF)


def mlp_bwd_kernel(bit_ref, n2_ref, cot_ref, wu_ref, wd_ref, slope_ref, keep_ref, part_ref, own_ref, send_ref, n2t, acc, *, rows, chunk):
    step = pl.program_id(0) * pl.num_programs(1) + pl.program_id(1)
    last = pl.num_programs(0) * pl.num_programs(1) - 1

    @pl.when(step == 0)
    def _():
        for i in range(rows // chunk):
            s = slice(i * chunk, (i + 1) * chunk)
            n2t[:, s] = n2_ref[s, :].T
        acc[...] = jnp.zeros_like(acc)

    total = jnp.zeros(wu_ref.shape, F32)
    for i in range(rows // chunk):
        s = slice(i * chunk, (i + 1) * chunk)
        grad = (nn(cot_ref[s, :], wd_ref[...]) * slope_ref[s, :].astype(F32)).astype(BF)
        acc[s, :] += nt(grad, wu_ref[...])
        total += nn(n2t[:, s], grad)
    split_store(total, bit_ref[0], keep_ref, part_ref, 2 * keep_ref.shape[0])

    @pl.when(step == last)
    def _():
        own_ref[...] = acc[: rows // 2]
        send_ref[...] = acc[rows // 2 :].astype(BF)


def mlp_fwd(n2, cot, wu, wd, bit, blocks, deps=()):
    return mlp_call(mlp_fwd_kernel, True, (n2, cot, wu, wd), bit, blocks, deps)


def mlp_bwd(n2, cot, wu, wd, slope, bit, blocks, deps=()):
    return mlp_call(mlp_bwd_kernel, False, (n2, cot, wu, wd, slope), bit, blocks, deps)


def mlp_call(kernel, forward, arrays, bit, blocks, deps):
    rows, width = arrays[0].shape
    cols = arrays[3].shape[2]
    blk = 256
    full = pl.BlockSpec((rows, width), lambda r, c, _: (0, 0))
    half = pl.BlockSpec((rows // 2, width), lambda r, c, _: (0, 0))
    weight = pl.BlockSpec((None, width, blk), lambda r, c, _: (r, 0, c))
    slope = pl.BlockSpec((None, rows, blk), lambda r, c, _: (r, 0, c))
    part = pl.BlockSpec((None, blocks // 2, width // blocks, blk), lambda r, c, _: (r, 0, 0, c))
    part_shape = jax.ShapeDtypeStruct((2, blocks // 2, width // blocks, cols), BF)
    out_specs = (part, part, half, half)
    out_shape = (part_shape, part_shape, jax.ShapeDtypeStruct((rows // 2, width), F32), jax.ShapeDtypeStruct((rows // 2, width), BF))
    if forward:
        out_specs = (slope, *out_specs)
        out_shape = (jax.ShapeDtypeStruct((2, rows, cols), BF), *out_shape)
    kern = functools.partial(kernel, rows=rows, chunk=256)
    return pl.pallas_call(
        drop_deps(kern, len(arrays) + 1, len(deps)),
        out_shape=out_shape,
        grid_spec=pltpu.PrefetchScalarGridSpec(
            num_scalar_prefetch=1,
            grid=(2, cols // blk),
            in_specs=[full, full, weight, weight, slope][: len(arrays)] + [ANY] * len(deps),
            out_specs=out_specs,
            scratch_shapes=[pltpu.VMEM((width, rows), BF), pltpu.VMEM((rows, width), F32)],
        ),
        compiler_params=pltpu.CompilerParams(vmem_limit_bytes=48 * 2**20),
        cost_estimate=cost(1.2e10),
        name="mlp_fwd" if forward else "mlp_bwd",
    )(bit.reshape(1), *arrays, *deps)


def proj_grad_kernel(bit_ref, gkv_ref, gq_ref, x_ref, w_ref, *rest, kv_cols, q_cols, atts):
    rest = list(rest)
    prev_ref = None if atts else rest.pop(0)
    att_refs = [rest.pop(0) for _ in range(atts)]
    branch_ref = rest.pop(0) if atts else None
    keep_ref, part_ref, gx_ref, accw = rest
    step = pl.program_id(0)
    own = pl.num_programs(0) // 2
    gkv = gkv_ref[...]
    x = x_ref[...]

    @pl.when(step == 0)
    def _():
        accw[...] = jnp.zeros_like(accw)

    accw[:kv_cols] += nn(gkv, x)
    base = nt(gkv.T, w_ref[:, :kv_cols])
    if prev_ref is not None:
        base += prev_ref[...].astype(F32)

    @pl.when(step >= own)
    def _():
        gx_ref[...] = base.astype(BF)

    @pl.when(step < own)
    def _():
        gq = gq_ref[...]
        accw[kv_cols : kv_cols + q_cols] += nn(gq, x)
        gx_ref[...] = (base + nt(gq.T, w_ref[:, kv_cols : kv_cols + q_cols])).astype(BF)
        for i, att in enumerate(att_refs):
            lo = kv_cols + (i + 1) * q_cols
            accw[lo : lo + q_cols] += nn(att[...], branch_ref[...])

    @pl.when(step == pl.num_programs(0) - 1)
    def _():
        split_store(accw[...].T, bit_ref[0], keep_ref, part_ref, 2 * keep_ref.shape[0])


def proj_grad(gkv, gq, x, w, bit, blocks, prev=None, atts=(), branch=None, deps=()):
    kv_cols, slots = gkv.shape
    q_cols, q_slots = gq.shape
    width = w.shape[0]
    cols = kv_cols + q_cols * (1 + len(atts))
    blk = slots // 4
    last = q_slots // blk - 1
    kern = functools.partial(proj_grad_kernel, kv_cols=kv_cols, q_cols=q_cols, atts=len(atts))
    thin = pl.BlockSpec((q_cols, blk), lambda s, _: (0, jnp.minimum(s, last)))
    arrays = [gkv, gq, x, w]
    specs = [
        pl.BlockSpec((kv_cols, blk), lambda s, _: (0, s)),
        thin,
        pl.BlockSpec((blk, width), lambda s, _: (s, 0)),
        pl.BlockSpec(w.shape, lambda s, _: (0, 0)),
    ]
    if prev is not None:
        arrays.append(prev)
        specs.append(pl.BlockSpec((None, blk, width), lambda s, _: (s, 0, 0)))
    else:
        arrays += [*atts, branch]
        specs += [thin] * len(atts) + [pl.BlockSpec((blk, width), lambda s, _: (jnp.minimum(s, last), 0))]
    part = (blocks // 2, width // blocks, cols)
    return pl.pallas_call(
        drop_deps(kern, len(arrays) + 1, len(deps)),
        out_shape=(jax.ShapeDtypeStruct(part, BF), jax.ShapeDtypeStruct(part, BF), jax.ShapeDtypeStruct((4, blk, width), BF)),
        grid_spec=pltpu.PrefetchScalarGridSpec(
            num_scalar_prefetch=1,
            grid=(4,),
            in_specs=specs + [ANY] * len(deps),
            out_specs=(whole(part), whole(part), pl.BlockSpec((None, blk, width), lambda s, _: (s, 0, 0))),
            scratch_shapes=[pltpu.VMEM((cols, width), F32)],
        ),
        compiler_params=pltpu.CompilerParams(vmem_limit_bytes=48 * 2**20),
        cost_estimate=cost(5e9),
        name="proj_grad",
    )(bit.reshape(1), *arrays, *deps)


def xor_perm(size, mask):
    return [(i, i ^ mask) for i in range(size)]


def swap(values, axis, mask):
    return lax.ppermute(values, axis, xor_perm(lax.axis_size(axis), mask))


def dp_levels():
    return list(reversed(range(lax.axis_size("dp").bit_length() - 1)))


def after(values, other):
    return values + (other[(0,) * other.ndim] * 0).astype(values.dtype)


def sum_all(values):
    values = values + swap(values, "tensor", 1)
    values = values + swap(values, "tensor", 2)
    for level in reversed(dp_levels()):
        values = values + swap(values, "dp", 1 << level)
    return values


def hat_of(values):
    center = values - jnp.mean(values, axis=-1, keepdims=True)
    inv = lax.rsqrt(jnp.mean(center * center, axis=-1, keepdims=True) + EPSILON)
    return center * inv, inv


def hat_back(grad, gain, hat, inv):
    u = grad * gain
    return inv * (u - jnp.mean(u, axis=-1, keepdims=True) - hat * jnp.mean(u * hat, axis=-1, keepdims=True))


def core_sum(own, send):
    return own.astype(F32) + swap(send, "tensor", 1).astype(F32)


def with_core(own):
    return jnp.concatenate([own, swap(own, "tensor", 1)], axis=0)


def mm(spec, *arrays):
    return jnp.einsum(spec, *arrays, preferred_element_type=F32)


def per_device(tokens, picture_ids, ln1_gain, ln1_bias, w_qkv, q_gain, k_gain, w_out, ln2_gain, ln2_bias, w_up, w_down, cotangent):
    slots, width = tokens.shape[1:]
    local = w_qkv.shape[2]
    fcols = w_up.shape[1]
    dp = lax.axis_size("dp")
    rows = width // dp
    tok = tokens[0]
    cot = cotangent[0]
    tensor = lax.axis_index("tensor")
    me = lax.axis_index("dp")
    levels = dp_levels()
    far, near = levels[:-1], levels[-1]
    bits = {level: (me >> level) & 1 for level in levels}
    n_dp = width // rows
    q_slots = 2 * slots

    def dp_swap(values, level):
        return swap(values, "dp", 1 << level)

    def grow(held, level, deps=(), cuts=None):
        return pair_dp(held, dp_swap(held, level), bits[level], cuts, deps)

    out_t = w_out.T
    part_0 = jnp.concatenate([w_qkv[:, 1], w_qkv[:, 2], w_qkv[:, 0]], axis=1)
    got = swap(jnp.concatenate([part_0, out_t], axis=1), "tensor", 2)
    tok_x = swap(after(tok, got), "tensor", 2)
    tok_c = swap(tok, "tensor", 1)
    part_1 = jnp.concatenate([got, out_t], axis=1)[None]
    part_0 = part_0[None]
    up = w_up[None]
    down = w_down.T[None]
    for i, level in enumerate(far):
        (part_0,) = grow(part_0, level, (part_1,))
        (part_1,) = grow(part_1, level, (part_0,))
        if i == 0:
            up = after(up, part_1)
    half = rows // 3 // 16 * 16 if rows >= 48 else rows // 2
    one = len(far) == 1
    up = grow(up, far[0], (part_1,), (half,) if one else None)
    down = after(down, up[0])
    for level in far[1:-1]:
        up = grow(up[0], level)
    (w_0,) = grow(part_0, near, tuple(up))
    w_0 = w_0.reshape(width, 3 * local)

    tok_xc = swap(tok_x, "tensor", 1)
    cot_all = with_core(cot)
    ids = picture_ids[0].reshape(4, slots)
    ids = jnp.concatenate([lax.dynamic_index_in_dim(ids, tensor ^ i, 0, keepdims=False) for i in range(4)])
    fq, fk, count, blocks = features(ids, q_slots, BQ, BK)
    hats = [hat_of(block.astype(F32)) for block in (tok, tok_c, tok_x, tok_xc)]
    normed = jnp.concatenate([(hat * ln1_gain + ln1_bias).astype(BF) for hat, _ in hats], axis=0)

    def forward(weights, deps):
        kv = mm("sd,dc->cs", normed, weights[:, : 2 * local]).reshape(2, local, 4 * slots)
        q = mm("sd,dc->cs", normed[:q_slots], weights[:, 2 * local : 3 * local])
        att, lse = attn_fwd(count, blocks, q, kv, fq, fk, q_gain, k_gain, HG=HGF, BQ=BQ, BK=BK, deps=deps)
        return q, kv, att, lse

    head_0 = forward(w_0, tuple(up))
    att_0 = head_0[2]
    if not one:
        up = grow(up[0], far[-1], (att_0,), (half,))
    up_a, up_b = up
    got_a = swap(up_a, "tensor", 2)
    got_b = dp_swap(up_b, near)
    down = grow(down, far[0], (up_a,), (half,) if one else None)
    for level in far[1:-1]:
        down = grow(down[0], level)
    (w_1,) = grow(part_1, near, tuple(down))
    w_1 = w_1.reshape(width, 5 * local)
    head_1 = forward(w_1, tuple(down))
    att_1 = head_1[2]

    up_a, up_b = pair_both(up_a, got_a, up_b, got_b, bits[near], (att_1,))
    got_a = dp_swap(up_a, near)
    got_b = swap(up_b, "tensor", 2)
    if not one:
        down = grow(down[0], far[-1], (up_b,), (half,))
    down_a, down_b = down
    dgot_a = swap(down_a, "tensor", 2)
    dgot_b = dp_swap(down_b, near)

    wo = jnp.stack([w_1[:, 4 * local :], w_1[:, 3 * local : 4 * local]])
    heads = (head_0, head_1)
    att_cols = jnp.stack([h[2].reshape(local, q_slots) for h in heads])
    share = mm("rcs,rdc->sd", att_cols, wo)
    middle = tok.astype(F32) + core_sum(share[:slots], share[slots:].astype(BF))
    hat2, inv2 = hat_of(middle)
    normed2 = with_core((hat2 * ln2_gain + ln2_bias).astype(BF))
    down_a, down_b = pair_both(down_a, dgot_a, down_b, dgot_b, bits[near], (normed2,))
    dgot_a = dp_swap(down_a, near)
    dgot_b = swap(down_b, "tensor", 2)
    wu = pair_last(up_a, got_a, up_b, got_b, bits[near])
    wd = pair_last(down_a, dgot_a, down_b, dgot_b, bits[near], (wu,))

    slope, d_keep, d_send, mlp_own, mlp_send = mlp_fwd(normed2, cot_all, wu, wd, bits[near], n_dp)
    d_got = dp_swap(d_send, near)
    u_keep, u_send, gn2_own, gn2_send = mlp_bwd(normed2, cot_all, wu, wd, slope, bits[near], n_dp, (d_send,))
    u_got = dp_swap(u_send, near)
    grad_normed2 = core_sum(gn2_own, gn2_send)
    grad_mid = cot.astype(F32) + hat_back(grad_normed2, ln2_gain, hat2, inv2)
    branch = with_core(grad_mid.astype(BF))
    grad_att = mm("sd,rdc->rcs", branch, wo).astype(BF)
    d_keep, d_send = fold_x(d_keep, d_got, bits[near], (branch,))
    d_got = swap(d_send, "tensor", 2)

    def back(g, deps):
        q, kv, att, lse = heads[g]
        gq, gkv, qg, kg = attn_bwd(
            count, blocks, q, kv, grad_att[g], att, lse, fq, fk, q_gain, k_gain, HG=HGB, BQ=BQ, BK=BK, deps=deps
        )
        return gq.reshape(local, q_slots), gkv.reshape(2 * local, 4 * slots), qg, kg

    rest = levels[::-1][1:]
    gq, gkv, qg_1, kg_1 = back(1, (u_send, d_send))
    u_keep, u_send = fold_x(u_keep, u_got, bits[near], (gq,))
    u_got = swap(u_send, "tensor", 2)
    d_keep, d_send = fold_dp(d_keep, d_got, bits[rest[0]], (gq,))
    d_got = dp_swap(d_send, rest[0])
    a_keep, a_send, gx = proj_grad(
        gkv, gq, normed, w_1, bits[near], n_dp, atts=(att_cols[1], att_cols[0]), branch=branch, deps=(u_send, d_send)
    )
    a_got = dp_swap(a_send, near)
    d_keep, d_send = fold_dp(d_keep, d_got, bits[rest[1]], (gx,))
    d_got = dp_swap(d_send, rest[1])
    gq, gkv, qg_0, kg_0 = back(0, (a_send, d_send))
    u_keep, u_send = fold_dp(u_keep, u_got, bits[rest[0]], (gq,))
    u_got = dp_swap(u_send, rest[0])
    a_keep, a_send = fold_dp(a_keep, a_got, bits[rest[0]], (gq,))
    a_got = dp_swap(a_send, rest[0])
    z_keep, z_send, gx = proj_grad(gkv, gq, normed, w_0, bits[near], n_dp, prev=gx, deps=(u_send, a_send))
    z_got = dp_swap(z_send, near)
    across = core_sum(gx[2], gx[3])
    got = swap(across.astype(BF), "tensor", 2)
    grad_normed = core_sum(gx[0], gx[1])
    u_keep, u_send = fold_dp(u_keep, u_got, bits[rest[1]], (gx,))
    u_got = dp_swap(u_send, rest[1])
    a_keep, a_send = fold_dp(a_keep, a_got, bits[rest[1]], (gx,))
    a_got = dp_swap(a_send, rest[1])

    def finish(keep, got, levels):
        for level in levels:
            keep, send = fold_dp(keep, got, bits[level])
            got = dp_swap(send, level)
        return (keep + got.astype(F32)).reshape(rows, -1)

    grad_zero = finish(z_keep, z_got, rest)
    grad_a = finish(a_keep, a_got, rest[2:])
    grad_u = finish(u_keep, u_got, rest[2:])
    grad_d = finish(d_keep, d_got, rest[2:])
    mine = jnp.concatenate([grad_zero, grad_a[:, 4 * local :]], axis=1)
    grad_one = mine + swap(grad_a[:, : 4 * local].astype(BF), "tensor", 2).astype(F32)

    grad_gain2 = jnp.sum(grad_normed2 * hat2, axis=0)
    grad_bias2 = jnp.sum(grad_normed2, axis=0)
    result = (middle + core_sum(mlp_own, mlp_send)).astype(BF)
    hat1, inv1 = hats[0]
    grad_gain1 = jnp.sum(grad_normed * hat1, axis=0) + jnp.sum(across * hats[2][0], axis=0)
    grad_bias1 = jnp.sum(grad_normed, axis=0) + jnp.sum(across, axis=0)
    gains = jnp.concatenate([(qg_0 + qg_1)[:, 0], (kg_0 + kg_1)[:, 0]])
    small = sum_all(jnp.stack([grad_gain1, grad_bias1, grad_gain2, grad_bias2, jnp.pad(gains, (0, width - 2 * HD))]))
    grad_normed = grad_normed + got.astype(F32)
    grad_tokens = (grad_mid + hat_back(grad_normed, ln1_gain, hat1, inv1)).astype(BF)

    grad_qkv = jnp.stack([grad_one[:, 2 * local : 3 * local], grad_one[:, :local], grad_one[:, local : 2 * local]], axis=1)
    return (
        result[None],
        grad_tokens[None],
        small[0],
        small[1],
        grad_qkv,
        small[4, :HD],
        small[4, HD : 2 * HD],
        grad_one[:, 3 * local :].T,
        small[2],
        small[3],
        grad_u,
        grad_d.T,
    )


BQ = 512
BK = 256
HGF = 3
HGB = 3


def solution(mesh):
    rows = P("dp", "tensor", None)
    wide = P("dp", "tensor")
    tall = P("tensor", "dp")
    qkv = P("dp", None, "tensor")
    in_specs = (rows, P("dp", None), P(), P(), qkv, P(), P(), tall, P(), P(), wide, tall, rows)
    out_specs = (rows, rows, P(), P(), qkv, P(), P(), tall, P(), P(), wide, tall)
    return jax.shard_map(per_device, mesh=mesh, in_specs=in_specs, out_specs=out_specs, check_vma=False)
```

```python
import jax
import jax.numpy as jnp
from jax import lax
from jax.experimental import pallas as pl
from jax.experimental.pallas import tpu as pltpu
from jax.sharding import PartitionSpec as P

HD = 64
EPSILON = 1e-6
LOG2E = 1.4426950408889634
QSCALE = LOG2E / 8.0
BIG = 256.0
F32 = jnp.float32
BF = jnp.bfloat16
BQ = 512
BK = 256
CHUNK = 512
SPLIT = 384


def nn(a, b):
    return lax.dot_general(a, b, (((1,), (0,)), ((), ())), preferred_element_type=F32)


def nt(a, b):
    return lax.dot_general(a, b, (((1,), (1,)), ((), ())), preferred_element_type=F32)


class Queue:
    def __init__(self):
        self.last = ()

    def __call__(self, name, kern, inputs, outs, scalars=(), scratch=(), vmem=8, us=0):
        count = len(scalars) + len(inputs)
        deps = self.last

        def body(*refs):
            kern(*refs[:count], *refs[count + len(deps) :])

        space = lambda where: pl.BlockSpec(memory_space=where)
        res = pl.pallas_call(
            body,
            out_shape=tuple(jax.ShapeDtypeStruct(s, t) for s, t in outs),
            in_specs=[space(pltpu.SMEM)] * len(scalars) + [space(pltpu.VMEM)] * len(inputs) + [space(pl.ANY)] * len(deps),
            out_specs=tuple(space(pltpu.VMEM) for _ in outs),
            scratch_shapes=list(scratch),
            compiler_params=pltpu.CompilerParams(vmem_limit_bytes=vmem * 2**20),
            cost_estimate=pl.CostEstimate(flops=int(us * 1e9), bytes_accessed=0, transcendentals=0),
            name=name,
        )(*scalars, *inputs, *deps)
        self.last = (res[0],)
        return res


def hat_of(values):
    center = values - jnp.mean(values, axis=-1, keepdims=True)
    inv = lax.rsqrt(jnp.mean(center * center, axis=-1, keepdims=True) + EPSILON)
    return center * inv, inv


def hat_back(grad, gain, hat, inv):
    u = grad * gain
    return inv * (u - jnp.mean(u, axis=-1, keepdims=True) - hat * jnp.mean(u * hat, axis=-1, keepdims=True))


STEP = 128


def each(rows, body):
    pl.loop(0, rows // STEP)(lambda i: body(pl.ds(pl.multiple_of(i * STEP, STEP), STEP)))


def norm_pair(queue, one, two, gain, bias, us=0):
    slots, width = one.shape

    def kern(one_ref, two_ref, gain_ref, bias_ref, out_ref):
        for i, ref in enumerate((one_ref, two_ref)):

            def body(s, i=i, ref=ref):
                hat, _ = hat_of(ref[s, :].astype(F32))
                at = pl.ds(pl.multiple_of(s.start + i * slots, STEP), STEP)
                out_ref[at, :] = (hat * gain_ref[...] + bias_ref[...]).astype(BF)

            each(slots, body)

    return queue("norm_pair", kern, (one, two, gain, bias), [((2 * slots, width), BF)], us=us)[0]


def norm_rows(x):
    c = x - jnp.mean(x, axis=0, keepdims=True)
    inv = lax.rsqrt(jnp.mean(c * c, axis=0, keepdims=True) + EPSILON)
    return c * inv, inv


def split3(v):
    hi = v.astype(BF).astype(F32)
    rest = v - hi
    mid = rest.astype(BF).astype(F32)
    return hi, mid, rest - mid


def attn_fwd(queue, tensor, ids, own, oth, w, lo, fq, fk, qg, kg):
    half, width = own.shape
    slots = 2 * half
    cols = (w.shape[1] - lo) // 3
    heads = cols // HD
    nk = slots // BK

    def kern(t_ref, ids_ref, own_ref, oth_ref, w_ref, fq_ref, fk_ref, qg_ref, kg_ref, att_ref, lse_ref, q_ref, k_ref, v_ref, wt_ref, kt, qn, vn, n_ref, l_ref):
        list_blocks(t_ref, ids_ref, slots, n_ref, l_ref)
        q_gain, k_gain = column(qg_ref[...]), column(kg_ref[...])
        ones = jnp.where(lax.broadcasted_iota(jnp.int32, (HD, CHUNK), 0) == 0, 1.0, 0.0).astype(F32)
        wt_ref[...] = w_ref[:, lo:].T
        for c in range(slots // CHUNK):
            s = slice(c * CHUNK, (c + 1) * CHUNK)
            mine = c * CHUNK < half
            x = own_ref[s, :] if mine else oth_ref[c * CHUNK - half : (c + 1) * CHUNK - half, :]
            raw = nt(wt_ref[: 2 * cols], x)
            k_ref[:, s] = raw[:cols]
            v_ref[:, s] = raw[cols:].astype(BF)
            for h in range(heads):
                r = slice(h * HD, (h + 1) * HD)
                kn, _ = norm_rows(raw[r])
                kt[h, :HD, s] = (kn * k_gain).astype(BF)
                kt[h, HD:, s] = fk_ref[:, s]
                vn[h, s, :] = jnp.concatenate([raw[cols + h * HD : cols + (h + 1) * HD], ones], axis=0).T.astype(BF)
            if mine:
                raw = nt(wt_ref[2 * cols :], x)
                q_ref[:, s] = raw
                for h in range(heads):
                    qh, _ = norm_rows(raw[h * HD : (h + 1) * HD])
                    qa = jnp.concatenate([qh * (q_gain * QSCALE), fq_ref[:, s].astype(F32)], axis=0)
                    qn[h, s, :] = qa.T.astype(BF)
        for qb in range(half // BQ):
            s = slice(qb * BQ, (qb + 1) * BQ)

            def body(i, accs, qb=qb, s=s):
                ks = pl.ds(pl.multiple_of(l_ref[qb * nk + i] * BK, BK), BK)
                out = []
                for h in range(heads):
                    p = jnp.exp2(nn(qn[h, s, :], kt[h, :, ks])).astype(BF)
                    out.append(accs[h] + nn(p, vn[h, ks, :]))
                return tuple(out)

            accs = lax.fori_loop(0, n_ref[qb], body, tuple(jnp.zeros((BQ, 2 * HD), F32) for _ in range(heads)))
            for h in range(heads):
                t = accs[h].T
                total = t[HD : HD + 1]
                att_ref[h * HD : (h + 1) * HD, s] = (t[:HD] / total).astype(BF)
                lse_ref[h : h + 1, s] = jnp.log2(total)

    return queue(
        "attn_fwd",
        kern,
        (own, oth, w, fq, fk, qg, kg),
        [((cols, half), BF), ((heads, half), F32), ((cols, half), F32), ((cols, slots), F32), ((cols, slots), BF), ((3 * cols, width), BF)],
        scalars=(tensor, ids),
        scratch=[pltpu.VMEM((heads, 2 * HD, slots), BF), pltpu.VMEM((heads, half, 2 * HD), BF), pltpu.VMEM((heads, slots, 2 * HD), BF), pltpu.SMEM((half // BQ,), jnp.int32), pltpu.SMEM((half // BQ * nk + 1,), jnp.int32)],
        vmem=12,
        us=50,
    )


def attn_bwd(queue, tensor, ids, q, k, v, att, lse, branch, wot, lo, fq, fk, qg, kg, us):
    cols, half = q.shape
    slots = k.shape[1]
    heads = cols // HD
    nk = slots // BK

    def kern(t_ref, ids_ref, q_ref, k_ref, v_ref, att_ref, lse_ref, b0_ref, b1_ref, wot_ref, fq_ref, fk_ref, qg_ref, kg_ref, g_ref, gq_ref, gains_ref, kt, kn, vn, qt, qn, dt, dn, dqt, dk, dv, n_ref, l_ref):
        list_blocks(t_ref, ids_ref, slots, n_ref, l_ref)
        q_gain, k_gain = column(qg_ref[...]), column(kg_ref[...])
        row = lax.broadcasted_iota(jnp.int32, (HD, CHUNK), 0)
        three = jnp.where(row < 3, 1.0, 0.0).astype(F32)
        for c in range(slots // CHUNK):
            s = slice(c * CHUNK, (c + 1) * CHUNK)
            for h in range(heads):
                r = slice(h * HD, (h + 1) * HD)
                hat, _ = norm_rows(k_ref[r, s])
                full = jnp.concatenate([hat * k_gain, fk_ref[:, s].astype(F32)], axis=0)
                kt[h, :, s] = full[:HD].astype(BF)
                kn[h, s, :] = full.T.astype(BF)
                vn[h, s, :] = jnp.concatenate([v_ref[r, s].astype(F32), three], axis=0).T.astype(BF)
                dk[h, s, :] = jnp.zeros((CHUNK, 2 * HD), F32)
                dv[h, s, :] = jnp.zeros((CHUNK, 2 * HD), F32)
        for c in range(half // CHUNK):
            s = slice(c * CHUNK, (c + 1) * CHUNK)
            grad = nt(wot_ref[lo : lo + cols], (b0_ref if c == 0 else b1_ref)[...]).astype(BF).astype(F32)
            for h in range(heads):
                r = slice(h * HD, (h + 1) * HD)
                hat, _ = norm_rows(q_ref[r, s])
                a, b, d = split3(-lse_ref[h : h + 1, s])
                f = fq_ref[:, s].astype(F32)
                f = jnp.where(row == 33, a, jnp.where(row == 34, b, jnp.where(row == 35, d, f)))
                full = jnp.concatenate([hat * (q_gain * QSCALE), f], axis=0)
                qt[h, :, s] = full.astype(BF)
                qn[h, s, :] = full.T.astype(BF)
                a, b, d = split3(-jnp.sum(grad[r] * att_ref[r, s].astype(F32), axis=0, keepdims=True))
                f = jnp.where(row == 0, a, jnp.where(row == 1, b, jnp.where(row == 2, d, 0.0)))
                full = jnp.concatenate([grad[r], f], axis=0)
                dt[h, :, s] = full.astype(BF)
                dn[h, s, :] = full.T.astype(BF)
        for qb in range(half // BQ):
            s = slice(qb * BQ, (qb + 1) * BQ)

            def body(i, accs, qb=qb, s=s):
                ks = pl.ds(pl.multiple_of(l_ref[qb * nk + i] * BK, BK), BK)
                out = []
                for h in range(heads):
                    p = jnp.exp2(nn(kn[h, ks, :], qt[h, :, s]))
                    ds = (p * nn(vn[h, ks, :], dt[h, :, s])).astype(BF)
                    dv[h, ks, :] += nn(p.astype(BF), dn[h, s, :])
                    dk[h, ks, :] += nn(ds, qn[h, s, :])
                    out.append(accs[h] + nn(kt[h, :, ks], ds))
                return tuple(out)

            accs = lax.fori_loop(0, n_ref[qb], body, tuple(jnp.zeros((HD, BQ), F32) for _ in range(heads)))
            for h in range(heads):
                dqt[h, :, s] = accs[h]

        def back(grad, gain, raw):
            hat, inv = norm_rows(raw)
            u = grad * gain
            out = inv * (u - jnp.mean(u, axis=0, keepdims=True) - hat * jnp.mean(u * hat, axis=0, keepdims=True))
            return out.astype(BF), jnp.sum(grad * hat, axis=1, keepdims=True)

        sum_q = jnp.zeros((HD, 1), F32)
        sum_k = jnp.zeros((HD, 1), F32)
        for h in range(heads):
            r = slice(h * HD, (h + 1) * HD)
            for c in range(slots // CHUNK):
                s = slice(c * CHUNK, (c + 1) * CHUNK)
                g_ref[r, s], more = back(dk[h, s, :].T[:HD] * (1.0 / LOG2E), k_gain, k_ref[r, s])
                sum_k += more
                g_ref[cols + h * HD : cols + (h + 1) * HD, s] = dv[h, s, :].T[:HD].astype(BF)
            for c in range(half // CHUNK):
                s = slice(c * CHUNK, (c + 1) * CHUNK)
                gq_ref[r, s], more = back(dqt[h, :, s] * 0.125, q_gain, q_ref[r, s])
                sum_q += more
        gains_ref[:, :1] = sum_q
        gains_ref[:, 1:] = sum_k

    big = (heads, slots, 2 * HD)
    small = (heads, half, 2 * HD)
    flat = (heads, 2 * HD, half)
    return queue(
        "attn_bwd",
        kern,
        (q, k, v, att, lse, *branch, wot, fq, fk, qg, kg),
        [((2 * cols, slots), BF), ((cols, half), BF), ((HD, 2), F32)],
        scalars=(tensor, ids),
        scratch=[
            pltpu.VMEM((heads, HD, slots), BF),
            pltpu.VMEM(big, BF),
            pltpu.VMEM(big, BF),
            pltpu.VMEM(flat, BF),
            pltpu.VMEM(small, BF),
            pltpu.VMEM(flat, BF),
            pltpu.VMEM(small, BF),
            pltpu.VMEM((heads, HD, half), F32),
            pltpu.VMEM(big, F32),
            pltpu.VMEM(big, F32),
            pltpu.SMEM((half // BQ,), jnp.int32),
            pltpu.SMEM((half // BQ * nk + 1,), jnp.int32),
        ],
        vmem=20,
        us=us,
    )


def features(queue, ids, tensor):
    parts, slots = ids.shape

    def kern(t_ref, ids_ref, fq_ref, fk_ref):
        row = lax.broadcasted_iota(jnp.int32, (HD, slots), 0)
        for i in range(parts):
            s = slice(i * slots, (i + 1) * slots)
            hot = ids_ref[pl.ds(t_ref[0] ^ i, 1), :] + 1 == row
            ones = (row >= 32) & (row < 36)
            fk_ref[:, s] = jnp.where((hot & (row < 32)) | ones, 1.0, 0.0).astype(BF)
            if i < 2:
                fq_ref[:, s] = jnp.where(hot & (row < 32), BIG, jnp.where(row == 32, -BIG, 0.0)).astype(BF)

    outs = [((HD, 2 * slots), BF), ((HD, parts * slots), BF)]
    return queue("features", kern, (ids,), outs, scalars=(tensor,))


def list_blocks(t_ref, ids_ref, slots, n_ref, l_ref):
    share = ids_ref.shape[0] // 4

    def ends(block, size):
        at = block * size
        at = (t_ref[0] ^ (at // share)) * share + at % share
        first, last = ids_ref[at], ids_ref[at + size - 1]
        return jnp.where(first < 0, 99, first), jnp.where(last < 0, 99, last)

    nk = slots // BK
    keys = [ends(kb, BK) for kb in range(nk)]
    for qb in range(slots // 2 // BQ):
        first, last = ends(qb, BQ)
        n = jnp.int32(0)
        for kb, (low, high) in enumerate(keys):
            l_ref[qb * nk + n] = kb
            n += ((first <= high) & (low <= last)).astype(jnp.int32)
        n_ref[qb] = n


def column(row):
    n = row.shape[1]
    same = lax.broadcasted_iota(jnp.int32, (n, n), 0) == lax.broadcasted_iota(jnp.int32, (n, n), 1)
    return jnp.sum(jnp.where(same, row, 0.0), axis=1, keepdims=True)


def gelu_pair(v):
    t = 1.0 / (1.0 + (0.3275911 * 0.5**0.5) * jnp.abs(v))
    e = jnp.exp2(v * v * (-0.5 * LOG2E))
    poly = ((((0.5307027145 * t - 0.7265760135) * t + 0.7107068705) * t - 0.142248368) * t + 0.127414796) * t
    tail = poly * e
    phi = jnp.where(v < 0, tail, 1.0 - tail)
    return v * phi, phi + v * e * 0.3989422804014327


def split_store(value, bit, keep, send, blocks, lead=(), at=slice(None)):
    rows = value.shape[0] // blocks
    value = value.astype(BF)
    for b in range(2):

        @pl.when(bit == b)
        def _(b=b):
            for j in range(blocks):
                part = value[j * rows : (j + 1) * rows]
                if j % 2 == b:
                    keep[(*lead, j // 2, slice(None), at)] = part
                else:
                    send[(*lead, j // 2, slice(None), at)] = part


def mlp(queue, xs, gs, wu, wd, bit, blocks, slope=None):
    half, width = xs[0].shape
    cols = wd.shape[2]
    forward = slope is None
    part = 384
    rows = 256
    steps = half // rows

    def kern(bit_ref, x0, x1, g0, g1, wu_ref, wd_ref, *rest):
        rest = list(rest)
        slope_ref = rest.pop(0)
        keep_a, send_a, keep_b, send_b, own_ref, out_ref, hid, turned = rest
        left = (g0, g1) if forward else (x0, x1)
        feed = (x0, x1) if forward else (g0, g1)
        w_in, w_out = (wu_ref, wd_ref) if forward else (wd_ref, wu_ref)
        for i, ref in enumerate(left):
            turned[:, i * half : (i + 1) * half] = ref[...].T
        for i, ref in enumerate(feed):

            @pl.loop(0, 2 * steps)
            def _(j, i=i, ref=ref):
                r = j // steps
                local = pl.multiple_of((j % steps) * rows, rows)
                s = pl.ds(local, rows)
                o = pl.ds(pl.multiple_of(local + i * half, rows), rows)
                for c in range(0, cols, part):
                    at = slice(c, c + part)
                    value = nn(ref[s, :], w_in[r, :, at])
                    if forward:
                        value, grad = gelu_pair(value)
                        slope_ref[r, o, at] = grad.astype(BF)
                    else:
                        value = value * slope_ref[r, o, at].astype(F32)
                    hid[r, o, at] = value.astype(BF)

        for r in range(2):
            for c in range(0, cols, part):
                value = nn(turned[...], hid[r, :, c : c + part])
                if c < SPLIT:
                    split_store(value, bit_ref[0], keep_a, send_a, blocks, (r,), slice(c, c + part))
                else:
                    (send_b if r else keep_b)[:, c - SPLIT : c - SPLIT + part] = value.astype(BF)

        @pl.loop(0, steps)
        def _(j):
            s = pl.ds(pl.multiple_of(j * rows, rows), rows)
            o = pl.ds(pl.multiple_of(j * rows + half, rows), rows)
            own_ref[s, :] = nt(hid[0, s, :], w_out[0]) + nt(hid[1, s, :], w_out[1])
            out_ref[s, :] = (nt(hid[0, o, :], w_out[0]) + nt(hid[1, o, :], w_out[1])).astype(BF)

    part_a = ((2, blocks // 2, width // blocks, SPLIT), BF)
    part_b = ((width, cols - SPLIT), BF)
    outs = [part_a, part_a, part_b, part_b, ((half, width), F32), ((half, width), BF)]
    inputs = [*xs, *gs, wu, wd]
    if forward:
        outs = [((2, 2 * half, cols), BF), *outs]
    else:
        inputs.append(slope)
    return queue(
        "mlp_fwd" if forward else "mlp_bwd",
        kern,
        inputs,
        outs,
        scalars=(bit,),
        scratch=[pltpu.VMEM((2, 2 * half, cols), BF), pltpu.VMEM((width, 2 * half), BF)],
        vmem=14,
        us=50,
    )


def out_proj(queue, atts, w, lo):
    cols, slots = atts[0].shape
    width = w.shape[0]
    half = slots // 2

    def kern(a0, a1, w_ref, own_ref, send_ref, wot_ref):
        wot_ref[...] = w_ref[:, :lo].T
        for i, out in enumerate((own_ref, send_ref)):
            s = slice(i * half, (i + 1) * half)
            both = jnp.concatenate([a0[:, s], a1[:, s]], axis=0)
            out[...] = nn(both.T, wot_ref[...]).astype(out.dtype)

    outs = [((half, width), F32), ((half, width), BF), ((lo, width), BF)]
    return queue("out_proj", kern, (*atts, w), outs)


def middle_norm(queue, own, got, tok, gain, bias):
    slots, width = own.shape

    def kern(own_ref, got_ref, tok_ref, gain_ref, bias_ref, mid_ref, out_ref):
        def body(s):
            mid = tok_ref[s, :].astype(F32) + own_ref[s, :] + got_ref[s, :].astype(F32)
            mid_ref[s, :] = mid
            hat, _ = hat_of(mid)
            out_ref[s, :] = (hat * gain_ref[...] + bias_ref[...]).astype(BF)

        each(slots, body)

    return queue("middle_norm", kern, (own, got, tok, gain, bias), [((slots, width), F32), ((slots, width), BF)])


def middle_back(queue, own, got, mid, cot, gain):
    slots, width = own.shape

    def kern(own_ref, got_ref, mid_ref, cot_ref, gain_ref, grad_ref, out_ref, sums_ref):
        sums_ref[...] = jnp.zeros_like(sums_ref)

        def body(s):
            grad = own_ref[s, :] + got_ref[s, :].astype(F32)
            hat, inv = hat_of(mid_ref[s, :])
            sums_ref[0:1] += jnp.sum(grad * hat, axis=0, keepdims=True)
            sums_ref[1:2] += jnp.sum(grad, axis=0, keepdims=True)
            grad = cot_ref[s, :].astype(F32) + hat_back(grad, gain_ref[...], hat, inv)
            grad_ref[s, :] = grad
            out_ref[s, :] = grad.astype(BF)

        each(slots, body)

    outs = [((slots, width), F32), ((slots, width), BF), ((2, width), F32)]
    return queue("middle_back", kern, (own, got, mid, cot, gain), outs, us=50)


def proj_grad(queue, g, gq, own, oth, wt, bit, blocks, prev=(), atts=(), branch=()):
    two, slots = g.shape
    cols, half = gq.shape
    width = own.shape[1]
    block = half // 2
    lead = cols * len(atts)

    def kern(bit_ref, g_ref, gq_ref, own_ref, oth_ref, wt_ref, *rest):
        rest = list(rest)
        prev_refs = [rest.pop(0) for _ in prev]
        att_refs = [rest.pop(0) for _ in atts]
        branch_refs = [rest.pop(0) for _ in branch]
        keep_ref, send_ref = rest[:2]
        outs = rest[2:]
        for i in reversed(range(4)):
            s = slice(i * block, (i + 1) * block)
            value = nn(g_ref[:, s].T, wt_ref[:two])
            if i < 2:
                value += nn(gq_ref[:, s].T, wt_ref[two:])
            if prev_refs:
                value += prev_refs[i][...].astype(F32)
            outs[i][...] = value.astype(BF)
        parts = []
        for att in att_refs:
            parts.append(nn(att[:, :block], branch_refs[0][...]) + nn(att[:, block:], branch_refs[1][...]))
        parts.append(nn(g_ref[:, :half], own_ref[...]) + nn(g_ref[:, half:], oth_ref[...]))
        parts.append(nn(gq_ref[...], own_ref[...]))
        split_store(jnp.concatenate(parts, axis=0).T, bit_ref[0], keep_ref, send_ref, blocks)

    share = ((blocks // 2, width // blocks, lead + two + cols), BF)
    return queue(
        "proj_grad",
        kern,
        (g, gq, own, oth, wt, *prev, *atts, *branch),
        [share, share] + [((block, width), BF)] * 4,
        scalars=(bit,),
        vmem=16,
        us=50,
    )


def norm_sums(queue, own, got, tok, across, tok_x):
    slots, width = tok.shape

    def kern(own_ref, got_ref, tok_ref, across_ref, tok_x_ref, grad_ref, sums_ref):
        sums_ref[...] = jnp.zeros_like(sums_ref)

        def body(s):
            grad = own_ref[s, :].astype(F32) + got_ref[s, :].astype(F32)
            grad_ref[s, :] = grad
            other = across_ref[s, :].astype(F32)
            hat, _ = hat_of(tok_ref[s, :].astype(F32))
            hat_x, _ = hat_of(tok_x_ref[s, :].astype(F32))
            sums_ref[0:1] += jnp.sum(grad * hat + other * hat_x, axis=0, keepdims=True)
            sums_ref[1:2] += jnp.sum(grad + other, axis=0, keepdims=True)

        each(slots, body)

    return queue("norm_sums", kern, (own, got, tok, across, tok_x), [((slots, width), F32), ((2, width), F32)])


def tokens_back(queue, grad, got, tok, gain, mid):
    slots, width = tok.shape

    def kern(grad_ref, got_ref, tok_ref, gain_ref, mid_ref, out_ref):
        def body(s):
            hat, inv = hat_of(tok_ref[s, :].astype(F32))
            grad = grad_ref[s, :] + got_ref[s, :].astype(F32)
            out_ref[s, :] = (mid_ref[s, :] + hat_back(grad, gain_ref[...], hat, inv)).astype(BF)

        each(slots, body)

    return queue("tokens_back", kern, (grad, got, tok, gain, mid), [((slots, width), BF)])[0]


def add_up(queue, one, two, dtype):
    def kern(a, b, out):
        out[...] = (a[...].astype(F32) + b[...].astype(F32)).astype(dtype)

    return queue("add_up", kern, (one, two), [(one.shape, dtype)])[0]


def side_by_side(queue, *arrays, us=0):
    edges = [0]
    for a in arrays:
        edges.append(edges[-1] + a.shape[1])

    def kern(*refs):
        for ref, lo, hi in zip(refs, edges, edges[1:]):
            refs[-1][:, lo:hi] = ref[...]

    return queue("side_by_side", kern, arrays, [((arrays[0].shape[0], edges[-1]), BF)], us=us)[0]


def pair_dp(queue, held, got, bit, cuts=None):
    m, rows, cols = held.shape
    cuts = [0, rows] if cuts is None else [0, *cuts, rows]

    def kern(bit_ref, held_ref, got_ref, *outs):
        bit = bit_ref[0]
        for i in range(m):
            for lo, hi, out in zip(cuts, cuts[1:], outs):
                out[2 * i + bit] = held_ref[i, lo:hi]
                out[2 * i + 1 - bit] = got_ref[i, lo:hi]

    outs = [((2 * m, hi - lo, cols), held.dtype) for lo, hi in zip(cuts, cuts[1:])]
    return queue("pair_dp", kern, (held, got), outs, scalars=(bit,))


def pair_both(queue, part_a, got_a, part_b, got_b, bit):
    m, rows_a, cols = part_a.shape
    rows_b = part_b.shape[1]

    def kern(bit_ref, a, ga, b, gb, out_a, out_b):
        bit = bit_ref[0]
        out_a[0] = a[...]
        out_a[1] = ga[...]
        for i in range(m):
            out_b[i, bit] = b[i]
            out_b[i, 1 - bit] = gb[i]

    outs = [((2, m, rows_a, cols), BF), ((m, 2, rows_b, cols), BF)]
    return queue("pair_both", kern, (part_a, got_a, part_b, got_b), outs, scalars=(bit,))


def pair_last(queue, part_a, got_a, part_b, got_b, bit):
    _, m, rows_a, cols = part_a.shape
    rows_b = part_b.shape[2]

    def kern(bit_ref, a, ga, b, gb, out):
        bit = bit_ref[0]
        for i in range(m):
            for t in range(2):
                out[t, i, bit, :rows_a] = a[t, i]
                out[t, i, 1 - bit, :rows_a] = ga[t, i]
            for y in range(2):
                out[0, i, y, rows_a:] = b[i, y]
                out[1, i, y, rows_a:] = gb[i, y]

    outs = [((2, m, 2, rows_a + rows_b, cols), BF)]
    (res,) = queue("pair_last", kern, (part_a, got_a, part_b, got_b), outs, scalars=(bit,))
    return res.reshape(2, 2 * m * (rows_a + rows_b), cols)


def fold_dp(queue, kept, got, bit):
    n, rows, cols = kept.shape

    def kern(bit_ref, kept_ref, got_ref, keep, send):
        bit = bit_ref[0]
        for i in range(n // 2):
            keep[i] = kept_ref[2 * i + bit].astype(F32) + got_ref[2 * i + bit].astype(F32)
            send[i] = (kept_ref[2 * i + 1 - bit].astype(F32) + got_ref[2 * i + 1 - bit].astype(F32)).astype(BF)

    outs = [((n // 2, rows, cols), F32), ((n // 2, rows, cols), BF)]
    return queue("fold_dp", kern, (kept, got), outs, scalars=(bit,))


def fold_both(queue, keep_a, got_a, keep_b, got_b, bit, us=0):
    _, n, rows, cols_a = keep_a.shape
    cols_b = keep_b.shape[-1]

    def kern(bit_ref, ka, ga, kb, gb, keep_a, send_a, keep_b, send_b):
        bit = bit_ref[0]
        keep_a[...] = ka[0].astype(F32) + ga[0].astype(F32)
        send_a[...] = (ka[1].astype(F32) + ga[1].astype(F32)).astype(BF)
        for i in range(n):
            keep_b[i] = kb[2 * i + bit].astype(F32) + gb[2 * i + bit].astype(F32)
            send_b[i] = (kb[2 * i + 1 - bit].astype(F32) + gb[2 * i + 1 - bit].astype(F32)).astype(BF)

    outs = [((n, rows, cols_a), F32), ((n, rows, cols_a), BF), ((n, rows, cols_b), F32), ((n, rows, cols_b), BF)]
    return queue("fold_both", kern, (keep_a, got_a, keep_b, got_b), outs, scalars=(bit,), us=us)


def fold_joined(queue, keep_a, got_a, keep_b, got_b, bit):
    n, rows, cols_a = keep_a.shape
    cols = cols_a + keep_b.shape[-1]

    def kern(bit_ref, ka, ga, kb, gb, keep, send):
        bit = bit_ref[0]
        for i in range(n // 2):
            for k, g, at in ((ka, ga, slice(0, cols_a)), (kb, gb, slice(cols_a, cols))):
                keep[i, :, at] = k[2 * i + bit] + g[2 * i + bit].astype(F32)
                send[i, :, at] = (k[2 * i + 1 - bit] + g[2 * i + 1 - bit].astype(F32)).astype(BF)

    outs = [((n // 2, rows, cols), F32), ((n // 2, rows, cols), BF)]
    return queue("fold_joined", kern, (keep_a, got_a, keep_b, got_b), outs, scalars=(bit,))


def fold_x(queue, kept, got, cols):
    n, rows, total = kept.shape

    def kern(kept_ref, got_ref, keep, send):
        for i in range(n):
            value = kept_ref[i].astype(F32) + got_ref[i].astype(F32)
            keep[i] = value[:, :cols].astype(BF)
            send[i] = value[:, cols:].astype(BF)

    return queue("fold_x", kern, (kept, got), [((n, rows, cols), BF), ((n, rows, total - cols), BF)])


def fold_joint(queue, lead, across, kept, got, bit):
    n, rows, cols = across.shape
    first = lead.shape[2]

    def kern(bit_ref, lead_ref, across_ref, kept_ref, got_ref, keep, send):
        bit = bit_ref[0]
        for i in range(n // 2):
            for out, j in ((keep, 2 * i + bit), (send, 2 * i + 1 - bit)):
                rest = kept_ref[j].astype(F32) + got_ref[j].astype(F32)
                value = jnp.concatenate([lead_ref[j].astype(F32), rest], axis=1) + across_ref[j].astype(F32)
                out[i] = value.astype(out.dtype)

    outs = [((n // 2, rows, cols), F32), ((n // 2, rows, cols), BF)]
    return queue("fold_joint", kern, (lead, across, kept, got), outs, scalars=(bit,))


def swap(values, axis, mask):
    return lax.ppermute(values, axis, [(i, i ^ mask) for i in range(lax.axis_size(axis))])


def swap_core(values):
    return swap(values, "tensor", 1)


def swap_x(values):
    return swap(values, "tensor", 2)


def per_device(tokens, picture_ids, ln1_gain, ln1_bias, w_qkv, q_gain, k_gain, w_out, ln2_gain, ln2_bias, w_up, w_down, cotangent):
    slots, width = tokens.shape[1:]
    local = w_qkv.shape[2]
    n_dp = lax.axis_size("dp")
    rows = width // n_dp
    q_slots = 2 * slots
    tok = tokens[0]
    cot = cotangent[0]
    tensor = lax.axis_index("tensor").reshape(1)
    me = lax.axis_index("dp")
    levels = list(reversed(range(n_dp.bit_length() - 1)))
    far, near = levels[:-1], levels[-1]
    bits = {level: ((me >> level) & 1).reshape(1) for level in levels}
    queue = Queue()
    gain1, bias1, gain2, bias2 = (v.reshape(1, width) for v in (ln1_gain, ln1_bias, ln2_gain, ln2_bias))
    qg, kg = q_gain.reshape(1, HD), k_gain.reshape(1, HD)

    def swap_dp(values, level):
        return swap(values, "dp", 1 << level)

    out_t = w_out.T
    part_0 = jnp.concatenate([w_qkv[:, 1], w_qkv[:, 2], w_qkv[:, 0]], axis=1)
    own_cols = jnp.concatenate([out_t, part_0], axis=1)
    part_0 = part_0[None]
    got_cols = swap_x(own_cols)
    got = swap_dp(part_0, far[0])
    tok_c = swap_core(tok)
    cot_c = swap_core(cot)
    ids = picture_ids[0]
    fq, fk = features(queue, ids.reshape(4, slots), tensor)

    half = rows // 2
    (part_0,) = pair_dp(queue, part_0, got, bits[far[0]])
    part_1 = side_by_side(queue, out_t, got_cols)[None]
    got_0 = swap_dp(part_0, levels[1])
    got_1 = swap_dp(part_1, far[0])
    tok_x = swap_x(side_by_side(queue, tok))
    up = side_by_side(queue, w_up)[None]
    down = side_by_side(queue, w_down.T)[None]
    for level, after_it in zip(levels[1:-1], levels[2:]):
        (part_0,) = pair_dp(queue, part_0, got_0, bits[level])
        got_0 = swap_dp(part_0, after_it)
    for level, after_it in zip(levels[:-2], levels[1:-1]):
        (part_1,) = pair_dp(queue, part_1, got_1, bits[level])
        got_1 = swap_dp(part_1, after_it)
    got_u = swap_dp(up, far[0])
    own = norm_pair(queue, tok, tok_c, gain1, bias1, us=50)
    (part_1,) = pair_dp(queue, part_1, got_1, bits[levels[-2]])
    got_1 = swap_dp(part_1, levels[-1])
    got_d = swap_dp(side_by_side(queue, down[0])[None], far[0])
    for level, after_it in zip(far[:-1], far[1:]):
        (up,) = pair_dp(queue, up, got_u, bits[level])
        got_u = swap_dp(up, after_it)
    tok_xc = swap_core(side_by_side(queue, tok_x, us=50))
    oth = norm_pair(queue, tok_x, tok_xc, gain1, bias1)
    (w_0,) = pair_dp(queue, part_0, got_0, bits[near])
    w_0 = w_0.reshape(width, 3 * local)
    att_0, lse_0, q_0, k_0, v_0, wt_0 = attn_fwd(queue, tensor, ids, own, oth, w_0, 0, fq, fk, qg, kg)
    for level, after_it in zip(far[:-1], far[1:]):
        (down,) = pair_dp(queue, down, got_d, bits[level])
        got_d = swap_dp(down, after_it)
    up_a, up_b = pair_dp(queue, up, got_u, bits[far[-1]], (half,))
    ua, ub = swap_x(up_a), swap_dp(up_b, near)
    (w_1,) = pair_dp(queue, part_1, got_1, bits[near])
    w_1 = w_1.reshape(width, 5 * local)
    att_1, lse_1, q_1, k_1, v_1, wt_1 = attn_fwd(queue, tensor, ids, own, oth, w_1, 2 * local, fq, fk, qg, kg)
    up_a, up_b = pair_both(queue, up_a, ua, up_b, ub, bits[near])
    down_a, down_b = pair_dp(queue, down, got_d, bits[far[-1]], (half,))
    ua, ub = swap_dp(up_a, near), swap_x(up_b)
    da, db = swap_x(down_a), swap_dp(down_b, near)
    branch_own, branch_send, wot = out_proj(queue, (att_0, att_1), w_1, 2 * local)
    middle, normed = middle_norm(queue, branch_own, swap_core(branch_send), tok, gain2, bias2)
    normed_c = swap_core(normed)
    down_a, down_b = pair_both(queue, down_a, da, down_b, db, bits[near])
    da, db = swap_dp(down_a, near), swap_x(down_b)
    wu = pair_last(queue, up_a, ua, up_b, ub, bits[near])
    wd = pair_last(queue, down_a, da, down_b, db, bits[near])

    bit = bits[near]
    rest = levels[::-1][1:]
    xs, gs = (normed, normed_c), (cot, cot_c)
    grid = (n_dp, rows, w_up.shape[1] - SPLIT)

    def first_step(parts):
        keep_a, send_a, keep_b, send_b = parts
        return keep_a, swap_dp(send_a, near), keep_b.reshape(grid), swap_x(send_b).reshape(grid)

    def second_step(keep_a, send_a, keep_b, send_b):
        return keep_a, swap_x(send_a), keep_b, swap_dp(send_b, near)

    def next_step(keep, send, level):
        return keep, swap_dp(send, level)

    slope, *parts, mlp_own, mlp_send = mlp(queue, xs, gs, wu, wd, bit, n_dp)
    d = first_step(parts)
    *parts, gn_own, gn_send = mlp(queue, xs, gs, wu, wd, bit, n_dp, slope)
    d = second_step(*fold_both(queue, *d, bit, us=50))
    u = first_step(parts)
    grad_mid, branch, sums2 = middle_back(queue, gn_own, swap_core(gn_send), middle, cot, gain2)
    branches = (branch, swap_core(branch))
    g, gq, gains_1 = attn_bwd(queue, tensor, ids, q_1, k_1, v_1, att_1, lse_1, branches, wot, local, fq, fk, qg, kg, 0)
    u = second_step(*fold_both(queue, *u, bit))
    d = next_step(*fold_joined(queue, *d, bits[rest[0]]), rest[0])
    a_keep, a_send, *gx = proj_grad(queue, g, gq, own, oth, wt_1, bit, n_dp, atts=(att_0, att_1), branch=branches)
    a = next_step(a_keep, a_send, near)
    u = next_step(*fold_joined(queue, *u, bits[rest[0]]), rest[0])
    d = next_step(*fold_dp(queue, *d, bits[rest[1]]), rest[1])
    g, gq, gains_0 = attn_bwd(queue, tensor, ids, q_0, k_0, v_0, att_0, lse_0, branches, wot, 0, fq, fk, qg, kg, 50)
    a_keep, a_send = fold_x(queue, *a, local)
    a_got = swap_x(a_send)
    u = next_step(*fold_dp(queue, *u, bits[rest[1]]), rest[1])
    for level in rest[2:]:
        d = next_step(*fold_dp(queue, *d, bits[level]), level)
        u = next_step(*fold_dp(queue, *u, bits[level]), level)
    z_keep, z_send, *gx = proj_grad(queue, g, gq, own, oth, wt_0, bit, n_dp, prev=gx)
    z = next_step(z_keep, z_send, near)
    got_own, got_across = swap_core(gx[1]), swap_core(gx[3])
    across = add_up(queue, gx[2], got_across, BF)
    got = swap_x(across)
    gains = jnp.pad((gains_0 + gains_1).T, ((0, 0), (0, width - HD)))
    grad_normed, sums1 = norm_sums(queue, gx[0], got_own, tok, across, tok_x)
    small = jnp.concatenate([sums1, sums2, gains])
    small = add_up(queue, small, swap_core(small), F32)
    small_got = swap_x(small)
    z = next_step(*fold_joint(queue, a_keep, a_got, *z, bits[rest[0]]), rest[0])
    grad_tokens = tokens_back(queue, grad_normed, got, tok, gain1, grad_mid)
    turns = levels[::-1]
    for turn, level in zip(turns, rest[1:] + [None] * 2):
        small = add_up(queue, small, small_got, F32)
        small_got = swap_dp(small, turn)
        if level is not None:
            z = next_step(*fold_dp(queue, *z, bits[level]), level)
    grad_d = add_up(queue, *d, F32).reshape(rows, -1)
    grad_u = add_up(queue, *u, F32).reshape(rows, -1)
    grad_z = add_up(queue, *z, F32).reshape(rows, -1)
    small = add_up(queue, small, small_got, F32)
    qkv = grad_z[:, local:]
    grad_qkv = jnp.stack([qkv[:, 2 * local :], qkv[:, :local], qkv[:, local : 2 * local]], axis=1)
    result = (middle + mlp_own + swap_core(mlp_send).astype(F32)).astype(BF)
    return (
        result[None],
        grad_tokens[None],
        small[0],
        small[1],
        grad_qkv,
        small[4, :HD],
        small[5, :HD],
        grad_z[:, :local].T,
        small[2],
        small[3],
        grad_u,
        grad_d.T,
    )


def solution(mesh):
    rows = P("dp", "tensor", None)
    wide = P("dp", "tensor")
    tall = P("tensor", "dp")
    qkv = P("dp", None, "tensor")
    in_specs = (rows, P("dp", None), P(), P(), qkv, P(), P(), tall, P(), P(), wide, tall, rows)
    out_specs = (rows, rows, P(), P(), qkv, P(), P(), tall, P(), P(), wide, tall)
    return jax.shard_map(per_device, mesh=mesh, in_specs=in_specs, out_specs=out_specs, check_vma=False)
```

```python
import jax
import jax.numpy as jnp
from jax import lax
from jax.experimental import pallas as pl
from jax.experimental.pallas import tpu as pltpu
from jax.sharding import PartitionSpec as P

HD = 64
EPSILON = 1e-6
LOG2E = 1.4426950408889634
QSCALE = LOG2E / 8.0
BIG = 256.0
F32 = jnp.float32
BF = jnp.bfloat16
BQ = 512
BK_FWD = 512
BK_BWD = 256
CHUNK = 512


def nn(a, b):
    return lax.dot_general(a, b, (((1,), (0,)), ((), ())), preferred_element_type=F32)


def nt(a, b):
    return lax.dot_general(a, b, (((1,), (1,)), ((), ())), preferred_element_type=F32)


class Queue:
    def __init__(self):
        self.last = ()

    def __call__(self, name, kern, inputs, outs, scalars=(), scratch=(), vmem=4, us=0, fetched=()):
        count = len(scalars) + len(inputs)
        deps = self.last
        skip = count + len(fetched) + len(deps)

        def body(*refs):
            if not fetched:
                return kern(*refs[:count], *refs[skip:])
            copies = refs[-1 - len(fetched) : -1]
            moves = [pltpu.make_async_copy(a, b, refs[-1].at[i]) for i, (a, b) in enumerate(zip(refs[count:skip], copies))]
            for move in moves:
                move.start()
            for move in moves:
                move.wait()
            kern(*refs[:count], *refs[skip:-1])

        space = lambda where: pl.BlockSpec(memory_space=where)
        landing = [pltpu.VMEM(a.shape, a.dtype) for a in fetched]
        if fetched:
            landing.append(pltpu.SemaphoreType.DMA((len(fetched),)))
        res = pl.pallas_call(
            body,
            out_shape=tuple(jax.ShapeDtypeStruct(s, t) for s, t in outs),
            in_specs=[space(pltpu.SMEM)] * len(scalars) + [space(pltpu.VMEM)] * len(inputs) + [space(pl.ANY)] * (len(fetched) + len(deps)),
            out_specs=tuple(space(pltpu.VMEM) for _ in outs),
            scratch_shapes=[*scratch, *landing],
            compiler_params=pltpu.CompilerParams(vmem_limit_bytes=vmem * 2**20),
            cost_estimate=pl.CostEstimate(flops=int(us * 50e8 / 50), bytes_accessed=0, transcendentals=0),
            name=name,
        )(*scalars, *inputs, *fetched, *deps)
        self.last = (res[0],)
        return res


def hat_of(values):
    center = values - jnp.mean(values, axis=-1, keepdims=True)
    inv = lax.rsqrt(jnp.mean(center * center, axis=-1, keepdims=True) + EPSILON)
    return center * inv, inv


def hat_back(grad, gain, hat, inv):
    u = grad * gain
    return inv * (u - jnp.mean(u, axis=-1, keepdims=True) - hat * jnp.mean(u * hat, axis=-1, keepdims=True))


STEP = 128


def each(rows, body):
    pl.loop(0, rows // STEP)(lambda i: body(pl.ds(pl.multiple_of(i * STEP, STEP), STEP)))


def norm_pair(queue, one, two, gain, bias, us=0):
    slots, width = one.shape

    def kern(one_ref, two_ref, gain_ref, bias_ref, out_ref):
        for i, ref in enumerate((one_ref, two_ref)):

            def body(s, i=i, ref=ref):
                hat, _ = hat_of(ref[s, :].astype(F32))
                at = pl.ds(pl.multiple_of(s.start + i * slots, STEP), STEP)
                out_ref[at, :] = (hat * gain_ref[...] + bias_ref[...]).astype(BF)

            each(slots, body)

    return queue("norm_pair", kern, (one, two, gain, bias), [((2 * slots, width), BF)], us=us)[0]


def norm_rows(x):
    c = x - jnp.mean(x, axis=0, keepdims=True)
    inv = lax.rsqrt(jnp.mean(c * c, axis=0, keepdims=True) + EPSILON)
    return c * inv, inv


def split3(v):
    hi = v.astype(BF).astype(F32)
    rest = v - hi
    mid = rest.astype(BF).astype(F32)
    return hi, mid, rest - mid


def attn_fwd(queue, tensor, ids, own, oth, w, lo, fq, fk, qg, kg):
    half, width = own.shape
    slots = 2 * half
    cols = (w.shape[1] - lo) // 3
    heads = cols // HD
    nk = slots // BK_FWD

    def kern(t_ref, ids_ref, own_ref, oth_ref, w_ref, fq_ref, fk_ref, qg_ref, kg_ref, att_ref, lse_ref, q_ref, k_ref, v_ref, wt_ref, qi_ref, ki_ref, kt, qn, vn, n_ref, l_ref):
        list_blocks(t_ref, ids_ref, slots, BK_FWD, n_ref, l_ref)
        q_gain, k_gain = column(qg_ref[...]), column(kg_ref[...])
        ones = jnp.where(lax.broadcasted_iota(jnp.int32, (HD, CHUNK), 0) == 0, 1.0, 0.0).astype(F32)
        wt_ref[...] = w_ref[:, lo:].T
        for c in range(slots // CHUNK):
            s = slice(c * CHUNK, (c + 1) * CHUNK)
            mine = c * CHUNK < half
            x = own_ref[s, :] if mine else oth_ref[c * CHUNK - half : (c + 1) * CHUNK - half, :]
            raw = nt(wt_ref[: 2 * cols], x)
            v_ref[:, s] = raw[cols:].astype(BF)
            for h in range(heads):
                r = slice(h * HD, (h + 1) * HD)
                kn, ki_ref[h : h + 1, s] = norm_rows(raw[r])
                kn = (kn * k_gain).astype(BF)
                k_ref[r, s] = kn
                kt[h, :HD, s] = kn
                kt[h, HD:, s] = fk_ref[:, s]
                vn[h, s, :] = jnp.concatenate([raw[cols + h * HD : cols + (h + 1) * HD], ones], axis=0).T.astype(BF)
            if mine:
                raw = nt(wt_ref[2 * cols :], x)
                for h in range(heads):
                    r = slice(h * HD, (h + 1) * HD)
                    qh, qi_ref[h : h + 1, s] = norm_rows(raw[r])
                    qh = qh * (q_gain * QSCALE)
                    q_ref[r, s] = qh.astype(BF)
                    qa = jnp.concatenate([qh, fq_ref[:, s].astype(F32)], axis=0)
                    qn[h, s, :] = qa.T.astype(BF)
        for qb in range(half // BQ):
            s = slice(qb * BQ, (qb + 1) * BQ)

            def body(i, accs, qb=qb, s=s):
                ks = pl.ds(pl.multiple_of(l_ref[qb * nk + i] * BK_FWD, BK_FWD), BK_FWD)
                out = []
                for h in range(heads):
                    p = jnp.exp2(nn(qn[h, s, :], kt[h, :, ks])).astype(BF)
                    out.append(accs[h] + nn(p, vn[h, ks, :]))
                return tuple(out)

            accs = lax.fori_loop(0, n_ref[qb], body, tuple(jnp.zeros((BQ, 2 * HD), F32) for _ in range(heads)))
            for h in range(heads):
                t = accs[h].T
                total = t[HD : HD + 1]
                att_ref[h * HD : (h + 1) * HD, s] = (t[:HD] / total).astype(BF)
                lse_ref[h : h + 1, s] = jnp.log2(total)

    return queue(
        "attn_fwd",
        kern,
        (own, oth, w, fq, fk, qg, kg),
        [
            ((cols, half), BF),
            ((heads, half), F32),
            ((cols, half), BF),
            ((cols, slots), BF),
            ((cols, slots), BF),
            ((3 * cols, width), BF),
            ((heads, half), F32),
            ((heads, slots), F32),
        ],
        scalars=(tensor, ids),
        scratch=[pltpu.VMEM((heads, 2 * HD, slots), BF), pltpu.VMEM((heads, half, 2 * HD), BF), pltpu.VMEM((heads, slots, 2 * HD), BF), pltpu.SMEM((half // BQ,), jnp.int32), pltpu.SMEM((half // BQ * nk + 1,), jnp.int32)],
        vmem=12,
        us=50,
    )


def attn_bwd(queue, tensor, ids, q, k, v, qi, ki, att, lse, branch, wot, lo, fq, fk, qg, kg, us):
    cols, half = q.shape
    slots = k.shape[1]
    heads = cols // HD
    nk = slots // BK_BWD

    def kern(t_ref, ids_ref, q_ref, k_ref, v_ref, qi_ref, ki_ref, att_ref, lse_ref, b0_ref, b1_ref, wot_ref, fq_ref, fk_ref, qg_ref, kg_ref, g_ref, gq_ref, gains_ref, kn, vn, qt, qn, dt, dn, dqt, dk, dv, n_ref, l_ref):
        list_blocks(t_ref, ids_ref, slots, BK_BWD, n_ref, l_ref)
        q_gain, k_gain = column(qg_ref[...]), column(kg_ref[...])
        row = lax.broadcasted_iota(jnp.int32, (HD, CHUNK), 0)
        three = jnp.where(row < 3, 1.0, 0.0).astype(F32)
        for c in range(slots // CHUNK):
            s = slice(c * CHUNK, (c + 1) * CHUNK)
            for h in range(heads):
                r = slice(h * HD, (h + 1) * HD)
                full = jnp.concatenate([k_ref[r, s], fk_ref[:, s]], axis=0).astype(F32)
                kn[h, s, :] = full.T.astype(BF)
                vn[h, s, :] = jnp.concatenate([v_ref[r, s].astype(F32), three], axis=0).T.astype(BF)
                dk[h, s, :] = jnp.zeros((CHUNK, 2 * HD), F32)
                dv[h, s, :] = jnp.zeros((CHUNK, 2 * HD), F32)
        for c in range(half // CHUNK):
            s = slice(c * CHUNK, (c + 1) * CHUNK)
            grad = nt(wot_ref[lo : lo + cols], (b0_ref if c == 0 else b1_ref)[...]).astype(BF).astype(F32)
            for h in range(heads):
                r = slice(h * HD, (h + 1) * HD)
                a, b, d = split3(-lse_ref[h : h + 1, s])
                f = fq_ref[:, s].astype(F32)
                f = jnp.where(row == 33, a, jnp.where(row == 34, b, jnp.where(row == 35, d, f)))
                full = jnp.concatenate([q_ref[r, s].astype(F32), f], axis=0)
                qt[h, :, s] = full.astype(BF)
                qn[h, s, :] = full.T.astype(BF)
                a, b, d = split3(-jnp.sum(grad[r] * att_ref[r, s].astype(F32), axis=0, keepdims=True))
                f = jnp.where(row == 0, a, jnp.where(row == 1, b, jnp.where(row == 2, d, 0.0)))
                full = jnp.concatenate([grad[r], f], axis=0)
                dt[h, :, s] = full.astype(BF)
                dn[h, s, :] = full.T.astype(BF)
        for qb in range(half // BQ):
            s = slice(qb * BQ, (qb + 1) * BQ)

            def body(i, accs, qb=qb, s=s):
                ks = pl.ds(pl.multiple_of(l_ref[qb * nk + i] * BK_BWD, BK_BWD), BK_BWD)
                out = []
                for h in range(heads):
                    p = jnp.exp2(nn(kn[h, ks, :], qt[h, :, s]))
                    ds = (p * nn(vn[h, ks, :], dt[h, :, s])).astype(BF)
                    dv[h, ks, :] += nn(p.astype(BF), dn[h, s, :])
                    dk[h, ks, :] += nn(ds, qn[h, s, :])
                    out.append(accs[h] + nn(k_ref[h * HD : (h + 1) * HD, ks], ds))
                return tuple(out)

            accs = lax.fori_loop(0, n_ref[qb], body, tuple(jnp.zeros((HD, BQ), F32) for _ in range(heads)))
            for h in range(heads):
                dqt[h, :, s] = accs[h]

        def back(grad, gain, hat, inv):
            u = grad * gain
            out = inv * (u - jnp.mean(u, axis=0, keepdims=True) - hat * jnp.mean(u * hat, axis=0, keepdims=True))
            return out.astype(BF), jnp.sum(grad * hat, axis=1, keepdims=True)

        sum_q = jnp.zeros((HD, 1), F32)
        sum_k = jnp.zeros((HD, 1), F32)
        for h in range(heads):
            r = slice(h * HD, (h + 1) * HD)
            for c in range(slots // CHUNK):
                s = slice(c * CHUNK, (c + 1) * CHUNK)
                g_ref[r, s], more = back(dk[h, s, :].T[:HD] * (1.0 / LOG2E), k_gain, k_ref[r, s].astype(F32) * (1.0 / k_gain), ki_ref[h : h + 1, s])
                sum_k += more
                g_ref[cols + h * HD : cols + (h + 1) * HD, s] = dv[h, s, :].T[:HD].astype(BF)
            for c in range(half // CHUNK):
                s = slice(c * CHUNK, (c + 1) * CHUNK)
                gq_ref[r, s], more = back(dqt[h, :, s] * 0.125, q_gain, q_ref[r, s].astype(F32) * (1.0 / (q_gain * QSCALE)), qi_ref[h : h + 1, s])
                sum_q += more
        gains_ref[:, :1] = sum_q
        gains_ref[:, 1:] = sum_k

    big = (heads, slots, 2 * HD)
    small = (heads, half, 2 * HD)
    flat = (heads, 2 * HD, half)
    return queue(
        "attn_bwd",
        kern,
        (q, k, v, qi, ki, att, lse, *branch, wot, fq, fk, qg, kg),
        [((2 * cols, slots), BF), ((cols, half), BF), ((HD, 2), F32)],
        scalars=(tensor, ids),
        scratch=[
            pltpu.VMEM(big, BF),
            pltpu.VMEM(big, BF),
            pltpu.VMEM(flat, BF),
            pltpu.VMEM(small, BF),
            pltpu.VMEM(flat, BF),
            pltpu.VMEM(small, BF),
            pltpu.VMEM((heads, HD, half), F32),
            pltpu.VMEM(big, F32),
            pltpu.VMEM(big, F32),
            pltpu.SMEM((half // BQ,), jnp.int32),
            pltpu.SMEM((half // BQ * nk + 1,), jnp.int32),
        ],
        vmem=18,
        us=us,
    )


def features(queue, ids, tensor):
    parts, slots = ids.shape

    def kern(t_ref, ids_ref, fq_ref, fk_ref):
        row = lax.broadcasted_iota(jnp.int32, (HD, slots), 0)
        for i in range(parts):
            s = slice(i * slots, (i + 1) * slots)
            hot = ids_ref[pl.ds(t_ref[0] ^ i, 1), :] + 1 == row
            ones = (row >= 32) & (row < 36)
            fk_ref[:, s] = jnp.where((hot & (row < 32)) | ones, 1.0, 0.0).astype(BF)
            if i < 2:
                fq_ref[:, s] = jnp.where(hot & (row < 32), BIG, jnp.where(row == 32, -BIG, 0.0)).astype(BF)

    outs = [((HD, 2 * slots), BF), ((HD, parts * slots), BF)]
    return queue("features", kern, (ids,), outs, scalars=(tensor,), us=50)


def list_blocks(t_ref, ids_ref, slots, size, n_ref, l_ref):
    share = ids_ref.shape[0] // 4

    def ends(block, length):
        at = block * length
        at = (t_ref[0] ^ (at // share)) * share + at % share
        first, last = ids_ref[at], ids_ref[at + length - 1]
        return jnp.where(first < 0, 99, first), jnp.where(last < 0, 99, last)

    nk = slots // size
    keys = [ends(kb, size) for kb in range(nk)]
    for qb in range(slots // 2 // BQ):
        first, last = ends(qb, BQ)
        n = jnp.int32(0)
        for kb, (low, high) in enumerate(keys):
            l_ref[qb * nk + n] = kb
            n += ((first <= high) & (low <= last)).astype(jnp.int32)
        n_ref[qb] = n


def column(row):
    n = row.shape[1]
    same = lax.broadcasted_iota(jnp.int32, (n, n), 0) == lax.broadcasted_iota(jnp.int32, (n, n), 1)
    return jnp.sum(jnp.where(same, row, 0.0), axis=1, keepdims=True)


def gelu_pair(v):
    t = 1.0 / (1.0 + (0.3275911 * 0.5**0.5) * jnp.abs(v))
    e = jnp.exp2(v * v * (-0.5 * LOG2E))
    poly = ((((0.5307027145 * t - 0.7265760135) * t + 0.7107068705) * t - 0.142248368) * t + 0.127414796) * t
    tail = poly * e
    phi = jnp.where(v < 0, tail, 1.0 - tail)
    return v * phi, phi + v * e * 0.3989422804014327


def split_store(value, bit, keep, send, blocks, lead=(), at=slice(None)):
    rows = value.shape[0] // blocks
    value = value.astype(BF)
    for b in range(2):

        @pl.when(bit == b)
        def _(b=b):
            for j in range(blocks):
                part = value[j * rows : (j + 1) * rows]
                if j % 2 == b:
                    keep[(*lead, j // 2, slice(None), at)] = part
                else:
                    send[(*lead, j // 2, slice(None), at)] = part


COLS = 256
PLACES = ((0, 0, 0, 256), (256, 1, 0, 256), (512, 0, 256, 128), (640, 1, 256, 128))
HALF_COLS = 384


def mlp(queue, xs, gs, both, bit, blocks, slope=None):
    half, width = xs[0].shape
    cols = both.shape[2] // 2
    forward = slope is None
    rows = 256

    def kern(bit_ref, x0, x1, g0, g1, w_ref, *rest):
        rest = list(rest)
        if forward:
            hid = rest.pop(0)
        slope_ref = rest.pop(0)
        if forward:
            keep_a, send_a, keep_b, send_b, turned = rest
        else:
            keep_a, send_a, keep_b, send_b, own_ref, out_ref, hid, turned = rest
        left = (g0, g1) if forward else (x0, x1)
        feed = (x0, x1) if forward else (g0, g1)
        w_in, w_out = (0, cols) if forward else (cols, 0)
        for i, ref in enumerate(left):
            turned[:, i * half : (i + 1) * half] = ref[...].T

        def units(r, i, c, lo):
            o = slice(lo + i * half, lo + i * half + rows)
            at = slice(c, c + COLS)
            value = nn(feed[i][lo : lo + rows, :], w_ref[r, :, w_in + c : w_in + c + COLS])
            if forward:
                value, grad = gelu_pair(value)
                slope_ref[r, o, at] = grad.astype(BF)
            else:
                value = value * slope_ref[r, o, at].astype(F32)
            hid[r, o, at] = value.astype(BF)

        def weights(r, c):
            value = nn(turned[...], hid[r, :, c : c + COLS])
            for first, part, to, count in PLACES:
                if c <= first < c + COLS:
                    piece = value[:, first - c : first - c + count]
                    if part == 0:
                        split_store(piece, bit_ref[0], keep_a, send_a, blocks, (r,), slice(to, to + count))
                    else:
                        (send_b if r else keep_b)[:, to : to + count] = piece.astype(BF)

        tiles = [(i, c, lo) for i in range(2) for lo in range(0, half, rows) for c in range(0, cols, COLS)]
        for tile in tiles:
            units(0, *tile)
        turn = len(tiles) * COLS // cols
        for k, tile in enumerate(tiles):
            units(1, *tile)
            if k % turn == turn - 1:
                weights(0, k // turn * COLS)
        for c in range(0, cols, COLS):
            weights(1, c)
        if not forward:
            shares(hid, w_ref, slice(w_out, w_out + cols), own_ref, out_ref)

    part_a = ((2, blocks // 2, width // blocks, HALF_COLS), BF)
    part_b = ((width, cols - HALF_COLS), BF)
    outs = [part_a, part_a, part_b, part_b]
    inputs = [*xs, *gs, both]
    flat = (2, 2 * half, cols)
    scratch = [pltpu.VMEM((width, 2 * half), BF)]
    if forward:
        outs = [(flat, BF), (flat, BF), *outs]
    else:
        inputs.append(slope)
        outs += [((half, width), F32), ((half, width), BF)]
        scratch.insert(0, pltpu.VMEM(flat, BF))
    return queue("mlp_fwd" if forward else "mlp_bwd", kern, inputs, outs, scalars=(bit,), scratch=scratch, vmem=16, us=0)


def shares(hid, w_ref, at, own_ref, out_ref):
    half = own_ref.shape[0]
    rows = 256
    for i, out in enumerate((own_ref, out_ref)):
        for lo in range(0, half, rows):
            o = slice(lo + i * half, lo + i * half + rows)
            out[lo : lo + rows, :] = (nt(hid[0, o, :], w_ref[0, :, at]) + nt(hid[1, o, :], w_ref[1, :, at])).astype(out.dtype)


def mlp_out(queue, hid, both, us):
    _, slots, cols = hid.shape
    width = both.shape[1]

    def kern(hid_ref, w_ref, own_ref, out_ref):
        shares(hid_ref, w_ref, slice(cols, 2 * cols), own_ref, out_ref)

    outs = [((slots // 2, width), F32), ((slots // 2, width), BF)]
    return queue("mlp_out", kern, (hid, both), outs, us=us)


def out_proj(queue, atts, w, lo):
    cols, slots = atts[0].shape
    width = w.shape[0]
    half = slots // 2

    def kern(a0, a1, w_ref, own_ref, send_ref, wot_ref):
        wot_ref[...] = w_ref[:, :lo].T
        for i, out in enumerate((own_ref, send_ref)):
            s = slice(i * half, (i + 1) * half)
            both = jnp.concatenate([a0[:, s], a1[:, s]], axis=0)
            out[...] = nn(both.T, wot_ref[...]).astype(out.dtype)

    outs = [((half, width), F32), ((half, width), BF), ((lo, width), BF)]
    return queue("out_proj", kern, (*atts, w), outs)


def middle_norm(queue, own, got, tok, gain, bias):
    slots, width = own.shape

    def kern(own_ref, got_ref, tok_ref, gain_ref, bias_ref, mid_ref, out_ref):
        def body(s):
            mid = tok_ref[s, :].astype(F32) + own_ref[s, :] + got_ref[s, :].astype(F32)
            mid_ref[s, :] = mid
            hat, _ = hat_of(mid)
            out_ref[s, :] = (hat * gain_ref[...] + bias_ref[...]).astype(BF)

        each(slots, body)

    outs = [((slots, width), F32), ((slots, width), BF)]
    return queue("middle_norm", kern, (own, got, tok, gain, bias), outs, us=50)


def middle_back(queue, own, got, mid, cot, gain):
    slots, width = own.shape

    def kern(own_ref, got_ref, mid_ref, cot_ref, gain_ref, grad_ref, out_ref, sums_ref):
        sums_ref[...] = jnp.zeros_like(sums_ref)

        def body(s):
            grad = own_ref[s, :] + got_ref[s, :].astype(F32)
            hat, inv = hat_of(mid_ref[s, :])
            sums_ref[0:1] += jnp.sum(grad * hat, axis=0, keepdims=True)
            sums_ref[1:2] += jnp.sum(grad, axis=0, keepdims=True)
            grad = cot_ref[s, :].astype(F32) + hat_back(grad, gain_ref[...], hat, inv)
            grad_ref[s, :] = grad
            out_ref[s, :] = grad.astype(BF)

        each(slots, body)

    outs = [((slots, width), F32), ((slots, width), BF), ((2, width), F32)]
    return queue("middle_back", kern, (own, got, mid, cot, gain), outs, us=50)


def proj_grad(queue, g, gq, own, oth, wt, bit, blocks, prev=(), atts=(), branch=()):
    two, slots = g.shape
    cols, half = gq.shape
    width = own.shape[1]
    block = half // 2
    lead = cols * len(atts)

    def kern(bit_ref, g_ref, gq_ref, own_ref, oth_ref, wt_ref, *rest):
        rest = list(rest)
        prev_refs = [rest.pop(0) for _ in prev]
        att_refs = [rest.pop(0) for _ in atts]
        branch_refs = [rest.pop(0) for _ in branch]
        keep_ref, send_ref = rest[:2]
        outs = rest[2:]
        for i in reversed(range(4)):
            s = slice(i * block, (i + 1) * block)
            value = nn(g_ref[:, s].T, wt_ref[:two])
            if i < 2:
                value += nn(gq_ref[:, s].T, wt_ref[two:])
            if prev_refs:
                value += prev_refs[i][...].astype(F32)
            outs[i][...] = value.astype(BF)
        parts = []
        for att in att_refs:
            parts.append(nn(att[:, :block], branch_refs[0][...]) + nn(att[:, block:], branch_refs[1][...]))
        parts.append(nn(g_ref[:, :half], own_ref[...]) + nn(g_ref[:, half:], oth_ref[...]))
        parts.append(nn(gq_ref[...], own_ref[...]))
        split_store(jnp.concatenate(parts, axis=0).T, bit_ref[0], keep_ref, send_ref, blocks)

    share = ((blocks // 2, width // blocks, lead + two + cols), BF)
    return queue(
        "proj_grad",
        kern,
        (g, gq, own, oth, wt, *prev, *atts, *branch),
        [share, share] + [((block, width), BF)] * 4,
        scalars=(bit,),
        vmem=8,
        us=50,
    )


def norm_sums(queue, grads, toks):
    slots, width = toks[0].shape

    def kern(*refs):
        sums_ref = refs[4]
        sums_ref[...] = jnp.zeros_like(sums_ref)

        def body(s):
            first = jnp.zeros((1, width), F32)
            second = jnp.zeros((1, width), F32)
            for grad_ref, tok_ref in zip(refs[:4], refs[5:]):
                grad = grad_ref[s, :].astype(F32)
                hat, _ = hat_of(tok_ref[s, :].astype(F32))
                first += jnp.sum(grad * hat, axis=0, keepdims=True)
                second += jnp.sum(grad, axis=0, keepdims=True)
            sums_ref[0:1] += first
            sums_ref[1:2] += second

        each(slots, body)

    return queue("norm_sums", kern, grads, [((2, width), F32)], vmem=6, fetched=toks)[0]


def tokens_back(queue, own, got_core, got_x, tok, gain, mid):
    slots, width = tok.shape

    def kern(own_ref, core_ref, x_ref, tok_ref, gain_ref, mid_ref, out_ref):
        def body(s):
            hat, inv = hat_of(tok_ref[s, :].astype(F32))
            grad = own_ref[s, :].astype(F32) + core_ref[s, :].astype(F32) + x_ref[s, :].astype(F32)
            out_ref[s, :] = (mid_ref[s, :] + hat_back(grad, gain_ref[...], hat, inv)).astype(BF)

        each(slots, body)

    return queue("tokens_back", kern, (own, got_core, got_x, tok, gain, mid), [((slots, width), BF)])[0]


def last_sum(queue, kept, got, cols):
    _, rows, _ = kept.shape

    def kern(kept_ref, got_ref, out_ref, qkv_ref):
        value = kept_ref[0] + got_ref[0].astype(F32)
        out_ref[...] = value[:, :cols].T
        for i in range(3):
            lo = cols * (1 + (2, 0, 1)[i])
            qkv_ref[:, i, :] = value[:, lo : lo + cols]

    return queue("last_sum", kern, (kept, got), [((cols, rows), F32), ((rows, 3, cols), F32)])


def gain_rows(queue, one, two, width, us):
    def kern(a, b, out):
        value = (a[...] + b[...]).T
        out[...] = jnp.concatenate([value, jnp.zeros((2, width - HD), F32)], axis=1)

    return queue("gain_rows", kern, (one, two), [((2, width), F32)], us=us)[0]


def add_up(queue, one, two, dtype, us=0):
    def kern(a, b, out):
        out[...] = (a[...].astype(F32) + b[...].astype(F32)).astype(dtype)

    return queue("add_up", kern, (one, two), [(one.shape, dtype)], us=us)[0]


def side_by_side(queue, *arrays, us=0):
    edges = [0]
    for a in arrays:
        edges.append(edges[-1] + a.shape[1])

    def kern(*refs):
        for ref, lo, hi in zip(refs, edges, edges[1:]):
            refs[-1][:, lo:hi] = ref[...]

    return queue("side_by_side", kern, arrays, [((arrays[0].shape[0], edges[-1]), BF)], us=us)[0]


def pair_dp(queue, held, got, bit, cuts=None):
    m, rows, cols = held.shape
    cuts = [0, rows] if cuts is None else [0, *cuts, rows]

    def kern(bit_ref, held_ref, got_ref, *outs):
        bit = bit_ref[0]
        for i in range(m):
            for lo, hi, out in zip(cuts, cuts[1:], outs):
                out[2 * i + bit] = held_ref[i, lo:hi]
                out[2 * i + 1 - bit] = got_ref[i, lo:hi]

    outs = [((2 * m, hi - lo, cols), held.dtype) for lo, hi in zip(cuts, cuts[1:])]
    return queue("pair_dp", kern, (held, got), outs, scalars=(bit,))


def pair_both(queue, part_a, got_a, part_b, got_b, bit):
    m, rows_a, cols = part_a.shape
    rows_b = part_b.shape[1]

    def kern(bit_ref, a, ga, b, gb, out_a, out_b):
        bit = bit_ref[0]
        out_a[0] = a[...]
        out_a[1] = ga[...]
        for i in range(m):
            out_b[i, bit] = b[i]
            out_b[i, 1 - bit] = gb[i]

    outs = [((2, m, rows_a, cols), BF), ((m, 2, rows_b, cols), BF)]
    return queue("pair_both", kern, (part_a, got_a, part_b, got_b), outs, scalars=(bit,))


def pair_last(queue, part_a, got_a, part_b, got_b, bit):
    _, m, rows_a, cols = part_a.shape
    rows_b = part_b.shape[2]

    def kern(bit_ref, a, ga, b, gb, out):
        bit = bit_ref[0]
        for i in range(m):
            for t in range(2):
                out[t, i, bit, :rows_a] = a[t, i]
                out[t, i, 1 - bit, :rows_a] = ga[t, i]
            for y in range(2):
                out[0, i, y, rows_a:] = b[i, y]
                out[1, i, y, rows_a:] = gb[i, y]

    outs = [((2, m, 2, rows_a + rows_b, cols), BF)]
    (res,) = queue("pair_last", kern, (part_a, got_a, part_b, got_b), outs, scalars=(bit,))
    return res.reshape(2, 2 * m * (rows_a + rows_b), cols)


def fold_dp(queue, kept, got, bit):
    n, rows, cols = kept.shape

    def kern(bit_ref, kept_ref, got_ref, keep, send):
        bit = bit_ref[0]
        for i in range(n // 2):
            keep[i] = kept_ref[2 * i + bit].astype(F32) + got_ref[2 * i + bit].astype(F32)
            send[i] = (kept_ref[2 * i + 1 - bit].astype(F32) + got_ref[2 * i + 1 - bit].astype(F32)).astype(BF)

    outs = [((n // 2, rows, cols), F32), ((n // 2, rows, cols), BF)]
    return queue("fold_dp", kern, (kept, got), outs, scalars=(bit,))


def fold_both(queue, keep_a, got_a, keep_b, got_b, bit, us=0):
    _, n, rows, cols_a = keep_a.shape
    cols_b = keep_b.shape[-1]

    def kern(bit_ref, ka, ga, kb, gb, keep_a, send_a, keep_b, send_b):
        bit = bit_ref[0]
        keep_a[...] = ka[0].astype(F32) + ga[0].astype(F32)
        send_a[...] = (ka[1].astype(F32) + ga[1].astype(F32)).astype(BF)
        for i in range(n):
            keep_b[i] = kb[2 * i + bit].astype(F32) + gb[2 * i + bit].astype(F32)
            send_b[i] = (kb[2 * i + 1 - bit].astype(F32) + gb[2 * i + 1 - bit].astype(F32)).astype(BF)

    outs = [((n, rows, cols_a), F32), ((n, rows, cols_a), BF), ((n, rows, cols_b), F32), ((n, rows, cols_b), BF)]
    return queue("fold_both", kern, (keep_a, got_a, keep_b, got_b), outs, scalars=(bit,), us=us)


def fold_joined(queue, keep_a, got_a, keep_b, got_b, bit):
    n, rows, cols_a = keep_a.shape
    cols = cols_a + keep_b.shape[-1]

    def kern(bit_ref, ka, ga, kb, gb, keep, send):
        bit = bit_ref[0]
        for i in range(n // 2):
            for first, part, at, count in PLACES:
                k, g = ((ka, ga), (kb, gb))[part]
                to, at = slice(first, first + count), slice(at, at + count)
                keep[i, :, to] = k[2 * i + bit, :, at] + g[2 * i + bit, :, at].astype(F32)
                send[i, :, to] = (k[2 * i + 1 - bit, :, at] + g[2 * i + 1 - bit, :, at].astype(F32)).astype(BF)

    outs = [((n // 2, rows, cols), F32), ((n // 2, rows, cols), BF)]
    return queue("fold_joined", kern, (keep_a, got_a, keep_b, got_b), outs, scalars=(bit,))


def fold_x(queue, kept, got, cols):
    n, rows, total = kept.shape

    def kern(kept_ref, got_ref, keep, send):
        for i in range(n):
            value = kept_ref[i].astype(F32) + got_ref[i].astype(F32)
            keep[i] = value[:, :cols].astype(BF)
            send[i] = value[:, cols:].astype(BF)

    return queue("fold_x", kern, (kept, got), [((n, rows, cols), BF), ((n, rows, total - cols), BF)])


def fold_joint(queue, lead, across, kept, got, bit):
    n, rows, cols = across.shape
    first = lead.shape[2]

    def kern(bit_ref, lead_ref, across_ref, kept_ref, got_ref, keep, send):
        bit = bit_ref[0]
        for i in range(n // 2):
            for out, j in ((keep, 2 * i + bit), (send, 2 * i + 1 - bit)):
                rest = kept_ref[j].astype(F32) + got_ref[j].astype(F32)
                value = jnp.concatenate([lead_ref[j].astype(F32), rest], axis=1) + across_ref[j].astype(F32)
                out[i] = value.astype(out.dtype)

    outs = [((n // 2, rows, cols), F32), ((n // 2, rows, cols), BF)]
    return queue("fold_joint", kern, (lead, across, kept, got), outs, scalars=(bit,))


def swap(values, axis, mask):
    return lax.ppermute(values, axis, [(i, i ^ mask) for i in range(lax.axis_size(axis))])


def swap_core(values):
    return swap(values, "tensor", 1)


def swap_x(values):
    return swap(values, "tensor", 2)


def per_device(tokens, picture_ids, ln1_gain, ln1_bias, w_qkv, q_gain, k_gain, w_out, ln2_gain, ln2_bias, w_up, w_down, cotangent):
    slots, width = tokens.shape[1:]
    local = w_qkv.shape[2]
    n_dp = lax.axis_size("dp")
    rows = width // n_dp
    q_slots = 2 * slots
    tok = tokens[0]
    cot = cotangent[0]
    tensor = lax.axis_index("tensor").reshape(1)
    me = lax.axis_index("dp")
    levels = list(reversed(range(n_dp.bit_length() - 1)))
    far, near = levels[:-1], levels[-1]
    bits = {level: ((me >> level) & 1).reshape(1) for level in levels}
    queue = Queue()
    gain1, bias1, gain2, bias2 = (v.reshape(1, width) for v in (ln1_gain, ln1_bias, ln2_gain, ln2_bias))
    qg, kg = q_gain.reshape(1, HD), k_gain.reshape(1, HD)

    def swap_dp(values, level):
        return swap(values, "dp", 1 << level)

    out_t = w_out.T
    part_0 = jnp.concatenate([w_qkv[:, 1], w_qkv[:, 2], w_qkv[:, 0]], axis=1)
    part_0 = side_by_side(queue, part_0)
    got_0 = swap_dp(part_0[None], far[0])
    ids = picture_ids[0]
    fq, fk = features(queue, ids.reshape(4, slots), tensor)
    got_cols = swap_x(side_by_side(queue, out_t, part_0))
    tok_x = swap_x(side_by_side(queue, tok, us=50))
    tok_c = swap_core(tok)
    cot_c = swap_core(cot)
    both = side_by_side(queue, w_up, w_down.T)[None]
    half = rows // 2
    (part_0,) = pair_dp(queue, part_0[None], got_0, bits[far[0]])
    part_1 = side_by_side(queue, out_t, got_cols)[None]
    got_0 = swap_dp(part_0, levels[1])
    got_1 = swap_dp(part_1, far[0])
    for level, after_it in zip(levels[1:-1], levels[2:]):
        (part_0,) = pair_dp(queue, part_0, got_0, bits[level])
        got_0 = swap_dp(part_0, after_it)
    for level, after_it in zip(levels[:-2], levels[1:-1]):
        (part_1,) = pair_dp(queue, part_1, got_1, bits[level])
        got_1 = swap_dp(part_1, after_it)
    both = side_by_side(queue, both[0])[None]
    got_b = swap_dp(both, far[0])
    own = norm_pair(queue, tok, tok_c, gain1, bias1, us=50)
    (part_1,) = pair_dp(queue, part_1, got_1, bits[levels[-2]])
    got_1 = swap_dp(part_1, levels[-1])
    (w_0,) = pair_dp(queue, part_0, got_0, bits[near])
    w_0 = w_0.reshape(width, 3 * local)
    for level, after_it in zip(far[:-1], far[1:]):
        (both,) = pair_dp(queue, both, got_b, bits[level])
        got_b = swap_dp(both, after_it)
    tok_xc = swap_core(side_by_side(queue, tok_x))
    oth = norm_pair(queue, tok_x, tok_xc, gain1, bias1)
    att_0, lse_0, q_0, k_0, v_0, wt_0, qi_0, ki_0 = attn_fwd(queue, tensor, ids, own, oth, w_0, 0, fq, fk, qg, kg)
    part_a, part_b = pair_dp(queue, both, got_b, bits[far[-1]], (half,))
    got_a, got_b = swap_x(part_a), swap_dp(part_b, near)
    (w_1,) = pair_dp(queue, part_1, got_1, bits[near])
    w_1 = w_1.reshape(width, 5 * local)
    att_1, lse_1, q_1, k_1, v_1, wt_1, qi_1, ki_1 = attn_fwd(queue, tensor, ids, own, oth, w_1, 2 * local, fq, fk, qg, kg)
    part_a, part_b = pair_both(queue, part_a, got_a, part_b, got_b, bits[near])
    got_a, got_b = swap_dp(part_a, near), swap_x(part_b)
    branch_own, branch_send, wot = out_proj(queue, (att_0, att_1), w_1, 2 * local)
    middle, normed = middle_norm(queue, branch_own, swap_core(branch_send), tok, gain2, bias2)
    normed_c = swap_core(normed)
    both = pair_last(queue, part_a, got_a, part_b, got_b, bits[near])

    bit = bits[near]
    rest = levels[::-1][1:]
    xs, gs = (normed, normed_c), (cot, cot_c)
    grid = (n_dp, rows, w_up.shape[1] - HALF_COLS)

    def first_step(parts):
        keep_a, send_a, keep_b, send_b = parts
        return keep_a, swap_dp(send_a, near), keep_b.reshape(grid), swap_x(send_b).reshape(grid)

    def second_step(keep_a, send_a, keep_b, send_b):
        return keep_a, swap_x(send_a), keep_b, swap_dp(send_b, near)

    def next_step(keep, send, level):
        return keep, swap_dp(send, level)

    hid, slope, *parts = mlp(queue, xs, gs, both, bit, n_dp)
    d = first_step(parts)
    mlp_own, mlp_send = mlp_out(queue, hid, both, 50)
    *parts, gn_own, gn_send = mlp(queue, xs, gs, both, bit, n_dp, slope)
    d = second_step(*fold_both(queue, *d, bit, us=50))
    u = first_step(parts)
    grad_mid, branch, sums2 = middle_back(queue, gn_own, swap_core(gn_send), middle, cot, gain2)
    branches = (branch, swap_core(branch))
    g, gq, gains_1 = attn_bwd(queue, tensor, ids, q_1, k_1, v_1, qi_1, ki_1, att_1, lse_1, branches, wot, local, fq, fk, qg, kg, 0)
    u = second_step(*fold_both(queue, *u, bit))
    d = next_step(*fold_joined(queue, *d, bits[rest[0]]), rest[0])
    a_keep, a_send, *gx = proj_grad(queue, g, gq, own, oth, wt_1, bit, n_dp, atts=(att_0, att_1), branch=branches)
    a = next_step(a_keep, a_send, near)
    u = next_step(*fold_joined(queue, *u, bits[rest[0]]), rest[0])
    d = next_step(*fold_dp(queue, *d, bits[rest[1]]), rest[1])
    g, gq, gains_0 = attn_bwd(queue, tensor, ids, q_0, k_0, v_0, qi_0, ki_0, att_0, lse_0, branches, wot, 0, fq, fk, qg, kg, 50)
    a_keep, a_send = fold_x(queue, *a, local)
    a_got = swap_x(a_send)
    u = next_step(*fold_dp(queue, *u, bits[rest[1]]), rest[1])
    for level in rest[2:]:
        d = next_step(*fold_dp(queue, *d, bits[level]), level)
        u = next_step(*fold_dp(queue, *u, bits[level]), level)
    z_keep, z_send, *gx = proj_grad(queue, g, gq, own, oth, wt_0, bit, n_dp, prev=gx)
    z = next_step(z_keep, z_send, near)
    got_own, got_across = swap_core(gx[1]), swap_core(gx[3])
    gains = gain_rows(queue, gains_0, gains_1, width, 50)
    got = swap_x(add_up(queue, gx[2], got_across, BF))
    sums1 = norm_sums(queue, gx, (tok, tok_c, tok_x, tok_xc))
    grad_d = add_up(queue, *d, F32).reshape(rows, -1)
    small = jnp.concatenate([sums1, sums2, gains])
    small_got = swap_core(small)
    grad_u = add_up(queue, *u, F32).reshape(rows, -1)
    z = next_step(*fold_joint(queue, a_keep, a_got, *z, bits[rest[0]]), rest[0])
    small = add_up(queue, small, small_got, F32)
    small_got = swap_x(small)
    grad_tokens = tokens_back(queue, gx[0], got_own, got, tok, gain1, grad_mid)
    small = add_up(queue, small, small_got, F32)
    small_got = swap_dp(small, near)
    for level in rest[1:]:
        z = next_step(*fold_dp(queue, *z, bits[level]), level)
    for level in rest:
        small = add_up(queue, small, small_got, F32)
        small_got = swap_dp(small, level)
    grad_out, grad_qkv = last_sum(queue, *z, local)
    small = add_up(queue, small, small_got, F32)
    result = (middle + mlp_own + swap_core(mlp_send).astype(F32)).astype(BF)
    return (
        result[None],
        grad_tokens[None],
        small[0],
        small[1],
        grad_qkv,
        small[4, :HD],
        small[5, :HD],
        grad_out,
        small[2],
        small[3],
        grad_u,
        grad_d.T,
    )


def solution(mesh):
    rows = P("dp", "tensor", None)
    wide = P("dp", "tensor")
    tall = P("tensor", "dp")
    qkv = P("dp", None, "tensor")
    in_specs = (rows, P("dp", None), P(), P(), qkv, P(), P(), tall, P(), P(), wide, tall, rows)
    out_specs = (rows, rows, P(), P(), qkv, P(), P(), tall, P(), P(), wide, tall)
    return jax.shard_map(per_device, mesh=mesh, in_specs=in_specs, out_specs=out_specs, check_vma=False)
```

```python
import jax
import jax.numpy as jnp
from jax import lax
from jax.experimental import pallas as pl
from jax.experimental.pallas import tpu as pltpu
from jax.sharding import PartitionSpec as P

HD = 64
EPSILON = 1e-6
LOG2E = 1.4426950408889634
QSCALE = LOG2E / 8.0
BIG = 256.0
F32 = jnp.float32
BF = jnp.bfloat16
BQ = 512
BK_FWD = 512
BK_BWD = 256
CHUNK = 512


def nn(a, b):
    return lax.dot_general(a, b, (((1,), (0,)), ((), ())), preferred_element_type=F32)


def nt(a, b):
    return lax.dot_general(a, b, (((1,), (1,)), ((), ())), preferred_element_type=F32)


class Queue:
    def __init__(self):
        self.last = ()

    def __call__(self, name, kern, inputs, outs, scalars=(), scratch=(), vmem=12, us=0, fetched=()):
        count = len(scalars) + len(inputs)
        deps = self.last
        skip = count + len(fetched) + len(deps)

        def body(*refs):
            if not fetched:
                return kern(*refs[:count], *refs[skip:])
            copies = refs[-1 - len(fetched) : -1]
            moves = [pltpu.make_async_copy(a, b, refs[-1].at[i]) for i, (a, b) in enumerate(zip(refs[count:skip], copies))]
            for move in moves:
                move.start()
            for move in moves:
                move.wait()
            kern(*refs[:count], *refs[skip:-1])

        space = lambda where: pl.BlockSpec(memory_space=where)
        landing = [pltpu.VMEM(a.shape, a.dtype) for a in fetched]
        if fetched:
            landing.append(pltpu.SemaphoreType.DMA((len(fetched),)))
        res = pl.pallas_call(
            body,
            out_shape=tuple(jax.ShapeDtypeStruct(s, t) for s, t in outs),
            in_specs=[space(pltpu.SMEM)] * len(scalars) + [space(pltpu.VMEM)] * len(inputs) + [space(pl.ANY)] * (len(fetched) + len(deps)),
            out_specs=tuple(space(pltpu.VMEM) for _ in outs),
            scratch_shapes=[*scratch, *landing],
            compiler_params=pltpu.CompilerParams(vmem_limit_bytes=vmem * 2**20),
            cost_estimate=pl.CostEstimate(flops=int(us * 50e8 / 50), bytes_accessed=0, transcendentals=0),
            name=name,
        )(*scalars, *inputs, *fetched, *deps)
        self.last = (res[0],)
        return res


def hat_of(values):
    center = values - jnp.mean(values, axis=-1, keepdims=True)
    inv = lax.rsqrt(jnp.mean(center * center, axis=-1, keepdims=True) + EPSILON)
    return center * inv, inv


def hat_back(grad, gain, hat, inv):
    u = grad * gain
    return inv * (u - jnp.mean(u, axis=-1, keepdims=True) - hat * jnp.mean(u * hat, axis=-1, keepdims=True))


STEP = 128


def each(rows, body):
    pl.loop(0, rows // STEP)(lambda i: body(pl.ds(pl.multiple_of(i * STEP, STEP), STEP)))


def norm_pair(queue, one, two, gain, bias, us=0):
    slots, width = one.shape

    def kern(one_ref, two_ref, gain_ref, bias_ref, out_ref):
        for i, ref in enumerate((one_ref, two_ref)):

            def body(s, i=i, ref=ref):
                hat, _ = hat_of(ref[s, :].astype(F32))
                at = pl.ds(pl.multiple_of(s.start + i * slots, STEP), STEP)
                out_ref[at, :] = (hat * gain_ref[...] + bias_ref[...]).astype(BF)

            each(slots, body)

    return queue("norm_pair", kern, (one, two, gain, bias), [((2 * slots, width), BF)], us=us)[0]


def norm_rows(x):
    c = x - jnp.mean(x, axis=0, keepdims=True)
    inv = lax.rsqrt(jnp.mean(c * c, axis=0, keepdims=True) + EPSILON)
    return c * inv, inv


def split3(v):
    hi = v.astype(BF).astype(F32)
    rest = v - hi
    mid = rest.astype(BF).astype(F32)
    return hi, mid, rest - mid


def attn_fwd(queue, tensor, ids, own, oth, w, lo, fq, fk, qg, kg):
    half, width = own.shape
    slots = 2 * half
    cols = (w.shape[1] - lo) // 3
    heads = cols // HD
    nk = slots // BK_FWD

    def kern(t_ref, ids_ref, own_ref, oth_ref, w_ref, fq_ref, fk_ref, qg_ref, kg_ref, att_ref, lse_ref, q_ref, k_ref, v_ref, wt_ref, qi_ref, ki_ref, kt, qn, vn, n_ref, l_ref):
        list_blocks(t_ref, ids_ref, slots, BK_FWD, n_ref, l_ref)
        q_gain, k_gain = column(qg_ref[...]), column(kg_ref[...])
        ones = jnp.where(lax.broadcasted_iota(jnp.int32, (HD, CHUNK), 0) == 0, 1.0, 0.0).astype(F32)
        wt_ref[...] = w_ref[:, lo:].T
        for c in range(slots // CHUNK):
            s = slice(c * CHUNK, (c + 1) * CHUNK)
            mine = c * CHUNK < half
            x = own_ref[s, :] if mine else oth_ref[c * CHUNK - half : (c + 1) * CHUNK - half, :]
            raw = nt(wt_ref[: 2 * cols], x)
            v_ref[:, s] = raw[cols:].astype(BF)
            for h in range(heads):
                r = slice(h * HD, (h + 1) * HD)
                kn, ki_ref[h : h + 1, s] = norm_rows(raw[r])
                kn = (kn * k_gain).astype(BF)
                k_ref[r, s] = kn
                kt[h, :HD, s] = kn
                kt[h, HD:, s] = fk_ref[:, s]
                vn[h, s, :] = jnp.concatenate([raw[cols + h * HD : cols + (h + 1) * HD], ones], axis=0).T.astype(BF)
            if mine:
                raw = nt(wt_ref[2 * cols :], x)
                for h in range(heads):
                    r = slice(h * HD, (h + 1) * HD)
                    qh, qi_ref[h : h + 1, s] = norm_rows(raw[r])
                    qh = qh * (q_gain * QSCALE)
                    q_ref[r, s] = qh.astype(BF)
                    qa = jnp.concatenate([qh, fq_ref[:, s].astype(F32)], axis=0)
                    qn[h, s, :] = qa.T.astype(BF)
        for qb in range(half // BQ):
            s = slice(qb * BQ, (qb + 1) * BQ)

            def body(i, accs, qb=qb, s=s):
                ks = pl.ds(pl.multiple_of(l_ref[qb * nk + i] * BK_FWD, BK_FWD), BK_FWD)
                out = []
                for h in range(heads):
                    p = jnp.exp2(nn(qn[h, s, :], kt[h, :, ks])).astype(BF)
                    out.append(accs[h] + nn(p, vn[h, ks, :]))
                return tuple(out)

            accs = lax.fori_loop(0, n_ref[qb], body, tuple(jnp.zeros((BQ, 2 * HD), F32) for _ in range(heads)))
            for h in range(heads):
                t = accs[h].T
                total = t[HD : HD + 1]
                att_ref[h * HD : (h + 1) * HD, s] = (t[:HD] / total).astype(BF)
                lse_ref[h : h + 1, s] = jnp.log2(total)

    return queue(
        "attn_fwd",
        kern,
        (own, oth, w, fq, fk, qg, kg),
        [
            ((cols, half), BF),
            ((heads, half), F32),
            ((cols, half), BF),
            ((cols, slots), BF),
            ((cols, slots), BF),
            ((3 * cols, width), BF),
            ((heads, half), F32),
            ((heads, slots), F32),
        ],
        scalars=(tensor, ids),
        scratch=[pltpu.VMEM((heads, 2 * HD, slots), BF), pltpu.VMEM((heads, half, 2 * HD), BF), pltpu.VMEM((heads, slots, 2 * HD), BF), pltpu.SMEM((half // BQ,), jnp.int32), pltpu.SMEM((half // BQ * nk + 1,), jnp.int32)],
        vmem=20,
        us=50,
    )


def attn_bwd(queue, tensor, ids, q, k, v, qi, ki, att, lse, branch, wot, lo, fq, fk, qg, kg, us):
    cols, half = q.shape
    slots = k.shape[1]
    heads = cols // HD
    nk = slots // BK_BWD

    def kern(t_ref, ids_ref, q_ref, k_ref, v_ref, qi_ref, ki_ref, att_ref, lse_ref, b0_ref, b1_ref, wot_ref, fq_ref, fk_ref, qg_ref, kg_ref, g_ref, gq_ref, gains_ref, kn, vn, qt, qn, dt, dn, dqt, dk, dv, n_ref, l_ref):
        list_blocks(t_ref, ids_ref, slots, BK_BWD, n_ref, l_ref)
        q_gain, k_gain = column(qg_ref[...]), column(kg_ref[...])
        row = lax.broadcasted_iota(jnp.int32, (HD, CHUNK), 0)
        three = jnp.where(row < 3, 1.0, 0.0).astype(F32)
        for c in range(slots // CHUNK):
            s = slice(c * CHUNK, (c + 1) * CHUNK)
            for h in range(heads):
                r = slice(h * HD, (h + 1) * HD)
                full = jnp.concatenate([k_ref[r, s], fk_ref[:, s]], axis=0).astype(F32)
                kn[h, s, :] = full.T.astype(BF)
                vn[h, s, :] = jnp.concatenate([v_ref[r, s].astype(F32), three], axis=0).T.astype(BF)
                dk[h, s, :] = jnp.zeros((CHUNK, 2 * HD), F32)
                dv[h, s, :] = jnp.zeros((CHUNK, 2 * HD), F32)
        for c in range(half // CHUNK):
            s = slice(c * CHUNK, (c + 1) * CHUNK)
            grad = nt(wot_ref[lo : lo + cols], (b0_ref if c == 0 else b1_ref)[...]).astype(BF).astype(F32)
            for h in range(heads):
                r = slice(h * HD, (h + 1) * HD)
                a, b, d = split3(-lse_ref[h : h + 1, s])
                f = fq_ref[:, s].astype(F32)
                f = jnp.where(row == 33, a, jnp.where(row == 34, b, jnp.where(row == 35, d, f)))
                full = jnp.concatenate([q_ref[r, s].astype(F32), f], axis=0)
                qt[h, :, s] = full.astype(BF)
                qn[h, s, :] = full.T.astype(BF)
                a, b, d = split3(-jnp.sum(grad[r] * att_ref[r, s].astype(F32), axis=0, keepdims=True))
                f = jnp.where(row == 0, a, jnp.where(row == 1, b, jnp.where(row == 2, d, 0.0)))
                full = jnp.concatenate([grad[r], f], axis=0)
                dt[h, :, s] = full.astype(BF)
                dn[h, s, :] = full.T.astype(BF)
        for qb in range(half // BQ):
            s = slice(qb * BQ, (qb + 1) * BQ)

            def body(i, accs, qb=qb, s=s):
                ks = pl.ds(pl.multiple_of(l_ref[qb * nk + i] * BK_BWD, BK_BWD), BK_BWD)
                out = []
                for h in range(heads):
                    p = jnp.exp2(nn(kn[h, ks, :], qt[h, :, s]))
                    ds = (p * nn(vn[h, ks, :], dt[h, :, s])).astype(BF)
                    dv[h, ks, :] += nn(p.astype(BF), dn[h, s, :])
                    dk[h, ks, :] += nn(ds, qn[h, s, :])
                    out.append(accs[h] + nn(k_ref[h * HD : (h + 1) * HD, ks], ds))
                return tuple(out)

            accs = lax.fori_loop(0, n_ref[qb], body, tuple(jnp.zeros((HD, BQ), F32) for _ in range(heads)))
            for h in range(heads):
                dqt[h, :, s] = accs[h]

        def back(grad, gain, hat, inv):
            u = grad * gain
            out = inv * (u - jnp.mean(u, axis=0, keepdims=True) - hat * jnp.mean(u * hat, axis=0, keepdims=True))
            return out.astype(BF), jnp.sum(grad * hat, axis=1, keepdims=True)

        sum_q = jnp.zeros((HD, 1), F32)
        sum_k = jnp.zeros((HD, 1), F32)
        for h in range(heads):
            r = slice(h * HD, (h + 1) * HD)
            for c in range(slots // CHUNK):
                s = slice(c * CHUNK, (c + 1) * CHUNK)
                g_ref[r, s], more = back(dk[h, s, :].T[:HD] * (1.0 / LOG2E), k_gain, k_ref[r, s].astype(F32) * (1.0 / k_gain), ki_ref[h : h + 1, s])
                sum_k += more
                g_ref[cols + h * HD : cols + (h + 1) * HD, s] = dv[h, s, :].T[:HD].astype(BF)
            for c in range(half // CHUNK):
                s = slice(c * CHUNK, (c + 1) * CHUNK)
                gq_ref[r, s], more = back(dqt[h, :, s] * 0.125, q_gain, q_ref[r, s].astype(F32) * (1.0 / (q_gain * QSCALE)), qi_ref[h : h + 1, s])
                sum_q += more
        gains_ref[:, :1] = sum_q
        gains_ref[:, 1:] = sum_k

    big = (heads, slots, 2 * HD)
    small = (heads, half, 2 * HD)
    flat = (heads, 2 * HD, half)
    return queue(
        "attn_bwd",
        kern,
        (q, k, v, qi, ki, att, lse, *branch, wot, fq, fk, qg, kg),
        [((2 * cols, slots), BF), ((cols, half), BF), ((HD, 2), F32)],
        scalars=(tensor, ids),
        scratch=[
            pltpu.VMEM(big, BF),
            pltpu.VMEM(big, BF),
            pltpu.VMEM(flat, BF),
            pltpu.VMEM(small, BF),
            pltpu.VMEM(flat, BF),
            pltpu.VMEM(small, BF),
            pltpu.VMEM((heads, HD, half), F32),
            pltpu.VMEM(big, F32),
            pltpu.VMEM(big, F32),
            pltpu.SMEM((half // BQ,), jnp.int32),
            pltpu.SMEM((half // BQ * nk + 1,), jnp.int32),
        ],
        vmem=28,
        us=us,
    )


def features(queue, ids, tensor):
    parts, slots = ids.shape

    def kern(t_ref, ids_ref, fq_ref, fk_ref):
        row = lax.broadcasted_iota(jnp.int32, (HD, slots), 0)
        for i in range(parts):
            s = slice(i * slots, (i + 1) * slots)
            hot = ids_ref[pl.ds(t_ref[0] ^ i, 1), :] + 1 == row
            ones = (row >= 32) & (row < 36)
            fk_ref[:, s] = jnp.where((hot & (row < 32)) | ones, 1.0, 0.0).astype(BF)
            if i < 2:
                fq_ref[:, s] = jnp.where(hot & (row < 32), BIG, jnp.where(row == 32, -BIG, 0.0)).astype(BF)

    outs = [((HD, 2 * slots), BF), ((HD, parts * slots), BF)]
    return queue("features", kern, (ids,), outs, scalars=(tensor,), us=50)


def list_blocks(t_ref, ids_ref, slots, size, n_ref, l_ref):
    share = ids_ref.shape[0] // 4

    def ends(block, length):
        at = block * length
        at = (t_ref[0] ^ (at // share)) * share + at % share
        first, last = ids_ref[at], ids_ref[at + length - 1]
        return jnp.where(first < 0, 99, first), jnp.where(last < 0, 99, last)

    nk = slots // size
    keys = [ends(kb, size) for kb in range(nk)]
    for qb in range(slots // 2 // BQ):
        first, last = ends(qb, BQ)
        n = jnp.int32(0)
        for kb, (low, high) in enumerate(keys):
            l_ref[qb * nk + n] = kb
            n += ((first <= high) & (low <= last)).astype(jnp.int32)
        n_ref[qb] = n


def column(row):
    n = row.shape[1]
    same = lax.broadcasted_iota(jnp.int32, (n, n), 0) == lax.broadcasted_iota(jnp.int32, (n, n), 1)
    return jnp.sum(jnp.where(same, row, 0.0), axis=1, keepdims=True)


def gelu_pair(v):
    t = 1.0 / (1.0 + (0.3275911 * 0.5**0.5) * jnp.abs(v))
    e = jnp.exp2(v * v * (-0.5 * LOG2E))
    poly = ((((0.5307027145 * t - 0.7265760135) * t + 0.7107068705) * t - 0.142248368) * t + 0.127414796) * t
    tail = poly * e
    phi = jnp.where(v < 0, tail, 1.0 - tail)
    return v * phi, phi + v * e * 0.3989422804014327


def split_store(value, bit, keep, send, blocks, lead=(), at=slice(None)):
    rows = value.shape[0] // blocks
    value = value.astype(BF)
    for b in range(2):

        @pl.when(bit == b)
        def _(b=b):
            for j in range(blocks):
                part = value[j * rows : (j + 1) * rows]
                if j % 2 == b:
                    keep[(*lead, j // 2, slice(None), at)] = part
                else:
                    send[(*lead, j // 2, slice(None), at)] = part


COLS = 256
PLACES = ((0, 0, 0, 256), (256, 1, 0, 256), (512, 0, 256, 128), (640, 1, 256, 128))
HALF_COLS = 384


def mlp(queue, xs, gs, both, bit, blocks, slope=None):
    half, width = xs[0].shape
    cols = both.shape[2] // 2
    forward = slope is None
    rows = 256

    def kern(bit_ref, x0, x1, g0, g1, w_ref, *rest):
        rest = list(rest)
        if forward:
            hid = rest.pop(0)
        slope_ref = rest.pop(0)
        if forward:
            keep_a, send_a, keep_b, send_b, turned = rest
        else:
            keep_a, send_a, keep_b, send_b, own_ref, out_ref, hid, turned = rest
        left = (g0, g1) if forward else (x0, x1)
        feed = (x0, x1) if forward else (g0, g1)
        w_in, w_out = (0, cols) if forward else (cols, 0)
        for i, ref in enumerate(left):
            turned[:, i * half : (i + 1) * half] = ref[...].T

        def units(r, i, c, lo):
            o = slice(lo + i * half, lo + i * half + rows)
            at = slice(c, c + COLS) if isinstance(c, int) else pl.ds(pl.multiple_of(c, COLS), COLS)
            w_at = slice(w_in + c, w_in + c + COLS) if isinstance(c, int) else pl.ds(pl.multiple_of(w_in + c, COLS), COLS)
            value = nn(feed[i][lo : lo + rows, :], w_ref[r, :, w_at])
            if forward:
                value, grad = gelu_pair(value)
                slope_ref[r, o, at] = grad.astype(BF)
            else:
                value = value * slope_ref[r, o, at].astype(F32)
            hid[r, o, at] = value.astype(BF)

        def weights(r, c):
            value = nn(turned[...], hid[r, :, c : c + COLS])
            for first, part, to, count in PLACES:
                if c <= first < c + COLS:
                    piece = value[:, first - c : first - c + count]
                    if part == 0:
                        split_store(piece, bit_ref[0], keep_a, send_a, blocks, (r,), slice(to, to + count))
                    else:
                        (send_b if r else keep_b)[:, to : to + count] = piece.astype(BF)

        spots = [(i, lo) for i in range(2) for lo in range(0, half, rows)]

        if forward:

            @pl.loop(0, cols // COLS)
            def _(k):
                for i, lo in spots:
                    units(0, i, k * COLS, lo)

        else:
            for c in range(0, cols, COLS):
                for i, lo in spots:
                    units(0, i, c, lo)

        for c in range(0, cols, COLS):
            for i, lo in spots:
                units(1, i, c, lo)
            weights(0, c)
        for c in range(0, cols, COLS):
            weights(1, c)
        if not forward:
            shares(hid, w_ref, slice(w_out, w_out + cols), own_ref, out_ref)

    part_a = ((2, blocks // 2, width // blocks, HALF_COLS), BF)
    part_b = ((width, cols - HALF_COLS), BF)
    outs = [part_a, part_a, part_b, part_b]
    inputs = [*xs, *gs, both]
    flat = (2, 2 * half, cols)
    scratch = [pltpu.VMEM((width, 2 * half), BF)]
    if forward:
        outs = [(flat, BF), (flat, BF), *outs]
    else:
        inputs.append(slope)
        outs += [((half, width), F32), ((half, width), BF)]
        scratch.insert(0, pltpu.VMEM(flat, BF))
    return queue("mlp_fwd" if forward else "mlp_bwd", kern, inputs, outs, scalars=(bit,), scratch=scratch, vmem=28, us=0)


def shares(hid, w_ref, at, own_ref, out_ref):
    half = own_ref.shape[0]
    rows = 256
    for i, out in enumerate((own_ref, out_ref)):
        for lo in range(0, half, rows):
            o = slice(lo + i * half, lo + i * half + rows)
            out[lo : lo + rows, :] = (nt(hid[0, o, :], w_ref[0, :, at]) + nt(hid[1, o, :], w_ref[1, :, at])).astype(out.dtype)


def mlp_out(queue, hid, both, us):
    _, slots, cols = hid.shape
    width = both.shape[1]

    def kern(hid_ref, w_ref, own_ref, out_ref):
        shares(hid_ref, w_ref, slice(cols, 2 * cols), own_ref, out_ref)

    outs = [((slots // 2, width), F32), ((slots // 2, width), BF)]
    return queue("mlp_out", kern, (hid, both), outs, us=us)


def out_proj(queue, atts, w, lo):
    cols, slots = atts[0].shape
    width = w.shape[0]
    half = slots // 2

    def kern(a0, a1, w_ref, own_ref, send_ref, wot_ref):
        wot_ref[...] = w_ref[:, :lo].T
        for i, out in enumerate((own_ref, send_ref)):
            s = slice(i * half, (i + 1) * half)
            both = jnp.concatenate([a0[:, s], a1[:, s]], axis=0)
            out[...] = nn(both.T, wot_ref[...]).astype(out.dtype)

    outs = [((half, width), F32), ((half, width), BF), ((lo, width), BF)]
    return queue("out_proj", kern, (*atts, w), outs)


def middle_norm(queue, own, got, tok, gain, bias):
    slots, width = own.shape

    def kern(own_ref, got_ref, tok_ref, gain_ref, bias_ref, mid_ref, out_ref):
        def body(s):
            mid = tok_ref[s, :].astype(F32) + own_ref[s, :] + got_ref[s, :].astype(F32)
            mid_ref[s, :] = mid
            hat, _ = hat_of(mid)
            out_ref[s, :] = (hat * gain_ref[...] + bias_ref[...]).astype(BF)

        each(slots, body)

    outs = [((slots, width), F32), ((slots, width), BF)]
    return queue("middle_norm", kern, (own, got, tok, gain, bias), outs, us=50)


def middle_back(queue, own, got, mid, cot, gain, branch_own, branch_got):
    slots, width = own.shape

    def kern(own_ref, got_ref, mid_ref, cot_ref, gain_ref, bo_ref, bg_ref, grad_ref, out_ref, sums_ref, result_ref):
        sums_ref[...] = jnp.zeros_like(sums_ref)

        def body(s):
            grad = own_ref[s, :] + got_ref[s, :].astype(F32)
            mid = mid_ref[s, :]
            result_ref[s, :] = (mid + bo_ref[s, :] + bg_ref[s, :].astype(F32)).astype(BF)
            hat, inv = hat_of(mid)
            sums_ref[0:1] += jnp.sum(grad * hat, axis=0, keepdims=True)
            sums_ref[1:2] += jnp.sum(grad, axis=0, keepdims=True)
            grad = cot_ref[s, :].astype(F32) + hat_back(grad, gain_ref[...], hat, inv)
            grad_ref[s, :] = grad
            out_ref[s, :] = grad.astype(BF)

        each(slots, body)

    outs = [((slots, width), F32), ((slots, width), BF), ((2, width), F32), ((slots, width), BF)]
    return queue("middle_back", kern, (own, got, mid, cot, gain, branch_own, branch_got), outs, us=50)


def proj_grad(queue, g, gq, own, oth, wt, bit, blocks, prev=(), atts=(), branch=()):
    two, slots = g.shape
    cols, half = gq.shape
    width = own.shape[1]
    block = half // 2
    lead = cols * len(atts)

    def kern(bit_ref, g_ref, gq_ref, own_ref, oth_ref, wt_ref, *rest):
        rest = list(rest)
        prev_refs = [rest.pop(0) for _ in prev]
        att_refs = [rest.pop(0) for _ in atts]
        branch_refs = [rest.pop(0) for _ in branch]
        keep_ref, send_ref = rest[:2]
        outs = rest[2:]
        for i in reversed(range(4)):
            s = slice(i * block, (i + 1) * block)
            value = nn(g_ref[:, s].T, wt_ref[:two])
            if i < 2:
                value += nn(gq_ref[:, s].T, wt_ref[two:])
            if prev_refs:
                value += prev_refs[i % 2][i // 2].astype(F32)
            outs[i % 2][i // 2] = value.astype(BF)
        parts = []
        for att in att_refs:
            parts.append(nn(att[:, :block], branch_refs[0][...]) + nn(att[:, block:], branch_refs[1][...]))
        parts.append(nn(g_ref[:, :half], own_ref[...]) + nn(g_ref[:, half:], oth_ref[...]))
        parts.append(nn(gq_ref[...], own_ref[...]))
        split_store(jnp.concatenate(parts, axis=0).T, bit_ref[0], keep_ref, send_ref, blocks)

    share = ((blocks // 2, width // blocks, lead + two + cols), BF)
    return queue(
        "proj_grad",
        kern,
        (g, gq, own, oth, wt, *prev, *atts, *branch),
        [share, share] + [((2, block, width), BF)] * 2,
        scalars=(bit,),
        vmem=22,
        us=50,
    )


def norm_sums(queue, grads, toks):
    slots, width = toks[0].shape

    def kern(*refs):
        sums_ref = refs[2]
        sums_ref[...] = jnp.zeros_like(sums_ref)

        def body(s):
            first = jnp.zeros((1, width), F32)
            second = jnp.zeros((1, width), F32)
            for i, tok_ref in enumerate(refs[3:]):
                grad = refs[i % 2][i // 2, s, :].astype(F32)
                hat, _ = hat_of(tok_ref[s, :].astype(F32))
                first += jnp.sum(grad * hat, axis=0, keepdims=True)
                second += jnp.sum(grad, axis=0, keepdims=True)
            sums_ref[0:1] += first
            sums_ref[1:2] += second

        each(slots, body)

    return queue("norm_sums", kern, grads, [((2, width), F32)], vmem=14, fetched=toks)[0]


def tokens_back(queue, own, got_x, tok, gain, mid):
    slots, width = tok.shape

    def kern(own_ref, x_ref, tok_ref, gain_ref, mid_ref, out_ref):
        def body(s):
            hat, inv = hat_of(tok_ref[s, :].astype(F32))
            grad = own_ref[s, :] + x_ref[s, :].astype(F32)
            out_ref[s, :] = (mid_ref[s, :] + hat_back(grad, gain_ref[...], hat, inv)).astype(BF)

        each(slots, body)

    return queue("tokens_back", kern, (own, got_x, tok, gain, mid), [((slots, width), BF)])[0]


def last_sum(queue, kept, got, lead, across):
    _, rows, _ = kept.shape
    cols = lead.shape[1]

    def kern(kept_ref, got_ref, lead_ref, across_ref, out_ref, qkv_ref):
        out_ref[...] = (lead_ref[...] + across_ref[:, :cols].astype(F32)).T
        value = kept_ref[0] + got_ref[0].astype(F32) + across_ref[:, cols:].astype(F32)
        for i in range(3):
            lo = cols * (2, 0, 1)[i]
            qkv_ref[:, i, :] = value[:, lo : lo + cols]

    return queue("last_sum", kern, (kept, got, lead, across), [((cols, rows), F32), ((rows, 3, cols), F32)])


def slot_sums(queue, kept, got):
    _, slots, width = kept.shape

    def kern(kept_ref, got_ref, across, own):
        across[...] = (kept_ref[1].astype(F32) + got_ref[1].astype(F32)).astype(BF)
        own[...] = kept_ref[0].astype(F32) + got_ref[0].astype(F32)

    return queue("slot_sums", kern, (kept, got), [((slots, width), BF), ((slots, width), F32)])


def gain_rows(queue, one, two, width, us):
    def kern(a, b, out):
        value = (a[...] + b[...]).T
        out[...] = jnp.concatenate([value, jnp.zeros((2, width - HD), F32)], axis=1)

    return queue("gain_rows", kern, (one, two), [((2, width), F32)], us=us)[0]


def add_up(queue, one, two, dtype, us=0):
    def kern(a, b, out):
        out[...] = (a[...].astype(F32) + b[...].astype(F32)).astype(dtype)

    return queue("add_up", kern, (one, two), [(one.shape, dtype)], us=us)[0]


def side_by_side(queue, *arrays, us=0):
    edges = [0]
    for a in arrays:
        edges.append(edges[-1] + a.shape[1])

    def kern(*refs):
        for ref, lo, hi in zip(refs, edges, edges[1:]):
            refs[-1][:, lo:hi] = ref[...]

    return queue("side_by_side", kern, arrays, [((arrays[0].shape[0], edges[-1]), BF)], us=us)[0]


def pair_dp(queue, held, got, bit, cuts=None):
    m, rows, cols = held.shape
    cuts = [0, rows] if cuts is None else [0, *cuts, rows]

    def kern(bit_ref, held_ref, got_ref, *outs):
        bit = bit_ref[0]
        for i in range(m):
            for lo, hi, out in zip(cuts, cuts[1:], outs):
                out[2 * i + bit] = held_ref[i, lo:hi]
                out[2 * i + 1 - bit] = got_ref[i, lo:hi]

    outs = [((2 * m, hi - lo, cols), held.dtype) for lo, hi in zip(cuts, cuts[1:])]
    return queue("pair_dp", kern, (held, got), outs, scalars=(bit,))


def pair_both(queue, part_a, got_a, part_b, got_b, bit):
    m, rows_a, cols = part_a.shape
    rows_b = part_b.shape[1]

    def kern(bit_ref, a, ga, b, gb, out_a, out_b):
        bit = bit_ref[0]
        out_a[0] = a[...]
        out_a[1] = ga[...]
        for i in range(m):
            out_b[i, bit] = b[i]
            out_b[i, 1 - bit] = gb[i]

    outs = [((2, m, rows_a, cols), BF), ((m, 2, rows_b, cols), BF)]
    return queue("pair_both", kern, (part_a, got_a, part_b, got_b), outs, scalars=(bit,))


def pair_last(queue, part_a, got_a, part_b, got_b, bit):
    _, m, rows_a, cols = part_a.shape
    rows_b = part_b.shape[2]

    def kern(bit_ref, a, ga, b, gb, out):
        bit = bit_ref[0]
        for i in range(m):
            for t in range(2):
                out[t, i, bit, :rows_a] = a[t, i]
                out[t, i, 1 - bit, :rows_a] = ga[t, i]
            for y in range(2):
                out[0, i, y, rows_a:] = b[i, y]
                out[1, i, y, rows_a:] = gb[i, y]

    outs = [((2, m, 2, rows_a + rows_b, cols), BF)]
    (res,) = queue("pair_last", kern, (part_a, got_a, part_b, got_b), outs, scalars=(bit,))
    return res.reshape(2, 2 * m * (rows_a + rows_b), cols)


def fold_dp(queue, kept, got, bit):
    n, rows, cols = kept.shape

    def kern(bit_ref, kept_ref, got_ref, keep, send):
        bit = bit_ref[0]
        for i in range(n // 2):
            keep[i] = kept_ref[2 * i + bit].astype(F32) + got_ref[2 * i + bit].astype(F32)
            send[i] = (kept_ref[2 * i + 1 - bit].astype(F32) + got_ref[2 * i + 1 - bit].astype(F32)).astype(BF)

    outs = [((n // 2, rows, cols), F32), ((n // 2, rows, cols), BF)]
    return queue("fold_dp", kern, (kept, got), outs, scalars=(bit,))


def fold_both(queue, keep_a, got_a, keep_b, got_b, bit, us=0):
    _, n, rows, cols_a = keep_a.shape
    cols_b = keep_b.shape[-1]

    def kern(bit_ref, ka, ga, kb, gb, keep_a, send_a, keep_b, send_b):
        bit = bit_ref[0]
        keep_a[...] = ka[0].astype(F32) + ga[0].astype(F32)
        send_a[...] = (ka[1].astype(F32) + ga[1].astype(F32)).astype(BF)
        for i in range(n):
            keep_b[i] = kb[2 * i + bit].astype(F32) + gb[2 * i + bit].astype(F32)
            send_b[i] = (kb[2 * i + 1 - bit].astype(F32) + gb[2 * i + 1 - bit].astype(F32)).astype(BF)

    outs = [((n, rows, cols_a), F32), ((n, rows, cols_a), BF), ((n, rows, cols_b), F32), ((n, rows, cols_b), BF)]
    return queue("fold_both", kern, (keep_a, got_a, keep_b, got_b), outs, scalars=(bit,), us=us)


def fold_joined(queue, keep_a, got_a, keep_b, got_b, bit):
    n, rows, cols_a = keep_a.shape
    cols = cols_a + keep_b.shape[-1]

    def kern(bit_ref, ka, ga, kb, gb, keep, send):
        bit = bit_ref[0]
        for i in range(n // 2):
            for first, part, at, count in PLACES:
                k, g = ((ka, ga), (kb, gb))[part]
                to, at = slice(first, first + count), slice(at, at + count)
                keep[i, :, to] = k[2 * i + bit, :, at] + g[2 * i + bit, :, at].astype(F32)
                send[i, :, to] = (k[2 * i + 1 - bit, :, at] + g[2 * i + 1 - bit, :, at].astype(F32)).astype(BF)

    outs = [((n // 2, rows, cols), F32), ((n // 2, rows, cols), BF)]
    return queue("fold_joined", kern, (keep_a, got_a, keep_b, got_b), outs, scalars=(bit,))


def sum_x(queue, kept, got, cols):
    _, rows, total = kept.shape

    def kern(kept_ref, got_ref, send, keep):
        value = kept_ref[0] + got_ref[0].astype(F32)
        keep[...] = value[:, :cols]
        send[...] = value[:, cols:].astype(BF)

    return queue("sum_x", kern, (kept, got), [((rows, total - cols), BF), ((rows, cols), F32)])


def swap(values, axis, mask):
    return lax.ppermute(values, axis, [(i, i ^ mask) for i in range(lax.axis_size(axis))])


def swap_core(values):
    return swap(values, "tensor", 1)


def swap_x(values):
    return swap(values, "tensor", 2)


def per_device(tokens, picture_ids, ln1_gain, ln1_bias, w_qkv, q_gain, k_gain, w_out, ln2_gain, ln2_bias, w_up, w_down, cotangent):
    slots, width = tokens.shape[1:]
    local = w_qkv.shape[2]
    n_dp = lax.axis_size("dp")
    rows = width // n_dp
    q_slots = 2 * slots
    tok = tokens[0]
    cot = cotangent[0]
    tensor = lax.axis_index("tensor").reshape(1)
    me = lax.axis_index("dp")
    levels = list(reversed(range(n_dp.bit_length() - 1)))
    far, near = levels[:-1], levels[-1]
    bits = {level: ((me >> level) & 1).reshape(1) for level in levels}
    queue = Queue()
    gain1, bias1, gain2, bias2 = (v.reshape(1, width) for v in (ln1_gain, ln1_bias, ln2_gain, ln2_bias))
    qg, kg = q_gain.reshape(1, HD), k_gain.reshape(1, HD)

    def swap_dp(values, level):
        return swap(values, "dp", 1 << level)

    out_t = w_out.T
    part_0 = jnp.concatenate([w_qkv[:, 1], w_qkv[:, 2], w_qkv[:, 0]], axis=1)
    part_0 = side_by_side(queue, part_0)
    got_0 = swap_dp(part_0[None], far[0])
    ids = picture_ids[0]
    fq, fk = features(queue, ids.reshape(4, slots), tensor)
    got_cols = swap_x(side_by_side(queue, out_t, part_0))
    tok_x = swap_x(side_by_side(queue, tok, us=50))
    tok_c = swap_core(tok)
    cot_c = swap_core(cot)
    both = side_by_side(queue, w_up, w_down.T)[None]
    half = rows // 2
    (part_0,) = pair_dp(queue, part_0[None], got_0, bits[far[0]])
    part_1 = side_by_side(queue, out_t, got_cols)[None]
    got_0 = swap_dp(part_0, levels[1])
    got_1 = swap_dp(part_1, far[0])
    for level, after_it in zip(levels[1:-1], levels[2:]):
        (part_0,) = pair_dp(queue, part_0, got_0, bits[level])
        got_0 = swap_dp(part_0, after_it)
    for level, after_it in zip(levels[:-2], levels[1:-1]):
        (part_1,) = pair_dp(queue, part_1, got_1, bits[level])
        got_1 = swap_dp(part_1, after_it)
    both = side_by_side(queue, both[0])[None]
    got_b = swap_dp(both, far[0])
    own = norm_pair(queue, tok, tok_c, gain1, bias1, us=50)
    (part_1,) = pair_dp(queue, part_1, got_1, bits[levels[-2]])
    got_1 = swap_dp(part_1, levels[-1])
    (w_0,) = pair_dp(queue, part_0, got_0, bits[near])
    w_0 = w_0.reshape(width, 3 * local)
    for level, after_it in zip(far[:-1], far[1:]):
        (both,) = pair_dp(queue, both, got_b, bits[level])
        got_b = swap_dp(both, after_it)
    tok_xc = swap_core(side_by_side(queue, tok_x))
    oth = norm_pair(queue, tok_x, tok_xc, gain1, bias1)
    att_0, lse_0, q_0, k_0, v_0, wt_0, qi_0, ki_0 = attn_fwd(queue, tensor, ids, own, oth, w_0, 0, fq, fk, qg, kg)
    part_a, part_b = pair_dp(queue, both, got_b, bits[far[-1]], (half,))
    got_a, got_b = swap_x(part_a), swap_dp(part_b, near)
    (w_1,) = pair_dp(queue, part_1, got_1, bits[near])
    w_1 = w_1.reshape(width, 5 * local)
    att_1, lse_1, q_1, k_1, v_1, wt_1, qi_1, ki_1 = attn_fwd(queue, tensor, ids, own, oth, w_1, 2 * local, fq, fk, qg, kg)
    part_a, part_b = pair_both(queue, part_a, got_a, part_b, got_b, bits[near])
    got_a, got_b = swap_dp(part_a, near), swap_x(part_b)
    branch_own, branch_send, wot = out_proj(queue, (att_0, att_1), w_1, 2 * local)
    middle, normed = middle_norm(queue, branch_own, swap_core(branch_send), tok, gain2, bias2)
    normed_c = swap_core(normed)
    both = pair_last(queue, part_a, got_a, part_b, got_b, bits[near])

    bit = bits[near]
    rest = levels[::-1][1:]
    xs, gs = (normed, normed_c), (cot, cot_c)
    grid = (n_dp, rows, w_up.shape[1] - HALF_COLS)

    def first_step(parts):
        keep_a, send_a, keep_b, send_b = parts
        return keep_a, swap_dp(send_a, near), keep_b.reshape(grid), swap_x(send_b).reshape(grid)

    def second_step(keep_a, send_a, keep_b, send_b):
        return keep_a, swap_x(send_a), keep_b, swap_dp(send_b, near)

    def next_step(keep, send, level):
        return keep, swap_dp(send, level)

    hid, slope, *parts = mlp(queue, xs, gs, both, bit, n_dp)
    d = first_step(parts)
    mlp_own, mlp_send = mlp_out(queue, hid, both, 50)
    *parts, gn_own, gn_send = mlp(queue, xs, gs, both, bit, n_dp, slope)
    d = second_step(*fold_both(queue, *d, bit, us=50))
    u = first_step(parts)
    grad_mid, branch, sums2, result = middle_back(
        queue, gn_own, swap_core(gn_send), middle, cot, gain2, mlp_own, swap_core(mlp_send)
    )
    branches = (branch, swap_core(branch))
    g, gq, gains_1 = attn_bwd(queue, tensor, ids, q_1, k_1, v_1, qi_1, ki_1, att_1, lse_1, branches, wot, local, fq, fk, qg, kg, 0)
    u = second_step(*fold_both(queue, *u, bit))
    d = next_step(*fold_joined(queue, *d, bits[rest[0]]), rest[0])
    a_keep, a_send, *gx = proj_grad(queue, g, gq, own, oth, wt_1, bit, n_dp, atts=(att_0, att_1), branch=branches)
    a = next_step(a_keep, a_send, near)
    u = next_step(*fold_joined(queue, *u, bits[rest[0]]), rest[0])
    d = next_step(*fold_dp(queue, *d, bits[rest[1]]), rest[1])
    g, gq, gains_0 = attn_bwd(queue, tensor, ids, q_0, k_0, v_0, qi_0, ki_0, att_0, lse_0, branches, wot, 0, fq, fk, qg, kg, 50)
    a = next_step(*fold_dp(queue, *a, bits[rest[0]]), rest[0])
    u = next_step(*fold_dp(queue, *u, bits[rest[1]]), rest[1])
    for level in rest[2:]:
        d = next_step(*fold_dp(queue, *d, bits[level]), level)
        u = next_step(*fold_dp(queue, *u, bits[level]), level)
    grad_d = add_up(queue, *d, F32).reshape(rows, -1)
    z_keep, z_send, *gx = proj_grad(queue, g, gq, own, oth, wt_0, bit, n_dp, prev=gx)
    z = next_step(z_keep, z_send, near)
    gx_got = swap_core(gx[1])
    gains = gain_rows(queue, gains_0, gains_1, width, 50)
    across, grad_normed = slot_sums(queue, gx[0], gx_got)
    got = swap_x(across)
    sums1 = norm_sums(queue, gx, (tok, tok_c, tok_x, tok_xc))
    small = jnp.concatenate([sums1, sums2, gains])
    small_got = swap_core(small)
    grad_u = add_up(queue, *u, F32).reshape(rows, -1)
    z = next_step(*fold_dp(queue, *z, bits[rest[0]]), rest[0])
    for level in rest[1:]:
        a = next_step(*fold_dp(queue, *a, bits[level]), level)
    small = add_up(queue, small, small_got, F32)
    small_got = swap_x(small)
    grad_tokens = tokens_back(queue, grad_normed, got, tok, gain1, grad_mid)
    small = add_up(queue, small, small_got, F32)
    small_got = swap_dp(small, near)
    for level in rest[1:]:
        z = next_step(*fold_dp(queue, *z, bits[level]), level)
    a_send, lead = sum_x(queue, *a, local)
    a_got = swap_x(a_send)
    for level in rest:
        small = add_up(queue, small, small_got, F32)
        small_got = swap_dp(small, level)
    grad_out, grad_qkv = last_sum(queue, *z, lead, a_got)
    small = add_up(queue, small, small_got, F32)
    return (
        result[None],
        grad_tokens[None],
        small[0],
        small[1],
        grad_qkv,
        small[4, :HD],
        small[5, :HD],
        grad_out,
        small[2],
        small[3],
        grad_u,
        grad_d.T,
    )


def solution(mesh):
    rows = P("dp", "tensor", None)
    wide = P("dp", "tensor")
    tall = P("tensor", "dp")
    qkv = P("dp", None, "tensor")
    in_specs = (rows, P("dp", None), P(), P(), qkv, P(), P(), tall, P(), P(), wide, tall, rows)
    out_specs = (rows, rows, P(), P(), qkv, P(), P(), tall, P(), P(), wide, tall)
    return jax.shard_map(per_device, mesh=mesh, in_specs=in_specs, out_specs=out_specs, check_vma=False)
```

```python
import jax
import jax.numpy as jnp
from jax import lax
from jax.experimental import pallas as pl
from jax.experimental.pallas import tpu as pltpu
from jax.sharding import PartitionSpec as P

HD = 64
EPSILON = 1e-6
LOG2E = 1.4426950408889634
QSCALE = LOG2E / 8.0
BIG = 256.0
F32 = jnp.float32
BF = jnp.bfloat16
BQ = 512
BK_FWD = 512
BK_BWD = 256
CHUNK = 512


def nn(a, b):
    return lax.dot_general(a, b, (((1,), (0,)), ((), ())), preferred_element_type=F32)


def nt(a, b):
    return lax.dot_general(a, b, (((1,), (1,)), ((), ())), preferred_element_type=F32)


class Queue:
    def __init__(self):
        self.last = ()

    def __call__(self, name, kern, inputs, outs, scalars=(), scratch=(), vmem=12, us=0, fetched=()):
        count = len(scalars) + len(inputs)
        deps = self.last
        skip = count + len(fetched) + len(deps)

        def body(*refs):
            if not fetched:
                return kern(*refs[:count], *refs[skip:])
            copies = refs[-1 - len(fetched) : -1]
            moves = [pltpu.make_async_copy(a, b, refs[-1].at[i]) for i, (a, b) in enumerate(zip(refs[count:skip], copies))]
            for move in moves:
                move.start()
            for move in moves:
                move.wait()
            kern(*refs[:count], *refs[skip:-1])

        space = lambda where: pl.BlockSpec(memory_space=where)
        landing = [pltpu.VMEM(a.shape, a.dtype) for a in fetched]
        if fetched:
            landing.append(pltpu.SemaphoreType.DMA((len(fetched),)))
        res = pl.pallas_call(
            body,
            out_shape=tuple(jax.ShapeDtypeStruct(s, t) for s, t in outs),
            in_specs=[space(pltpu.SMEM)] * len(scalars) + [space(pltpu.VMEM)] * len(inputs) + [space(pl.ANY)] * (len(fetched) + len(deps)),
            out_specs=tuple(space(pltpu.VMEM) for _ in outs),
            scratch_shapes=[*scratch, *landing],
            compiler_params=pltpu.CompilerParams(vmem_limit_bytes=vmem * 2**20),
            cost_estimate=pl.CostEstimate(flops=int(us * 50e8 / 50), bytes_accessed=0, transcendentals=0),
            name=name,
        )(*scalars, *inputs, *fetched, *deps)
        self.last = (res[0],)
        return res


def hat_of(values):
    center = values - jnp.mean(values, axis=-1, keepdims=True)
    inv = lax.rsqrt(jnp.mean(center * center, axis=-1, keepdims=True) + EPSILON)
    return center * inv, inv


def hat_back(grad, gain, hat, inv):
    u = grad * gain
    return inv * (u - jnp.mean(u, axis=-1, keepdims=True) - hat * jnp.mean(u * hat, axis=-1, keepdims=True))


STEP = 128


def each(rows, body):
    pl.loop(0, rows // STEP)(lambda i: body(pl.ds(pl.multiple_of(i * STEP, STEP), STEP)))


def norm_pair(queue, one, two, gain, bias, us=0):
    slots, width = one.shape

    def kern(one_ref, two_ref, gain_ref, bias_ref, out_ref):
        for i, ref in enumerate((one_ref, two_ref)):

            def body(s, i=i, ref=ref):
                hat, _ = hat_of(ref[s, :].astype(F32))
                at = pl.ds(pl.multiple_of(s.start + i * slots, STEP), STEP)
                out_ref[at, :] = (hat * gain_ref[...] + bias_ref[...]).astype(BF)

            each(slots, body)

    return queue("norm_pair", kern, (one, two, gain, bias), [((2 * slots, width), BF)], us=us)[0]


def norm_rows(x):
    c = x - jnp.mean(x, axis=0, keepdims=True)
    inv = lax.rsqrt(jnp.mean(c * c, axis=0, keepdims=True) + EPSILON)
    return c * inv, inv


def split3(v):
    hi = v.astype(BF).astype(F32)
    rest = v - hi
    mid = rest.astype(BF).astype(F32)
    return hi, mid, rest - mid


def attn_fwd(queue, tensor, ids, own, oth, w, lo, fq, fk, qg, kg):
    half, width = own.shape
    slots = 2 * half
    cols = (w.shape[1] - lo) // 3
    heads = cols // HD
    nk = slots // BK_FWD

    def kern(t_ref, ids_ref, own_ref, oth_ref, w_ref, fq_ref, fk_ref, qg_ref, kg_ref, att_ref, lse_ref, q_ref, k_ref, v_ref, wt_ref, qi_ref, ki_ref, kt, qn, vn, n_ref, l_ref):
        list_blocks(t_ref, ids_ref, slots, BK_FWD, n_ref, l_ref)
        q_gain, k_gain = column(qg_ref[...]), column(kg_ref[...])
        ones = jnp.where(lax.broadcasted_iota(jnp.int32, (HD, CHUNK), 0) == 0, 1.0, 0.0).astype(F32)
        wt_ref[...] = w_ref[:, lo:].T
        for c in range(slots // CHUNK):
            s = slice(c * CHUNK, (c + 1) * CHUNK)
            mine = c * CHUNK < half
            x = own_ref[s, :] if mine else oth_ref[c * CHUNK - half : (c + 1) * CHUNK - half, :]
            raw = nt(wt_ref[: 2 * cols], x)
            v_ref[:, s] = raw[cols:].astype(BF)
            for h in range(heads):
                r = slice(h * HD, (h + 1) * HD)
                kn, ki_ref[h : h + 1, s] = norm_rows(raw[r])
                kn = (kn * k_gain).astype(BF)
                k_ref[r, s] = kn
                kt[h, :HD, s] = kn
                kt[h, HD:, s] = fk_ref[:, s]
                vn[h, s, :] = jnp.concatenate([raw[cols + h * HD : cols + (h + 1) * HD], ones], axis=0).T.astype(BF)
            if mine:
                raw = nt(wt_ref[2 * cols :], x)
                for h in range(heads):
                    r = slice(h * HD, (h + 1) * HD)
                    qh, qi_ref[h : h + 1, s] = norm_rows(raw[r])
                    qh = qh * (q_gain * QSCALE)
                    q_ref[r, s] = qh.astype(BF)
                    qa = jnp.concatenate([qh, fq_ref[:, s].astype(F32)], axis=0)
                    qn[h, s, :] = qa.T.astype(BF)
        for qb in range(half // BQ):
            s = slice(qb * BQ, (qb + 1) * BQ)

            def body(i, accs, qb=qb, s=s):
                ks = pl.ds(pl.multiple_of(l_ref[qb * nk + i] * BK_FWD, BK_FWD), BK_FWD)
                out = []
                for h in range(heads):
                    p = jnp.exp2(nn(qn[h, s, :], kt[h, :, ks])).astype(BF)
                    out.append(accs[h] + nn(p, vn[h, ks, :]))
                return tuple(out)

            accs = lax.fori_loop(0, n_ref[qb], body, tuple(jnp.zeros((BQ, 2 * HD), F32) for _ in range(heads)))
            for h in range(heads):
                t = accs[h].T
                total = t[HD : HD + 1]
                att_ref[h * HD : (h + 1) * HD, s] = (t[:HD] / total).astype(BF)
                lse_ref[h : h + 1, s] = jnp.log2(total)

    return queue(
        "attn_fwd",
        kern,
        (own, oth, w, fq, fk, qg, kg),
        [
            ((cols, half), BF),
            ((heads, half), F32),
            ((cols, half), BF),
            ((cols, slots), BF),
            ((cols, slots), BF),
            ((3 * cols, width), BF),
            ((heads, half), F32),
            ((heads, slots), F32),
        ],
        scalars=(tensor, ids),
        scratch=[pltpu.VMEM((heads, 2 * HD, slots), BF), pltpu.VMEM((heads, half, 2 * HD), BF), pltpu.VMEM((heads, slots, 2 * HD), BF), pltpu.SMEM((half // BQ,), jnp.int32), pltpu.SMEM((half // BQ * nk + 1,), jnp.int32)],
        vmem=20,
        us=50,
    )


def attn_bwd(queue, tensor, ids, q, k, v, qi, ki, att, lse, branch, wot, lo, fq, fk, qg, kg, us):
    cols, half = q.shape
    slots = k.shape[1]
    heads = cols // HD
    nk = slots // BK_BWD

    def kern(t_ref, ids_ref, q_ref, k_ref, v_ref, qi_ref, ki_ref, att_ref, lse_ref, b0_ref, b1_ref, wot_ref, fq_ref, fk_ref, qg_ref, kg_ref, g_ref, gq_ref, gains_ref, kn, vn, qt, qn, dt, dn, dqt, dk, dv, n_ref, l_ref):
        list_blocks(t_ref, ids_ref, slots, BK_BWD, n_ref, l_ref)
        q_gain, k_gain = column(qg_ref[...]), column(kg_ref[...])
        row = lax.broadcasted_iota(jnp.int32, (HD, CHUNK), 0)
        three = jnp.where(row < 3, 1.0, 0.0).astype(F32)
        for c in range(slots // CHUNK):
            s = slice(c * CHUNK, (c + 1) * CHUNK)
            for h in range(heads):
                r = slice(h * HD, (h + 1) * HD)
                full = jnp.concatenate([k_ref[r, s], fk_ref[:, s]], axis=0).astype(F32)
                kn[h, s, :] = full.T.astype(BF)
                vn[h, s, :] = jnp.concatenate([v_ref[r, s].astype(F32), three], axis=0).T.astype(BF)
                dk[h, s, :] = jnp.zeros((CHUNK, 2 * HD), F32)
                dv[h, s, :] = jnp.zeros((CHUNK, 2 * HD), F32)
        for c in range(half // CHUNK):
            s = slice(c * CHUNK, (c + 1) * CHUNK)
            grad = nt(wot_ref[lo : lo + cols], (b0_ref if c == 0 else b1_ref)[...]).astype(BF).astype(F32)
            for h in range(heads):
                r = slice(h * HD, (h + 1) * HD)
                a, b, d = split3(-lse_ref[h : h + 1, s])
                f = fq_ref[:, s].astype(F32)
                f = jnp.where(row == 33, a, jnp.where(row == 34, b, jnp.where(row == 35, d, f)))
                full = jnp.concatenate([q_ref[r, s].astype(F32), f], axis=0)
                qt[h, :, s] = full.astype(BF)
                qn[h, s, :] = full.T.astype(BF)
                a, b, d = split3(-jnp.sum(grad[r] * att_ref[r, s].astype(F32), axis=0, keepdims=True))
                f = jnp.where(row == 0, a, jnp.where(row == 1, b, jnp.where(row == 2, d, 0.0)))
                full = jnp.concatenate([grad[r], f], axis=0)
                dt[h, :, s] = full.astype(BF)
                dn[h, s, :] = full.T.astype(BF)
        for qb in range(half // BQ):
            s = slice(qb * BQ, (qb + 1) * BQ)

            def body(i, accs, qb=qb, s=s):
                ks = pl.ds(pl.multiple_of(l_ref[qb * nk + i] * BK_BWD, BK_BWD), BK_BWD)
                out = []
                for h in range(heads):
                    p = jnp.exp2(nn(kn[h, ks, :], qt[h, :, s]))
                    ds = (p * nn(vn[h, ks, :], dt[h, :, s])).astype(BF)
                    dv[h, ks, :] += nn(p.astype(BF), dn[h, s, :])
                    dk[h, ks, :] += nn(ds, qn[h, s, :])
                    out.append(accs[h] + nn(k_ref[h * HD : (h + 1) * HD, ks], ds))
                return tuple(out)

            accs = lax.fori_loop(0, n_ref[qb], body, tuple(jnp.zeros((HD, BQ), F32) for _ in range(heads)))
            for h in range(heads):
                dqt[h, :, s] = accs[h]

        def back(grad, gain, hat, inv):
            u = grad * gain
            out = inv * (u - jnp.mean(u, axis=0, keepdims=True) - hat * jnp.mean(u * hat, axis=0, keepdims=True))
            return out.astype(BF), jnp.sum(grad * hat, axis=1, keepdims=True)

        sum_q = jnp.zeros((HD, 1), F32)
        sum_k = jnp.zeros((HD, 1), F32)
        for h in range(heads):
            r = slice(h * HD, (h + 1) * HD)
            for c in range(slots // CHUNK):
                s = slice(c * CHUNK, (c + 1) * CHUNK)
                g_ref[r, s], more = back(dk[h, s, :].T[:HD] * (1.0 / LOG2E), k_gain, k_ref[r, s].astype(F32) * (1.0 / k_gain), ki_ref[h : h + 1, s])
                sum_k += more
                g_ref[cols + h * HD : cols + (h + 1) * HD, s] = dv[h, s, :].T[:HD].astype(BF)
            for c in range(half // CHUNK):
                s = slice(c * CHUNK, (c + 1) * CHUNK)
                gq_ref[r, s], more = back(dqt[h, :, s] * 0.125, q_gain, q_ref[r, s].astype(F32) * (1.0 / (q_gain * QSCALE)), qi_ref[h : h + 1, s])
                sum_q += more
        gains_ref[:, :1] = sum_q
        gains_ref[:, 1:] = sum_k

    big = (heads, slots, 2 * HD)
    small = (heads, half, 2 * HD)
    flat = (heads, 2 * HD, half)
    return queue(
        "attn_bwd",
        kern,
        (q, k, v, qi, ki, att, lse, *branch, wot, fq, fk, qg, kg),
        [((2 * cols, slots), BF), ((cols, half), BF), ((HD, 2), F32)],
        scalars=(tensor, ids),
        scratch=[
            pltpu.VMEM(big, BF),
            pltpu.VMEM(big, BF),
            pltpu.VMEM(flat, BF),
            pltpu.VMEM(small, BF),
            pltpu.VMEM(flat, BF),
            pltpu.VMEM(small, BF),
            pltpu.VMEM((heads, HD, half), F32),
            pltpu.VMEM(big, F32),
            pltpu.VMEM(big, F32),
            pltpu.SMEM((half // BQ,), jnp.int32),
            pltpu.SMEM((half // BQ * nk + 1,), jnp.int32),
        ],
        vmem=28,
        us=us,
    )


def features(queue, ids, tensor):
    parts, slots = ids.shape

    def kern(t_ref, ids_ref, fq_ref, fk_ref):
        row = lax.broadcasted_iota(jnp.int32, (HD, slots), 0)
        for i in range(parts):
            s = slice(i * slots, (i + 1) * slots)
            hot = ids_ref[pl.ds(t_ref[0] ^ i, 1), :] + 1 == row
            ones = (row >= 32) & (row < 36)
            fk_ref[:, s] = jnp.where((hot & (row < 32)) | ones, 1.0, 0.0).astype(BF)
            if i < 2:
                fq_ref[:, s] = jnp.where(hot & (row < 32), BIG, jnp.where(row == 32, -BIG, 0.0)).astype(BF)

    outs = [((HD, 2 * slots), BF), ((HD, parts * slots), BF)]
    return queue("features", kern, (ids,), outs, scalars=(tensor,), us=50)


def list_blocks(t_ref, ids_ref, slots, size, n_ref, l_ref):
    share = ids_ref.shape[0] // 4

    def ends(block, length):
        at = block * length
        at = (t_ref[0] ^ (at // share)) * share + at % share
        first, last = ids_ref[at], ids_ref[at + length - 1]
        return jnp.where(first < 0, 99, first), jnp.where(last < 0, 99, last)

    nk = slots // size
    keys = [ends(kb, size) for kb in range(nk)]
    for qb in range(slots // 2 // BQ):
        first, last = ends(qb, BQ)
        n = jnp.int32(0)
        for kb, (low, high) in enumerate(keys):
            l_ref[qb * nk + n] = kb
            n += ((first <= high) & (low <= last)).astype(jnp.int32)
        n_ref[qb] = n


def column(row):
    n = row.shape[1]
    same = lax.broadcasted_iota(jnp.int32, (n, n), 0) == lax.broadcasted_iota(jnp.int32, (n, n), 1)
    return jnp.sum(jnp.where(same, row, 0.0), axis=1, keepdims=True)


def gelu_pair(v):
    t = 1.0 / (1.0 + (0.3275911 * 0.5**0.5) * jnp.abs(v))
    e = jnp.exp2(v * v * (-0.5 * LOG2E))
    poly = ((((0.5307027145 * t - 0.7265760135) * t + 0.7107068705) * t - 0.142248368) * t + 0.127414796) * t
    tail = poly * e
    phi = jnp.where(v < 0, tail, 1.0 - tail)
    return v * phi, phi + v * e * 0.3989422804014327


def split_store(value, bit, keep, send, blocks, lead=(), at=slice(None)):
    rows = value.shape[0] // blocks
    value = value.astype(BF)
    for b in range(2):

        @pl.when(bit == b)
        def _(b=b):
            for j in range(blocks):
                part = value[j * rows : (j + 1) * rows]
                if j % 2 == b:
                    keep[(*lead, j // 2, slice(None), at)] = part
                else:
                    send[(*lead, j // 2, slice(None), at)] = part


COLS = 256
PLACES = ((0, 0, 0, 256), (256, 1, 0, 256), (512, 0, 256, 128), (640, 1, 256, 128))
HALF_COLS = 384


def mlp(queue, xs, gs, both, bit, blocks, slope=None):
    half, width = xs[0].shape
    cols = both.shape[2] // 2
    forward = slope is None
    rows = 256

    def kern(bit_ref, x0, x1, g0, g1, w_ref, *rest):
        rest = list(rest)
        if forward:
            hid = rest.pop(0)
        slope_ref = rest.pop(0)
        if forward:
            keep_a, send_a, keep_b, send_b, turned = rest
        else:
            keep_a, send_a, keep_b, send_b, own_ref, out_ref, hid, turned = rest
        left = (g0, g1) if forward else (x0, x1)
        feed = (x0, x1) if forward else (g0, g1)
        w_in, w_out = (0, cols) if forward else (cols, 0)
        for i, ref in enumerate(left):
            turned[:, i * half : (i + 1) * half] = ref[...].T

        def units(r, i, c, lo):
            o = slice(lo + i * half, lo + i * half + rows)
            at = slice(c, c + COLS) if isinstance(c, int) else pl.ds(pl.multiple_of(c, COLS), COLS)
            w_at = slice(w_in + c, w_in + c + COLS) if isinstance(c, int) else pl.ds(pl.multiple_of(w_in + c, COLS), COLS)
            value = nn(feed[i][lo : lo + rows, :], w_ref[r, :, w_at])
            if forward:
                value, grad = gelu_pair(value)
                slope_ref[r, o, at] = grad.astype(BF)
            else:
                value = value * slope_ref[r, o, at].astype(F32)
            hid[r, o, at] = value.astype(BF)

        def weights(r, c):
            value = nn(turned[...], hid[r, :, c : c + COLS])
            for first, part, to, count in PLACES:
                if c <= first < c + COLS:
                    piece = value[:, first - c : first - c + count]
                    if part == 0:
                        split_store(piece, bit_ref[0], keep_a, send_a, blocks, (r,), slice(to, to + count))
                    else:
                        (send_b if r else keep_b)[:, to : to + count] = piece.astype(BF)

        spots = [(i, lo) for i in range(2) for lo in range(0, half, rows)]

        if forward:

            @pl.loop(0, cols // COLS)
            def _(k):
                for i, lo in spots:
                    units(0, i, k * COLS, lo)

        else:
            for c in range(0, cols, COLS):
                for i, lo in spots:
                    units(0, i, c, lo)

        for c in range(0, cols, COLS):
            for i, lo in spots:
                units(1, i, c, lo)
            weights(0, c)
        for c in range(0, cols, COLS):
            weights(1, c)
        if not forward:
            shares(hid, w_ref, slice(w_out, w_out + cols), own_ref, out_ref)

    part_a = ((2, blocks // 2, width // blocks, HALF_COLS), BF)
    part_b = ((width, cols - HALF_COLS), BF)
    outs = [part_a, part_a, part_b, part_b]
    inputs = [*xs, *gs, both]
    flat = (2, 2 * half, cols)
    scratch = [pltpu.VMEM((width, 2 * half), BF)]
    if forward:
        outs = [(flat, BF), (flat, BF), *outs]
    else:
        inputs.append(slope)
        outs += [((half, width), F32), ((half, width), BF)]
        scratch.insert(0, pltpu.VMEM(flat, BF))
    return queue("mlp_fwd" if forward else "mlp_bwd", kern, inputs, outs, scalars=(bit,), scratch=scratch, vmem=28, us=0)


def shares(hid, w_ref, at, own_ref, out_ref):
    half = own_ref.shape[0]
    rows = 256
    for i, out in enumerate((own_ref, out_ref)):
        for lo in range(0, half, rows):
            o = slice(lo + i * half, lo + i * half + rows)
            out[lo : lo + rows, :] = (nt(hid[0, o, :], w_ref[0, :, at]) + nt(hid[1, o, :], w_ref[1, :, at])).astype(out.dtype)


def mlp_out(queue, hid, both, us):
    _, slots, cols = hid.shape
    width = both.shape[1]

    def kern(hid_ref, w_ref, own_ref, out_ref):
        shares(hid_ref, w_ref, slice(cols, 2 * cols), own_ref, out_ref)

    outs = [((slots // 2, width), F32), ((slots // 2, width), BF)]
    return queue("mlp_out", kern, (hid, both), outs, us=us)


def out_proj(queue, atts, w, lo):
    cols, slots = atts[0].shape
    width = w.shape[0]
    half = slots // 2

    def kern(a0, a1, w_ref, own_ref, send_ref, wot_ref):
        wot_ref[...] = w_ref[:, :lo].T
        for i, out in enumerate((own_ref, send_ref)):
            s = slice(i * half, (i + 1) * half)
            both = jnp.concatenate([a0[:, s], a1[:, s]], axis=0)
            out[...] = nn(both.T, wot_ref[...]).astype(out.dtype)

    outs = [((half, width), F32), ((half, width), BF), ((lo, width), BF)]
    return queue("out_proj", kern, (*atts, w), outs)


def middle_norm(queue, own, got, tok, gain, bias):
    slots, width = own.shape

    def kern(own_ref, got_ref, tok_ref, gain_ref, bias_ref, mid_ref, out_ref):
        def body(s):
            mid = tok_ref[s, :].astype(F32) + own_ref[s, :] + got_ref[s, :].astype(F32)
            mid_ref[s, :] = mid
            hat, _ = hat_of(mid)
            out_ref[s, :] = (hat * gain_ref[...] + bias_ref[...]).astype(BF)

        each(slots, body)

    outs = [((slots, width), F32), ((slots, width), BF)]
    return queue("middle_norm", kern, (own, got, tok, gain, bias), outs, us=50)


def middle_back(queue, own, got, mid, cot, gain, branch_own, branch_got):
    slots, width = own.shape

    def kern(own_ref, got_ref, mid_ref, cot_ref, gain_ref, bo_ref, bg_ref, grad_ref, out_ref, sums_ref, result_ref):
        sums_ref[...] = jnp.zeros_like(sums_ref)

        def body(s):
            grad = own_ref[s, :] + got_ref[s, :].astype(F32)
            mid = mid_ref[s, :]
            result_ref[s, :] = (mid + bo_ref[s, :] + bg_ref[s, :].astype(F32)).astype(BF)
            hat, inv = hat_of(mid)
            sums_ref[0:1] += jnp.sum(grad * hat, axis=0, keepdims=True)
            sums_ref[1:2] += jnp.sum(grad, axis=0, keepdims=True)
            grad = cot_ref[s, :].astype(F32) + hat_back(grad, gain_ref[...], hat, inv)
            grad_ref[s, :] = grad
            out_ref[s, :] = grad.astype(BF)

        each(slots, body)

    outs = [((slots, width), F32), ((slots, width), BF), ((2, width), F32), ((slots, width), BF)]
    return queue("middle_back", kern, (own, got, mid, cot, gain, branch_own, branch_got), outs, us=50)


def proj_grad(queue, g, gq, own, oth, wt, bit, blocks, prev=(), atts=(), branch=()):
    two, slots = g.shape
    cols, half = gq.shape
    width = own.shape[1]
    block = half // 2
    lead = cols * len(atts)

    def kern(bit_ref, g_ref, gq_ref, own_ref, oth_ref, wt_ref, *rest):
        rest = list(rest)
        prev_refs = [rest.pop(0) for _ in prev]
        att_refs = [rest.pop(0) for _ in atts]
        branch_refs = [rest.pop(0) for _ in branch]
        keep_ref, send_ref = rest[:2]
        outs = rest[2:]
        for i in reversed(range(4)):
            s = slice(i * block, (i + 1) * block)
            value = nn(g_ref[:, s].T, wt_ref[:two])
            if i < 2:
                value += nn(gq_ref[:, s].T, wt_ref[two:])
            if prev_refs:
                value += prev_refs[i % 2][i // 2].astype(F32)
            outs[i % 2][i // 2] = value.astype(BF)
        parts = []
        for att in att_refs:
            parts.append(nn(att[:, :block], branch_refs[0][...]) + nn(att[:, block:], branch_refs[1][...]))
        parts.append(nn(g_ref[:, :half], own_ref[...]) + nn(g_ref[:, half:], oth_ref[...]))
        parts.append(nn(gq_ref[...], own_ref[...]))
        split_store(jnp.concatenate(parts, axis=0).T, bit_ref[0], keep_ref, send_ref, blocks)

    share = ((blocks // 2, width // blocks, lead + two + cols), BF)
    return queue(
        "proj_grad",
        kern,
        (g, gq, own, oth, wt, *prev, *atts, *branch),
        [share, share] + [((2, block, width), BF)] * 2,
        scalars=(bit,),
        vmem=22,
        us=50,
    )


def norm_sums(queue, grads, toks):
    slots, width = toks[0].shape

    def kern(*refs):
        sums_ref = refs[2]
        sums_ref[...] = jnp.zeros_like(sums_ref)

        def body(s):
            first = jnp.zeros((1, width), F32)
            second = jnp.zeros((1, width), F32)
            for i, tok_ref in enumerate(refs[3:]):
                grad = refs[i % 2][i // 2, s, :].astype(F32)
                hat, _ = hat_of(tok_ref[s, :].astype(F32))
                first += jnp.sum(grad * hat, axis=0, keepdims=True)
                second += jnp.sum(grad, axis=0, keepdims=True)
            sums_ref[0:1] += first
            sums_ref[1:2] += second

        each(slots, body)

    return queue("norm_sums", kern, grads, [((2, width), F32)], vmem=14, fetched=toks)[0]


def tokens_back(queue, own, got_x, tok, gain, mid):
    slots, width = tok.shape

    def kern(own_ref, x_ref, tok_ref, gain_ref, mid_ref, out_ref):
        def body(s):
            hat, inv = hat_of(tok_ref[s, :].astype(F32))
            grad = own_ref[s, :] + x_ref[s, :].astype(F32)
            out_ref[s, :] = (mid_ref[s, :] + hat_back(grad, gain_ref[...], hat, inv)).astype(BF)

        each(slots, body)

    return queue("tokens_back", kern, (own, got_x, tok, gain, mid), [((slots, width), BF)])[0]


def last_sum(queue, kept, got, lead, across):
    _, rows, _ = kept.shape
    cols = lead.shape[1]

    def kern(kept_ref, got_ref, lead_ref, across_ref, out_ref, qkv_ref):
        out_ref[...] = (lead_ref[...] + across_ref[:, :cols].astype(F32)).T
        value = kept_ref[0] + got_ref[0].astype(F32) + across_ref[:, cols:].astype(F32)
        for i in range(3):
            lo = cols * (2, 0, 1)[i]
            qkv_ref[:, i, :] = value[:, lo : lo + cols]

    return queue("last_sum", kern, (kept, got, lead, across), [((cols, rows), F32), ((rows, 3, cols), F32)])


def slot_sums(queue, kept, got):
    _, slots, width = kept.shape

    def kern(kept_ref, got_ref, across, own):
        across[...] = (kept_ref[1].astype(F32) + got_ref[1].astype(F32)).astype(BF)
        own[...] = kept_ref[0].astype(F32) + got_ref[0].astype(F32)

    return queue("slot_sums", kern, (kept, got), [((slots, width), BF), ((slots, width), F32)])


def gain_rows(queue, one, two, width, us):
    def kern(a, b, out):
        value = (a[...] + b[...]).T
        out[...] = jnp.concatenate([value, jnp.zeros((2, width - HD), F32)], axis=1)

    return queue("gain_rows", kern, (one, two), [((2, width), F32)], us=us)[0]


def add_up(queue, one, two, dtype, us=0):
    def kern(a, b, out):
        out[...] = (a[...].astype(F32) + b[...].astype(F32)).astype(dtype)

    return queue("add_up", kern, (one, two), [(one.shape, dtype)], us=us)[0]


def side_by_side(queue, *arrays, us=0):
    edges = [0]
    for a in arrays:
        edges.append(edges[-1] + a.shape[1])

    def kern(*refs):
        for ref, lo, hi in zip(refs, edges, edges[1:]):
            refs[-1][:, lo:hi] = ref[...]

    return queue("side_by_side", kern, arrays, [((arrays[0].shape[0], edges[-1]), BF)], us=us)[0]


def pair_dp(queue, held, got, bit, cuts=None):
    m, rows, cols = held.shape
    cuts = [0, rows] if cuts is None else [0, *cuts, rows]

    def kern(bit_ref, held_ref, got_ref, *outs):
        bit = bit_ref[0]
        for i in range(m):
            for lo, hi, out in zip(cuts, cuts[1:], outs):
                out[2 * i + bit] = held_ref[i, lo:hi]
                out[2 * i + 1 - bit] = got_ref[i, lo:hi]

    outs = [((2 * m, hi - lo, cols), held.dtype) for lo, hi in zip(cuts, cuts[1:])]
    return queue("pair_dp", kern, (held, got), outs, scalars=(bit,))


def pair_both(queue, part_a, got_a, part_b, got_b, bit):
    m, rows_a, cols = part_a.shape
    rows_b = part_b.shape[1]

    def kern(bit_ref, a, ga, b, gb, out_a, out_b):
        bit = bit_ref[0]
        out_a[0] = a[...]
        out_a[1] = ga[...]
        for i in range(m):
            out_b[i, bit] = b[i]
            out_b[i, 1 - bit] = gb[i]

    outs = [((2, m, rows_a, cols), BF), ((m, 2, rows_b, cols), BF)]
    return queue("pair_both", kern, (part_a, got_a, part_b, got_b), outs, scalars=(bit,))


def pair_last(queue, part_a, got_a, part_b, got_b, bit):
    _, m, rows_a, cols = part_a.shape
    rows_b = part_b.shape[2]

    def kern(bit_ref, a, ga, b, gb, out):
        bit = bit_ref[0]
        for i in range(m):
            for t in range(2):
                out[t, i, bit, :rows_a] = a[t, i]
                out[t, i, 1 - bit, :rows_a] = ga[t, i]
            for y in range(2):
                out[0, i, y, rows_a:] = b[i, y]
                out[1, i, y, rows_a:] = gb[i, y]

    outs = [((2, m, 2, rows_a + rows_b, cols), BF)]
    (res,) = queue("pair_last", kern, (part_a, got_a, part_b, got_b), outs, scalars=(bit,))
    return res.reshape(2, 2 * m * (rows_a + rows_b), cols)


def fold_dp(queue, kept, got, bit):
    n, rows, cols = kept.shape

    def kern(bit_ref, kept_ref, got_ref, keep, send):
        bit = bit_ref[0]
        for i in range(n // 2):
            keep[i] = kept_ref[2 * i + bit].astype(F32) + got_ref[2 * i + bit].astype(F32)
            send[i] = (kept_ref[2 * i + 1 - bit].astype(F32) + got_ref[2 * i + 1 - bit].astype(F32)).astype(BF)

    outs = [((n // 2, rows, cols), F32), ((n // 2, rows, cols), BF)]
    return queue("fold_dp", kern, (kept, got), outs, scalars=(bit,))


def fold_first(queue, keep_a, got_a, keep_b, got_b, next_a, next_b, bit, us):
    _, n, rows, cols = keep_a.shape

    def kern(bit_ref, ka, ga, kb, gb, na, nb, x_msg, y_msg, keep_a, keep_b):
        bit = bit_ref[0]
        keep_a[...] = ka[0].astype(F32) + ga[0].astype(F32)
        x_msg[:n] = (ka[1].astype(F32) + ga[1].astype(F32)).astype(BF)
        x_msg[n:] = nb[...]
        for i in range(n):
            keep_b[i] = kb[2 * i + bit].astype(F32) + gb[2 * i + bit].astype(F32)
            y_msg[i] = (kb[2 * i + 1 - bit].astype(F32) + gb[2 * i + 1 - bit].astype(F32)).astype(BF)
            y_msg[n + i] = na[0, i]
            y_msg[2 * n + i] = na[1, i]

    outs = [((3 * n, rows, cols), BF)] * 2 + [((n, rows, cols), F32)] * 2
    return queue("fold_first", kern, (keep_a, got_a, keep_b, got_b, next_a, next_b), outs, scalars=(bit,), us=us)


def fold_second(queue, keep_a, keep_b, next_a, next_b, x_got, y_got, bit, far_bit):
    n, rows, cols = keep_a.shape

    def kern(bit_ref, far_ref, ka, kb, na, nb, xg, yg, keep, send, keep_na, send_na, keep_nb, send_nb):
        bit, far = bit_ref[0], far_ref[0]
        for i in range(n // 2):
            for first, part, at, count in PLACES:
                k, g = ((ka, xg), (kb, yg))[part]
                to, at = slice(first, first + count), slice(at, at + count)
                keep[i, :, to] = k[2 * i + far, :, at] + g[2 * i + far, :, at].astype(F32)
                send[i, :, to] = (k[2 * i + 1 - far, :, at] + g[2 * i + 1 - far, :, at].astype(F32)).astype(BF)
        for i in range(n):
            keep_na[i] = na[0, i].astype(F32) + yg[n + i].astype(F32)
            send_na[i] = (na[1, i].astype(F32) + yg[2 * n + i].astype(F32)).astype(BF)
            keep_nb[i] = nb[2 * i + bit].astype(F32) + xg[n + 2 * i + bit].astype(F32)
            send_nb[i] = (nb[2 * i + 1 - bit].astype(F32) + xg[n + 2 * i + 1 - bit].astype(F32)).astype(BF)

    half = (n, rows, cols)
    outs = [((n // 2, rows, 2 * cols), F32), ((n // 2, rows, 2 * cols), BF), (half, F32), (half, BF), (half, F32), (half, BF)]
    arrays = (keep_a, keep_b, next_a, next_b, x_got, y_got)
    return queue("fold_second", kern, arrays, outs, scalars=(bit, far_bit))


def fold_joined(queue, keep_a, got_a, keep_b, got_b, bit):
    n, rows, cols_a = keep_a.shape
    cols = cols_a + keep_b.shape[-1]

    def kern(bit_ref, ka, ga, kb, gb, keep, send):
        bit = bit_ref[0]
        for i in range(n // 2):
            for first, part, at, count in PLACES:
                k, g = ((ka, ga), (kb, gb))[part]
                to, at = slice(first, first + count), slice(at, at + count)
                keep[i, :, to] = k[2 * i + bit, :, at] + g[2 * i + bit, :, at].astype(F32)
                send[i, :, to] = (k[2 * i + 1 - bit, :, at] + g[2 * i + 1 - bit, :, at].astype(F32)).astype(BF)

    outs = [((n // 2, rows, cols), F32), ((n // 2, rows, cols), BF)]
    return queue("fold_joined", kern, (keep_a, got_a, keep_b, got_b), outs, scalars=(bit,))


def sum_x(queue, kept, got, cols):
    _, rows, total = kept.shape

    def kern(kept_ref, got_ref, send, keep):
        value = kept_ref[0] + got_ref[0].astype(F32)
        keep[...] = value[:, :cols]
        send[...] = value[:, cols:].astype(BF)

    return queue("sum_x", kern, (kept, got), [((rows, total - cols), BF), ((rows, cols), F32)])


def swap(values, axis, mask):
    return lax.ppermute(values, axis, [(i, i ^ mask) for i in range(lax.axis_size(axis))])


def swap_core(values):
    return swap(values, "tensor", 1)


def swap_x(values):
    return swap(values, "tensor", 2)


def per_device(tokens, picture_ids, ln1_gain, ln1_bias, w_qkv, q_gain, k_gain, w_out, ln2_gain, ln2_bias, w_up, w_down, cotangent):
    slots, width = tokens.shape[1:]
    local = w_qkv.shape[2]
    n_dp = lax.axis_size("dp")
    rows = width // n_dp
    q_slots = 2 * slots
    tok = tokens[0]
    cot = cotangent[0]
    tensor = lax.axis_index("tensor").reshape(1)
    me = lax.axis_index("dp")
    levels = list(reversed(range(n_dp.bit_length() - 1)))
    far, near = levels[:-1], levels[-1]
    bits = {level: ((me >> level) & 1).reshape(1) for level in levels}
    queue = Queue()
    gain1, bias1, gain2, bias2 = (v.reshape(1, width) for v in (ln1_gain, ln1_bias, ln2_gain, ln2_bias))
    qg, kg = q_gain.reshape(1, HD), k_gain.reshape(1, HD)

    def swap_dp(values, level):
        return swap(values, "dp", 1 << level)

    out_t = w_out.T
    part_0 = jnp.concatenate([w_qkv[:, 1], w_qkv[:, 2], w_qkv[:, 0]], axis=1)
    part_0 = side_by_side(queue, part_0)
    got_0 = swap_dp(part_0[None], far[0])
    ids = picture_ids[0]
    fq, fk = features(queue, ids.reshape(4, slots), tensor)
    got_cols = swap_x(side_by_side(queue, out_t, part_0))
    tok_x = swap_x(side_by_side(queue, tok, us=50))
    tok_c = swap_core(tok)
    cot_c = swap_core(cot)
    both = side_by_side(queue, w_up, w_down.T)[None]
    half = rows // 2
    (part_0,) = pair_dp(queue, part_0[None], got_0, bits[far[0]])
    part_1 = side_by_side(queue, out_t, got_cols)[None]
    got_0 = swap_dp(part_0, levels[1])
    got_1 = swap_dp(part_1, far[0])
    for level, after_it in zip(levels[1:-1], levels[2:]):
        (part_0,) = pair_dp(queue, part_0, got_0, bits[level])
        got_0 = swap_dp(part_0, after_it)
    for level, after_it in zip(levels[:-2], levels[1:-1]):
        (part_1,) = pair_dp(queue, part_1, got_1, bits[level])
        got_1 = swap_dp(part_1, after_it)
    both = side_by_side(queue, both[0])[None]
    got_b = swap_dp(both, far[0])
    own = norm_pair(queue, tok, tok_c, gain1, bias1, us=50)
    (part_1,) = pair_dp(queue, part_1, got_1, bits[levels[-2]])
    got_1 = swap_dp(part_1, levels[-1])
    (w_0,) = pair_dp(queue, part_0, got_0, bits[near])
    w_0 = w_0.reshape(width, 3 * local)
    for level, after_it in zip(far[:-1], far[1:]):
        (both,) = pair_dp(queue, both, got_b, bits[level])
        got_b = swap_dp(both, after_it)
    tok_xc = swap_core(side_by_side(queue, tok_x))
    oth = norm_pair(queue, tok_x, tok_xc, gain1, bias1)
    att_0, lse_0, q_0, k_0, v_0, wt_0, qi_0, ki_0 = attn_fwd(queue, tensor, ids, own, oth, w_0, 0, fq, fk, qg, kg)
    part_a, part_b = pair_dp(queue, both, got_b, bits[far[-1]], (half,))
    got_a, got_b = swap_x(part_a), swap_dp(part_b, near)
    (w_1,) = pair_dp(queue, part_1, got_1, bits[near])
    w_1 = w_1.reshape(width, 5 * local)
    att_1, lse_1, q_1, k_1, v_1, wt_1, qi_1, ki_1 = attn_fwd(queue, tensor, ids, own, oth, w_1, 2 * local, fq, fk, qg, kg)
    part_a, part_b = pair_both(queue, part_a, got_a, part_b, got_b, bits[near])
    got_a, got_b = swap_dp(part_a, near), swap_x(part_b)
    branch_own, branch_send, wot = out_proj(queue, (att_0, att_1), w_1, 2 * local)
    middle, normed = middle_norm(queue, branch_own, swap_core(branch_send), tok, gain2, bias2)
    normed_c = swap_core(normed)
    both = pair_last(queue, part_a, got_a, part_b, got_b, bits[near])

    bit = bits[near]
    rest = levels[::-1][1:]
    xs, gs = (normed, normed_c), (cot, cot_c)
    grid = (n_dp, rows, w_up.shape[1] - HALF_COLS)

    def first_step(parts):
        keep_a, send_a, keep_b, send_b = parts
        return keep_a, swap_dp(send_a, near), keep_b.reshape(grid), swap_x(send_b).reshape(grid)

    def second_step(keep_a, send_a, keep_b, send_b):
        return keep_a, swap_x(send_a), keep_b, swap_dp(send_b, near)

    def next_step(keep, send, level):
        return keep, swap_dp(send, level)

    hid, slope, *parts = mlp(queue, xs, gs, both, bit, n_dp)
    d = first_step(parts)
    mlp_own, mlp_send = mlp_out(queue, hid, both, 50)
    *parts, gn_own, gn_send = mlp(queue, xs, gs, both, bit, n_dp, slope)
    u_keep_a, u_send_a, u_keep_b, u_send_b = parts
    x_msg, y_msg, *d = fold_first(queue, *d, u_send_a, u_send_b.reshape(grid), bit, 50)
    x_got, y_got = swap_x(x_msg), swap_dp(y_msg, near)
    grad_mid, branch, sums2, result = middle_back(
        queue, gn_own, swap_core(gn_send), middle, cot, gain2, mlp_own, swap_core(mlp_send)
    )
    branches = (branch, swap_core(branch))
    g, gq, gains_1 = attn_bwd(queue, tensor, ids, q_1, k_1, v_1, qi_1, ki_1, att_1, lse_1, branches, wot, local, fq, fk, qg, kg, 0)
    *d, u_keep_a, u_send_a, u_keep_b, u_send_b = fold_second(
        queue, *d, u_keep_a, u_keep_b.reshape(grid), x_got, y_got, bit, bits[rest[0]]
    )
    u = second_step(u_keep_a, u_send_a, u_keep_b, u_send_b)
    d = next_step(*d, rest[0])
    a_keep, a_send, *gx = proj_grad(queue, g, gq, own, oth, wt_1, bit, n_dp, atts=(att_0, att_1), branch=branches)
    a = next_step(a_keep, a_send, near)
    u = next_step(*fold_joined(queue, *u, bits[rest[0]]), rest[0])
    d = next_step(*fold_dp(queue, *d, bits[rest[1]]), rest[1])
    g, gq, gains_0 = attn_bwd(queue, tensor, ids, q_0, k_0, v_0, qi_0, ki_0, att_0, lse_0, branches, wot, 0, fq, fk, qg, kg, 50)
    a = next_step(*fold_dp(queue, *a, bits[rest[0]]), rest[0])
    u = next_step(*fold_dp(queue, *u, bits[rest[1]]), rest[1])
    for level in rest[2:]:
        d = next_step(*fold_dp(queue, *d, bits[level]), level)
        u = next_step(*fold_dp(queue, *u, bits[level]), level)
    grad_d = add_up(queue, *d, F32).reshape(rows, -1)
    z_keep, z_send, *gx = proj_grad(queue, g, gq, own, oth, wt_0, bit, n_dp, prev=gx)
    z = next_step(z_keep, z_send, near)
    gx_got = swap_core(gx[1])
    gains = gain_rows(queue, gains_0, gains_1, width, 50)
    across, grad_normed = slot_sums(queue, gx[0], gx_got)
    got = swap_x(across)
    sums1 = norm_sums(queue, gx, (tok, tok_c, tok_x, tok_xc))
    small = jnp.concatenate([sums1, sums2, gains])
    small_got = swap_core(small)
    grad_u = add_up(queue, *u, F32).reshape(rows, -1)
    z = next_step(*fold_dp(queue, *z, bits[rest[0]]), rest[0])
    for level in rest[1:]:
        a = next_step(*fold_dp(queue, *a, bits[level]), level)
    small = add_up(queue, small, small_got, F32)
    small_got = swap_x(small)
    grad_tokens = tokens_back(queue, grad_normed, got, tok, gain1, grad_mid)
    small = add_up(queue, small, small_got, F32)
    small_got = swap_dp(small, near)
    for level in rest[1:]:
        z = next_step(*fold_dp(queue, *z, bits[level]), level)
    a_send, lead = sum_x(queue, *a, local)
    a_got = swap_x(a_send)
    for level in rest:
        small = add_up(queue, small, small_got, F32)
        small_got = swap_dp(small, level)
    grad_out, grad_qkv = last_sum(queue, *z, lead, a_got)
    small = add_up(queue, small, small_got, F32)
    return (
        result[None],
        grad_tokens[None],
        small[0],
        small[1],
        grad_qkv,
        small[4, :HD],
        small[5, :HD],
        grad_out,
        small[2],
        small[3],
        grad_u,
        grad_d.T,
    )


def solution(mesh):
    rows = P("dp", "tensor", None)
    wide = P("dp", "tensor")
    tall = P("tensor", "dp")
    qkv = P("dp", None, "tensor")
    in_specs = (rows, P("dp", None), P(), P(), qkv, P(), P(), tall, P(), P(), wide, tall, rows)
    out_specs = (rows, rows, P(), P(), qkv, P(), P(), tall, P(), P(), wide, tall)
    return jax.shard_map(per_device, mesh=mesh, in_specs=in_specs, out_specs=out_specs, check_vma=False)
```

```python
import jax
import jax.numpy as jnp
from jax import lax
from jax.experimental import pallas as pl
from jax.experimental.pallas import tpu as pltpu
from jax.sharding import PartitionSpec as P

HD = 64
EPSILON = 1e-6
LOG2E = 1.4426950408889634
QSCALE = LOG2E / 8.0
BIG = 256.0
F32 = jnp.float32
BF = jnp.bfloat16
BQ = 512
BK_FWD = 512
BK_BWD = 256
CHUNK = 512


def nn(a, b):
    return lax.dot_general(a, b, (((1,), (0,)), ((), ())), preferred_element_type=F32)


def nt(a, b):
    return lax.dot_general(a, b, (((1,), (1,)), ((), ())), preferred_element_type=F32)


class Queue:
    def __init__(self):
        self.last = ()

    def __call__(self, name, kern, inputs, outs, scalars=(), scratch=(), vmem=12, us=0, fetched=()):
        count = len(scalars) + len(inputs)
        deps = self.last
        skip = count + len(fetched) + len(deps)

        def body(*refs):
            if not fetched:
                return kern(*refs[:count], *refs[skip:])
            copies = refs[-1 - len(fetched) : -1]
            moves = [pltpu.make_async_copy(a, b, refs[-1].at[i]) for i, (a, b) in enumerate(zip(refs[count:skip], copies))]
            for move in moves:
                move.start()
            for move in moves:
                move.wait()
            kern(*refs[:count], *refs[skip:-1])

        space = lambda where: pl.BlockSpec(memory_space=where)
        landing = [pltpu.VMEM(a.shape, a.dtype) for a in fetched]
        if fetched:
            landing.append(pltpu.SemaphoreType.DMA((len(fetched),)))
        res = pl.pallas_call(
            body,
            out_shape=tuple(jax.ShapeDtypeStruct(s, t) for s, t in outs),
            in_specs=[space(pltpu.SMEM)] * len(scalars) + [space(pltpu.VMEM)] * len(inputs) + [space(pl.ANY)] * (len(fetched) + len(deps)),
            out_specs=tuple(space(pltpu.VMEM) for _ in outs),
            scratch_shapes=[*scratch, *landing],
            compiler_params=pltpu.CompilerParams(vmem_limit_bytes=vmem * 2**20),
            cost_estimate=pl.CostEstimate(flops=int(us * 50e8 / 50), bytes_accessed=0, transcendentals=0),
            name=name,
        )(*scalars, *inputs, *fetched, *deps)
        self.last = (res[0],)
        return res


def hat_of(values):
    center = values - jnp.mean(values, axis=-1, keepdims=True)
    inv = lax.rsqrt(jnp.mean(center * center, axis=-1, keepdims=True) + EPSILON)
    return center * inv, inv


def hat_back(grad, gain, hat, inv):
    u = grad * gain
    return inv * (u - jnp.mean(u, axis=-1, keepdims=True) - hat * jnp.mean(u * hat, axis=-1, keepdims=True))


STEP = 128


def each(rows, body):
    pl.loop(0, rows // STEP)(lambda i: body(pl.ds(pl.multiple_of(i * STEP, STEP), STEP)))


def norm_pair(queue, one, two, gain, bias, us=0):
    slots, width = one.shape

    def kern(one_ref, two_ref, gain_ref, bias_ref, out_ref):
        for i, ref in enumerate((one_ref, two_ref)):

            def body(s, i=i, ref=ref):
                hat, _ = hat_of(ref[s, :].astype(F32))
                at = pl.ds(pl.multiple_of(s.start + i * slots, STEP), STEP)
                out_ref[at, :] = (hat * gain_ref[...] + bias_ref[...]).astype(BF)

            each(slots, body)

    return queue("norm_pair", kern, (one, two, gain, bias), [((2 * slots, width), BF)], us=us)[0]


def norm_rows(x):
    c = x - jnp.mean(x, axis=0, keepdims=True)
    inv = lax.rsqrt(jnp.mean(c * c, axis=0, keepdims=True) + EPSILON)
    return c * inv, inv


def split3(v):
    hi = v.astype(BF).astype(F32)
    rest = v - hi
    mid = rest.astype(BF).astype(F32)
    return hi, mid, rest - mid


def attn_fwd(queue, tensor, ids, own, oth, w, lo, fq, fk, qg, kg):
    half, width = own.shape
    slots = 2 * half
    cols = (w.shape[1] - lo) // 3
    heads = cols // HD
    nk = slots // BK_FWD

    def kern(t_ref, ids_ref, own_ref, oth_ref, w_ref, fq_ref, fk_ref, qg_ref, kg_ref, att_ref, lse_ref, q_ref, k_ref, v_ref, wt_ref, qi_ref, ki_ref, kt, qn, vn, n_ref, l_ref):
        list_blocks(t_ref, ids_ref, slots, BK_FWD, n_ref, l_ref)
        q_gain, k_gain = column(qg_ref[...]), column(kg_ref[...])
        ones = jnp.where(lax.broadcasted_iota(jnp.int32, (HD, CHUNK), 0) == 0, 1.0, 0.0).astype(F32)
        wt_ref[...] = w_ref[:, lo:].T
        for c in range(slots // CHUNK):
            s = slice(c * CHUNK, (c + 1) * CHUNK)
            mine = c * CHUNK < half
            x = own_ref[s, :] if mine else oth_ref[c * CHUNK - half : (c + 1) * CHUNK - half, :]
            raw = nt(wt_ref[: 2 * cols], x)
            v_ref[:, s] = raw[cols:].astype(BF)
            for h in range(heads):
                r = slice(h * HD, (h + 1) * HD)
                kn, ki_ref[h : h + 1, s] = norm_rows(raw[r])
                kn = (kn * k_gain).astype(BF)
                k_ref[r, s] = kn
                kt[h, :HD, s] = kn
                kt[h, HD:, s] = fk_ref[:, s]
                vn[h, s, :] = jnp.concatenate([raw[cols + h * HD : cols + (h + 1) * HD], ones], axis=0).T.astype(BF)
            if mine:
                raw = nt(wt_ref[2 * cols :], x)
                for h in range(heads):
                    r = slice(h * HD, (h + 1) * HD)
                    qh, qi_ref[h : h + 1, s] = norm_rows(raw[r])
                    qh = qh * (q_gain * QSCALE)
                    q_ref[r, s] = qh.astype(BF)
                    qa = jnp.concatenate([qh, fq_ref[:, s].astype(F32)], axis=0)
                    qn[h, s, :] = qa.T.astype(BF)
        for qb in range(half // BQ):
            s = slice(qb * BQ, (qb + 1) * BQ)

            def body(i, accs, qb=qb, s=s):
                ks = pl.ds(pl.multiple_of(l_ref[qb * nk + i] * BK_FWD, BK_FWD), BK_FWD)
                out = []
                for h in range(heads):
                    p = jnp.exp2(nn(qn[h, s, :], kt[h, :, ks])).astype(BF)
                    out.append(accs[h] + nn(p, vn[h, ks, :]))
                return tuple(out)

            accs = lax.fori_loop(0, n_ref[qb], body, tuple(jnp.zeros((BQ, 2 * HD), F32) for _ in range(heads)))
            for h in range(heads):
                t = accs[h].T
                total = t[HD : HD + 1]
                att_ref[h * HD : (h + 1) * HD, s] = (t[:HD] / total).astype(BF)
                lse_ref[h : h + 1, s] = jnp.log2(total)

    return queue(
        "attn_fwd",
        kern,
        (own, oth, w, fq, fk, qg, kg),
        [
            ((cols, half), BF),
            ((heads, half), F32),
            ((cols, half), BF),
            ((cols, slots), BF),
            ((cols, slots), BF),
            ((3 * cols, width), BF),
            ((heads, half), F32),
            ((heads, slots), F32),
        ],
        scalars=(tensor, ids),
        scratch=[pltpu.VMEM((heads, 2 * HD, slots), BF), pltpu.VMEM((heads, half, 2 * HD), BF), pltpu.VMEM((heads, slots, 2 * HD), BF), pltpu.SMEM((half // BQ,), jnp.int32), pltpu.SMEM((half // BQ * nk + 1,), jnp.int32)],
        vmem=20,
        us=50,
    )


def attn_bwd(queue, tensor, ids, q, k, v, qi, ki, att, lse, branch, wot, lo, fq, fk, qg, kg, us):
    cols, half = q.shape
    slots = k.shape[1]
    heads = cols // HD
    nk = slots // BK_BWD

    def kern(t_ref, ids_ref, q_ref, k_ref, v_ref, qi_ref, ki_ref, att_ref, lse_ref, b0_ref, b1_ref, wot_ref, fq_ref, fk_ref, qg_ref, kg_ref, g_ref, gq_ref, gains_ref, kn, vn, qt, qn, dt, dn, dqt, dk, dv, n_ref, l_ref):
        list_blocks(t_ref, ids_ref, slots, BK_BWD, n_ref, l_ref)
        q_gain, k_gain = column(qg_ref[...]), column(kg_ref[...])
        row = lax.broadcasted_iota(jnp.int32, (HD, CHUNK), 0)
        three = jnp.where(row < 3, 1.0, 0.0).astype(F32)
        for c in range(slots // CHUNK):
            s = slice(c * CHUNK, (c + 1) * CHUNK)
            for h in range(heads):
                r = slice(h * HD, (h + 1) * HD)
                full = jnp.concatenate([k_ref[r, s], fk_ref[:, s]], axis=0).astype(F32)
                kn[h, s, :] = full.T.astype(BF)
                vn[h, s, :] = jnp.concatenate([v_ref[r, s].astype(F32), three], axis=0).T.astype(BF)
                dk[h, s, :] = jnp.zeros((CHUNK, 2 * HD), F32)
                dv[h, s, :] = jnp.zeros((CHUNK, 2 * HD), F32)
        for c in range(half // CHUNK):
            s = slice(c * CHUNK, (c + 1) * CHUNK)
            grad = nt(wot_ref[lo : lo + cols], (b0_ref if c == 0 else b1_ref)[...]).astype(BF).astype(F32)
            for h in range(heads):
                r = slice(h * HD, (h + 1) * HD)
                a, b, d = split3(-lse_ref[h : h + 1, s])
                f = fq_ref[:, s].astype(F32)
                f = jnp.where(row == 33, a, jnp.where(row == 34, b, jnp.where(row == 35, d, f)))
                full = jnp.concatenate([q_ref[r, s].astype(F32), f], axis=0)
                qt[h, :, s] = full.astype(BF)
                qn[h, s, :] = full.T.astype(BF)
                a, b, d = split3(-jnp.sum(grad[r] * att_ref[r, s].astype(F32), axis=0, keepdims=True))
                f = jnp.where(row == 0, a, jnp.where(row == 1, b, jnp.where(row == 2, d, 0.0)))
                full = jnp.concatenate([grad[r], f], axis=0)
                dt[h, :, s] = full.astype(BF)
                dn[h, s, :] = full.T.astype(BF)
        for qb in range(half // BQ):
            s = slice(qb * BQ, (qb + 1) * BQ)

            def body(i, accs, qb=qb, s=s):
                ks = pl.ds(pl.multiple_of(l_ref[qb * nk + i] * BK_BWD, BK_BWD), BK_BWD)
                out = []
                for h in range(heads):
                    p = jnp.exp2(nn(kn[h, ks, :], qt[h, :, s]))
                    ds = (p * nn(vn[h, ks, :], dt[h, :, s])).astype(BF)
                    dv[h, ks, :] += nn(p.astype(BF), dn[h, s, :])
                    dk[h, ks, :] += nn(ds, qn[h, s, :])
                    out.append(accs[h] + nn(k_ref[h * HD : (h + 1) * HD, ks], ds))
                return tuple(out)

            accs = lax.fori_loop(0, n_ref[qb], body, tuple(jnp.zeros((HD, BQ), F32) for _ in range(heads)))
            for h in range(heads):
                dqt[h, :, s] = accs[h]

        def back(grad, gain, hat, inv):
            u = grad * gain
            out = inv * (u - jnp.mean(u, axis=0, keepdims=True) - hat * jnp.mean(u * hat, axis=0, keepdims=True))
            return out.astype(BF), jnp.sum(grad * hat, axis=1, keepdims=True)

        sum_q = jnp.zeros((HD, 1), F32)
        sum_k = jnp.zeros((HD, 1), F32)
        for h in range(heads):
            r = slice(h * HD, (h + 1) * HD)
            for c in range(slots // CHUNK):
                s = slice(c * CHUNK, (c + 1) * CHUNK)
                g_ref[r, s], more = back(dk[h, s, :].T[:HD] * (1.0 / LOG2E), k_gain, k_ref[r, s].astype(F32) * (1.0 / k_gain), ki_ref[h : h + 1, s])
                sum_k += more
                g_ref[cols + h * HD : cols + (h + 1) * HD, s] = dv[h, s, :].T[:HD].astype(BF)
            for c in range(half // CHUNK):
                s = slice(c * CHUNK, (c + 1) * CHUNK)
                gq_ref[r, s], more = back(dqt[h, :, s] * 0.125, q_gain, q_ref[r, s].astype(F32) * (1.0 / (q_gain * QSCALE)), qi_ref[h : h + 1, s])
                sum_q += more
        gains_ref[:, :1] = sum_q
        gains_ref[:, 1:] = sum_k

    big = (heads, slots, 2 * HD)
    small = (heads, half, 2 * HD)
    flat = (heads, 2 * HD, half)
    return queue(
        "attn_bwd",
        kern,
        (q, k, v, qi, ki, att, lse, *branch, wot, fq, fk, qg, kg),
        [((2 * cols, slots), BF), ((cols, half), BF), ((HD, 2), F32)],
        scalars=(tensor, ids),
        scratch=[
            pltpu.VMEM(big, BF),
            pltpu.VMEM(big, BF),
            pltpu.VMEM(flat, BF),
            pltpu.VMEM(small, BF),
            pltpu.VMEM(flat, BF),
            pltpu.VMEM(small, BF),
            pltpu.VMEM((heads, HD, half), F32),
            pltpu.VMEM(big, F32),
            pltpu.VMEM(big, F32),
            pltpu.SMEM((half // BQ,), jnp.int32),
            pltpu.SMEM((half // BQ * nk + 1,), jnp.int32),
        ],
        vmem=28,
        us=us,
    )


def features(queue, ids, tensor):
    parts, slots = ids.shape

    def kern(t_ref, ids_ref, fq_ref, fk_ref):
        row = lax.broadcasted_iota(jnp.int32, (HD, slots), 0)
        for i in range(parts):
            s = slice(i * slots, (i + 1) * slots)
            hot = ids_ref[pl.ds(t_ref[0] ^ i, 1), :] + 1 == row
            ones = (row >= 32) & (row < 36)
            fk_ref[:, s] = jnp.where((hot & (row < 32)) | ones, 1.0, 0.0).astype(BF)
            if i < 2:
                fq_ref[:, s] = jnp.where(hot & (row < 32), BIG, jnp.where(row == 32, -BIG, 0.0)).astype(BF)

    outs = [((HD, 2 * slots), BF), ((HD, parts * slots), BF)]
    return queue("features", kern, (ids,), outs, scalars=(tensor,), us=50)


def list_blocks(t_ref, ids_ref, slots, size, n_ref, l_ref):
    share = ids_ref.shape[0] // 4

    def ends(block, length):
        at = block * length
        at = (t_ref[0] ^ (at // share)) * share + at % share
        first, last = ids_ref[at], ids_ref[at + length - 1]
        return jnp.where(first < 0, 99, first), jnp.where(last < 0, 99, last)

    nk = slots // size
    keys = [ends(kb, size) for kb in range(nk)]
    for qb in range(slots // 2 // BQ):
        first, last = ends(qb, BQ)
        n = jnp.int32(0)
        for kb, (low, high) in enumerate(keys):
            l_ref[qb * nk + n] = kb
            n += ((first <= high) & (low <= last)).astype(jnp.int32)
        n_ref[qb] = n


def column(row):
    n = row.shape[1]
    same = lax.broadcasted_iota(jnp.int32, (n, n), 0) == lax.broadcasted_iota(jnp.int32, (n, n), 1)
    return jnp.sum(jnp.where(same, row, 0.0), axis=1, keepdims=True)


def gelu_pair(v):
    t = 1.0 / (1.0 + (0.3275911 * 0.5**0.5) * jnp.abs(v))
    e = jnp.exp2(v * v * (-0.5 * LOG2E))
    poly = ((((0.5307027145 * t - 0.7265760135) * t + 0.7107068705) * t - 0.142248368) * t + 0.127414796) * t
    tail = poly * e
    phi = jnp.where(v < 0, tail, 1.0 - tail)
    return v * phi, phi + v * e * 0.3989422804014327


def split_store(value, bit, keep, send, blocks, lead=(), at=slice(None)):
    rows = value.shape[0] // blocks
    value = value.astype(BF)
    for b in range(2):

        @pl.when(bit == b)
        def _(b=b):
            for j in range(blocks):
                part = value[j * rows : (j + 1) * rows]
                if j % 2 == b:
                    keep[(*lead, j // 2, slice(None), at)] = part
                else:
                    send[(*lead, j // 2, slice(None), at)] = part


COLS = 256
PLACES = ((0, 0, 0, 256), (256, 1, 0, 256), (512, 0, 256, 128), (640, 1, 256, 128))
HALF_COLS = 384


def mlp(queue, xs, gs, both, bit, blocks, slope=None):
    half, width = xs[0].shape
    cols = both.shape[2] // 2
    forward = slope is None
    rows = 256

    def kern(bit_ref, x0, x1, g0, g1, w_ref, *rest):
        rest = list(rest)
        if forward:
            hid = rest.pop(0)
        slope_ref = rest.pop(0)
        if forward:
            keep_a, send_a, keep_b, send_b, turned = rest
        else:
            keep_a, send_a, keep_b, send_b, own_ref, out_ref, hid, turned = rest
        left = (g0, g1) if forward else (x0, x1)
        feed = (x0, x1) if forward else (g0, g1)
        w_in, w_out = (0, cols) if forward else (cols, 0)
        for i, ref in enumerate(left):
            turned[:, i * half : (i + 1) * half] = ref[...].T

        def units(r, i, c, lo):
            o = slice(lo + i * half, lo + i * half + rows)
            at = slice(c, c + COLS) if isinstance(c, int) else pl.ds(pl.multiple_of(c, COLS), COLS)
            w_at = slice(w_in + c, w_in + c + COLS) if isinstance(c, int) else pl.ds(pl.multiple_of(w_in + c, COLS), COLS)
            value = nn(feed[i][lo : lo + rows, :], w_ref[r, :, w_at])
            if forward:
                value, grad = gelu_pair(value)
                slope_ref[r, o, at] = grad.astype(BF)
            else:
                value = value * slope_ref[r, o, at].astype(F32)
            hid[r, o, at] = value.astype(BF)

        def weights(r, c):
            value = nn(turned[...], hid[r, :, c : c + COLS])
            for first, part, to, count in PLACES:
                if c <= first < c + COLS:
                    piece = value[:, first - c : first - c + count]
                    if part == 0:
                        split_store(piece, bit_ref[0], keep_a, send_a, blocks, (r,), slice(to, to + count))
                    else:
                        (send_b if r else keep_b)[:, to : to + count] = piece.astype(BF)

        spots = [(i, lo) for i in range(2) for lo in range(0, half, rows)]

        if forward:

            @pl.loop(0, cols // COLS)
            def _(k):
                for i, lo in spots:
                    units(0, i, k * COLS, lo)

        else:
            for c in range(0, cols, COLS):
                for i, lo in spots:
                    units(0, i, c, lo)

        for c in range(0, cols, COLS):
            for i, lo in spots:
                units(1, i, c, lo)
            weights(0, c)
        for c in range(0, cols, COLS):
            weights(1, c)
        if not forward:
            shares(hid, w_ref, slice(w_out, w_out + cols), own_ref, out_ref)

    part_a = ((2, blocks // 2, width // blocks, HALF_COLS), BF)
    part_b = ((width, cols - HALF_COLS), BF)
    outs = [part_a, part_a, part_b, part_b]
    inputs = [*xs, *gs, both]
    flat = (2, 2 * half, cols)
    scratch = [pltpu.VMEM((width, 2 * half), BF)]
    if forward:
        outs = [(flat, BF), (flat, BF), *outs]
    else:
        inputs.append(slope)
        outs += [((half, width), F32), ((half, width), BF)]
        scratch.insert(0, pltpu.VMEM(flat, BF))
    return queue("mlp_fwd" if forward else "mlp_bwd", kern, inputs, outs, scalars=(bit,), scratch=scratch, vmem=28, us=0)


def shares(hid, w_ref, at, own_ref, out_ref):
    half = own_ref.shape[0]
    rows = 256
    for i, out in enumerate((own_ref, out_ref)):
        for lo in range(0, half, rows):
            o = slice(lo + i * half, lo + i * half + rows)
            out[lo : lo + rows, :] = (nt(hid[0, o, :], w_ref[0, :, at]) + nt(hid[1, o, :], w_ref[1, :, at])).astype(out.dtype)


def mlp_out(queue, hid, both, us):
    _, slots, cols = hid.shape
    width = both.shape[1]

    def kern(hid_ref, w_ref, own_ref, out_ref):
        shares(hid_ref, w_ref, slice(cols, 2 * cols), own_ref, out_ref)

    outs = [((slots // 2, width), F32), ((slots // 2, width), BF)]
    return queue("mlp_out", kern, (hid, both), outs, us=us)


def out_proj(queue, atts, w, lo):
    cols, slots = atts[0].shape
    width = w.shape[0]
    half = slots // 2

    def kern(a0, a1, w_ref, own_ref, send_ref, wot_ref):
        wot_ref[...] = w_ref[:, :lo].T
        for i, out in enumerate((own_ref, send_ref)):
            s = slice(i * half, (i + 1) * half)
            both = jnp.concatenate([a0[:, s], a1[:, s]], axis=0)
            out[...] = nn(both.T, wot_ref[...]).astype(out.dtype)

    outs = [((half, width), F32), ((half, width), BF), ((lo, width), BF)]
    return queue("out_proj", kern, (*atts, w), outs)


def middle_norm(queue, own, got, tok, gain, bias):
    slots, width = own.shape

    def kern(own_ref, got_ref, tok_ref, gain_ref, bias_ref, mid_ref, out_ref):
        def body(s):
            mid = tok_ref[s, :].astype(F32) + own_ref[s, :] + got_ref[s, :].astype(F32)
            mid_ref[s, :] = mid
            hat, _ = hat_of(mid)
            out_ref[s, :] = (hat * gain_ref[...] + bias_ref[...]).astype(BF)

        each(slots, body)

    outs = [((slots, width), F32), ((slots, width), BF)]
    return queue("middle_norm", kern, (own, got, tok, gain, bias), outs, us=50)


def middle_back(queue, own, got, mid, cot, gain, branch_own, branch_got):
    slots, width = own.shape

    def kern(own_ref, got_ref, mid_ref, cot_ref, gain_ref, bo_ref, bg_ref, grad_ref, out_ref, sums_ref, result_ref):
        sums_ref[...] = jnp.zeros_like(sums_ref)

        def body(s):
            grad = own_ref[s, :] + got_ref[s, :].astype(F32)
            mid = mid_ref[s, :]
            result_ref[s, :] = (mid + bo_ref[s, :] + bg_ref[s, :].astype(F32)).astype(BF)
            hat, inv = hat_of(mid)
            sums_ref[0:1] += jnp.sum(grad * hat, axis=0, keepdims=True)
            sums_ref[1:2] += jnp.sum(grad, axis=0, keepdims=True)
            grad = cot_ref[s, :].astype(F32) + hat_back(grad, gain_ref[...], hat, inv)
            grad_ref[s, :] = grad
            out_ref[s, :] = grad.astype(BF)

        each(slots, body)

    outs = [((slots, width), F32), ((slots, width), BF), ((2, width), F32), ((slots, width), BF)]
    return queue("middle_back", kern, (own, got, mid, cot, gain, branch_own, branch_got), outs, us=50)


def proj_grad(queue, g, gq, own, oth, wt, bit, blocks, prev=(), atts=(), branch=()):
    two, slots = g.shape
    cols, half = gq.shape
    width = own.shape[1]
    block = half // 2
    lead = cols * len(atts)

    def kern(bit_ref, g_ref, gq_ref, own_ref, oth_ref, wt_ref, *rest):
        rest = list(rest)
        prev_refs = [rest.pop(0) for _ in prev]
        att_refs = [rest.pop(0) for _ in atts]
        branch_refs = [rest.pop(0) for _ in branch]
        keep_ref, send_ref = rest[:2]
        outs = rest[2:]
        for i in reversed(range(4)):
            s = slice(i * block, (i + 1) * block)
            value = nn(g_ref[:, s].T, wt_ref[:two])
            if i < 2:
                value += nn(gq_ref[:, s].T, wt_ref[two:])
            if prev_refs:
                value += prev_refs[i % 2][i // 2].astype(F32)
            outs[i % 2][i // 2] = value.astype(BF)
        parts = []
        for att in att_refs:
            parts.append(nn(att[:, :block], branch_refs[0][...]) + nn(att[:, block:], branch_refs[1][...]))
        parts.append(nn(g_ref[:, :half], own_ref[...]) + nn(g_ref[:, half:], oth_ref[...]))
        parts.append(nn(gq_ref[...], own_ref[...]))
        split_store(jnp.concatenate(parts, axis=0).T, bit_ref[0], keep_ref, send_ref, blocks)

    share = ((blocks // 2, width // blocks, lead + two + cols), BF)
    return queue(
        "proj_grad",
        kern,
        (g, gq, own, oth, wt, *prev, *atts, *branch),
        [share, share] + [((2, block, width), BF)] * 2,
        scalars=(bit,),
        vmem=22,
        us=50,
    )


def norm_sums(queue, grads, toks):
    slots, width = toks[0].shape

    def kern(*refs):
        sums_ref = refs[2]
        sums_ref[...] = jnp.zeros_like(sums_ref)

        def body(s):
            first = jnp.zeros((1, width), F32)
            second = jnp.zeros((1, width), F32)
            for i, tok_ref in enumerate(refs[3:]):
                grad = refs[i % 2][i // 2, s, :].astype(F32)
                hat, _ = hat_of(tok_ref[s, :].astype(F32))
                first += jnp.sum(grad * hat, axis=0, keepdims=True)
                second += jnp.sum(grad, axis=0, keepdims=True)
            sums_ref[0:1] += first
            sums_ref[1:2] += second

        each(slots, body)

    return queue("norm_sums", kern, grads, [((2, width), F32)], vmem=14, fetched=toks)[0]


def tokens_back(queue, own, got_x, tok, gain, mid):
    slots, width = tok.shape

    def kern(own_ref, x_ref, tok_ref, gain_ref, mid_ref, out_ref):
        def body(s):
            hat, inv = hat_of(tok_ref[s, :].astype(F32))
            grad = own_ref[s, :] + x_ref[s, :].astype(F32)
            out_ref[s, :] = (mid_ref[s, :] + hat_back(grad, gain_ref[...], hat, inv)).astype(BF)

        each(slots, body)

    return queue("tokens_back", kern, (own, got_x, tok, gain, mid), [((slots, width), BF)])[0]


def last_sum(queue, kept, got, lead, across):
    _, rows, _ = kept.shape
    cols = lead.shape[1]

    def kern(kept_ref, got_ref, lead_ref, across_ref, out_ref, qkv_ref):
        out_ref[...] = (lead_ref[...] + across_ref[:, :cols].astype(F32)).T
        value = kept_ref[0] + got_ref[0].astype(F32) + across_ref[:, cols:].astype(F32)
        for i in range(3):
            lo = cols * (2, 0, 1)[i]
            qkv_ref[:, i, :] = value[:, lo : lo + cols]

    return queue("last_sum", kern, (kept, got, lead, across), [((cols, rows), F32), ((rows, 3, cols), F32)])


def slot_sums(queue, kept, got):
    _, slots, width = kept.shape

    def kern(kept_ref, got_ref, across, own):
        across[...] = (kept_ref[1].astype(F32) + got_ref[1].astype(F32)).astype(BF)
        own[...] = kept_ref[0].astype(F32) + got_ref[0].astype(F32)

    return queue("slot_sums", kern, (kept, got), [((slots, width), BF), ((slots, width), F32)])


def gain_rows(queue, one, two, width, us):
    def kern(a, b, out):
        value = (a[...] + b[...]).T
        out[...] = jnp.concatenate([value, jnp.zeros((2, width - HD), F32)], axis=1)

    return queue("gain_rows", kern, (one, two), [((2, width), F32)], us=us)[0]


def add_up(queue, one, two, dtype, us=0):
    def kern(a, b, out):
        out[...] = (a[...].astype(F32) + b[...].astype(F32)).astype(dtype)

    return queue("add_up", kern, (one, two), [(one.shape, dtype)], us=us)[0]


def side_by_side(queue, *arrays, us=0):
    edges = [0]
    for a in arrays:
        edges.append(edges[-1] + a.shape[1])

    def kern(*refs):
        for ref, lo, hi in zip(refs, edges, edges[1:]):
            refs[-1][:, lo:hi] = ref[...]

    return queue("side_by_side", kern, arrays, [((arrays[0].shape[0], edges[-1]), BF)], us=us)[0]


def pair_dp(queue, held, got, bit, cuts=None):
    m, rows, cols = held.shape
    cuts = [0, rows] if cuts is None else [0, *cuts, rows]

    def kern(bit_ref, held_ref, got_ref, *outs):
        bit = bit_ref[0]
        for i in range(m):
            for lo, hi, out in zip(cuts, cuts[1:], outs):
                out[2 * i + bit] = held_ref[i, lo:hi]
                out[2 * i + 1 - bit] = got_ref[i, lo:hi]

    outs = [((2 * m, hi - lo, cols), held.dtype) for lo, hi in zip(cuts, cuts[1:])]
    return queue("pair_dp", kern, (held, got), outs, scalars=(bit,))


def pair_both(queue, part_a, got_a, part_b, got_b, bit):
    m, rows_a, cols = part_a.shape
    rows_b = part_b.shape[1]

    def kern(bit_ref, a, ga, b, gb, out_a, out_b):
        bit = bit_ref[0]
        out_a[0] = a[...]
        out_a[1] = ga[...]
        for i in range(m):
            out_b[i, bit] = b[i]
            out_b[i, 1 - bit] = gb[i]

    outs = [((2, m, rows_a, cols), BF), ((m, 2, rows_b, cols), BF)]
    return queue("pair_both", kern, (part_a, got_a, part_b, got_b), outs, scalars=(bit,))


def pair_last(queue, part_a, got_a, part_b, got_b, bit):
    _, m, rows_a, cols = part_a.shape
    rows_b = part_b.shape[2]

    def kern(bit_ref, a, ga, b, gb, out):
        bit = bit_ref[0]
        for i in range(m):
            for t in range(2):
                out[t, i, bit, :rows_a] = a[t, i]
                out[t, i, 1 - bit, :rows_a] = ga[t, i]
            for y in range(2):
                out[0, i, y, rows_a:] = b[i, y]
                out[1, i, y, rows_a:] = gb[i, y]

    outs = [((2, m, 2, rows_a + rows_b, cols), BF)]
    (res,) = queue("pair_last", kern, (part_a, got_a, part_b, got_b), outs, scalars=(bit,))
    return res.reshape(2, 2 * m * (rows_a + rows_b), cols)


def fold_dp(queue, kept, got, bit):
    n, rows, cols = kept.shape

    def kern(bit_ref, kept_ref, got_ref, keep, send):
        bit = bit_ref[0]
        for i in range(n // 2):
            keep[i] = kept_ref[2 * i + bit].astype(F32) + got_ref[2 * i + bit].astype(F32)
            send[i] = (kept_ref[2 * i + 1 - bit].astype(F32) + got_ref[2 * i + 1 - bit].astype(F32)).astype(BF)

    outs = [((n // 2, rows, cols), F32), ((n // 2, rows, cols), BF)]
    return queue("fold_dp", kern, (kept, got), outs, scalars=(bit,))


def fold_first(queue, keep_a, got_a, keep_b, got_b, next_a, next_b, bit, us):
    _, n, rows, cols = keep_a.shape

    def kern(bit_ref, ka, ga, kb, gb, na, nb, x_msg, y_msg, keep_a, keep_b):
        bit = bit_ref[0]
        keep_a[...] = ka[0].astype(F32) + ga[0].astype(F32)
        x_msg[:n] = (ka[1].astype(F32) + ga[1].astype(F32)).astype(BF)
        x_msg[n:] = nb[...]
        for i in range(n):
            keep_b[i] = kb[2 * i + bit].astype(F32) + gb[2 * i + bit].astype(F32)
            y_msg[i] = (kb[2 * i + 1 - bit].astype(F32) + gb[2 * i + 1 - bit].astype(F32)).astype(BF)
            y_msg[n + i] = na[0, i]
            y_msg[2 * n + i] = na[1, i]

    outs = [((3 * n, rows, cols), BF)] * 2 + [((n, rows, cols), F32)] * 2
    return queue("fold_first", kern, (keep_a, got_a, keep_b, got_b, next_a, next_b), outs, scalars=(bit,), us=us)


def fold_second(queue, keep_a, keep_b, next_a, next_b, x_got, y_got, bit, far_bit):
    n, rows, cols = keep_a.shape

    def kern(bit_ref, far_ref, ka, kb, na, nb, xg, yg, keep, send, keep_na, send_na, keep_nb, send_nb):
        bit, far = bit_ref[0], far_ref[0]
        for i in range(n // 2):
            for first, part, at, count in PLACES:
                k, g = ((ka, xg), (kb, yg))[part]
                to, at = slice(first, first + count), slice(at, at + count)
                keep[i, :, to] = k[2 * i + far, :, at] + g[2 * i + far, :, at].astype(F32)
                send[i, :, to] = (k[2 * i + 1 - far, :, at] + g[2 * i + 1 - far, :, at].astype(F32)).astype(BF)
        for i in range(n):
            keep_na[i] = na[0, i].astype(F32) + yg[n + i].astype(F32)
            send_na[i] = (na[1, i].astype(F32) + yg[2 * n + i].astype(F32)).astype(BF)
            keep_nb[i] = nb[2 * i + bit].astype(F32) + xg[n + 2 * i + bit].astype(F32)
            send_nb[i] = (nb[2 * i + 1 - bit].astype(F32) + xg[n + 2 * i + 1 - bit].astype(F32)).astype(BF)

    half = (n, rows, cols)
    outs = [((n // 2, rows, 2 * cols), F32), ((n // 2, rows, 2 * cols), BF), (half, F32), (half, BF), (half, F32), (half, BF)]
    arrays = (keep_a, keep_b, next_a, next_b, x_got, y_got)
    return queue("fold_second", kern, arrays, outs, scalars=(bit, far_bit))


def fold_joined(queue, keep_a, got_a, keep_b, got_b, bit):
    n, rows, cols_a = keep_a.shape
    cols = cols_a + keep_b.shape[-1]

    def kern(bit_ref, ka, ga, kb, gb, keep, send):
        bit = bit_ref[0]
        for i in range(n // 2):
            for first, part, at, count in PLACES:
                k, g = ((ka, ga), (kb, gb))[part]
                to, at = slice(first, first + count), slice(at, at + count)
                keep[i, :, to] = k[2 * i + bit, :, at] + g[2 * i + bit, :, at].astype(F32)
                send[i, :, to] = (k[2 * i + 1 - bit, :, at] + g[2 * i + 1 - bit, :, at].astype(F32)).astype(BF)

    outs = [((n // 2, rows, cols), F32), ((n // 2, rows, cols), BF)]
    return queue("fold_joined", kern, (keep_a, got_a, keep_b, got_b), outs, scalars=(bit,))


def sum_x(queue, kept, got, cols):
    _, rows, total = kept.shape

    def kern(kept_ref, got_ref, send, keep):
        value = kept_ref[0] + got_ref[0].astype(F32)
        keep[...] = value[:, :cols]
        send[...] = value[:, cols:].astype(BF)

    return queue("sum_x", kern, (kept, got), [((rows, total - cols), BF), ((rows, cols), F32)])


def swap(values, axis, mask):
    return lax.ppermute(values, axis, [(i, i ^ mask) for i in range(lax.axis_size(axis))])


def swap_core(values):
    return swap(values, "tensor", 1)


def swap_x(values):
    return swap(values, "tensor", 2)


def per_device(tokens, picture_ids, ln1_gain, ln1_bias, w_qkv, q_gain, k_gain, w_out, ln2_gain, ln2_bias, w_up, w_down, cotangent):
    slots, width = tokens.shape[1:]
    local = w_qkv.shape[2]
    n_dp = lax.axis_size("dp")
    rows = width // n_dp
    q_slots = 2 * slots
    tok = tokens[0]
    cot = cotangent[0]
    tensor = lax.axis_index("tensor").reshape(1)
    me = lax.axis_index("dp")
    levels = list(reversed(range(n_dp.bit_length() - 1)))
    far, near = levels[:-1], levels[-1]
    bits = {level: ((me >> level) & 1).reshape(1) for level in levels}
    queue = Queue()
    gain1, bias1, gain2, bias2 = (v.reshape(1, width) for v in (ln1_gain, ln1_bias, ln2_gain, ln2_bias))
    qg, kg = q_gain.reshape(1, HD), k_gain.reshape(1, HD)

    def swap_dp(values, level):
        return swap(values, "dp", 1 << level)

    out_t = w_out.T
    part_0 = jnp.concatenate([w_qkv[:, 1], w_qkv[:, 2], w_qkv[:, 0]], axis=1)
    part_0 = side_by_side(queue, part_0)
    got_0 = swap_dp(part_0[None], far[0])
    ids = picture_ids[0]
    fq, fk = features(queue, ids.reshape(4, slots), tensor)
    got_cols = swap_x(side_by_side(queue, out_t, part_0))
    tok_x = swap_x(side_by_side(queue, tok, us=50))
    tok_c = swap_core(tok)
    cot_c = swap_core(cot)
    both = side_by_side(queue, w_up, w_down.T)[None]
    half = rows // 2
    (part_0,) = pair_dp(queue, part_0[None], got_0, bits[far[0]])
    part_1 = side_by_side(queue, out_t, got_cols)[None]
    got_0 = swap_dp(part_0, levels[1])
    got_1 = swap_dp(part_1, far[0])
    for level, after_it in zip(levels[1:-1], levels[2:]):
        (part_0,) = pair_dp(queue, part_0, got_0, bits[level])
        got_0 = swap_dp(part_0, after_it)
    for level, after_it in zip(levels[:-2], levels[1:-1]):
        (part_1,) = pair_dp(queue, part_1, got_1, bits[level])
        got_1 = swap_dp(part_1, after_it)
    both = side_by_side(queue, both[0])[None]
    got_b = swap_dp(both, far[0])
    own = norm_pair(queue, tok, tok_c, gain1, bias1, us=50)
    (part_1,) = pair_dp(queue, part_1, got_1, bits[levels[-2]])
    got_1 = swap_dp(part_1, levels[-1])
    (w_0,) = pair_dp(queue, part_0, got_0, bits[near])
    w_0 = w_0.reshape(width, 3 * local)
    for level, after_it in zip(far[:-1], far[1:]):
        (both,) = pair_dp(queue, both, got_b, bits[level])
        got_b = swap_dp(both, after_it)
    tok_xc = swap_core(side_by_side(queue, tok_x))
    oth = norm_pair(queue, tok_x, tok_xc, gain1, bias1)
    att_0, lse_0, q_0, k_0, v_0, wt_0, qi_0, ki_0 = attn_fwd(queue, tensor, ids, own, oth, w_0, 0, fq, fk, qg, kg)
    part_a, part_b = pair_dp(queue, both, got_b, bits[far[-1]], (half,))
    got_a, got_b = swap_x(part_a), swap_dp(part_b, near)
    (w_1,) = pair_dp(queue, part_1, got_1, bits[near])
    w_1 = w_1.reshape(width, 5 * local)
    att_1, lse_1, q_1, k_1, v_1, wt_1, qi_1, ki_1 = attn_fwd(queue, tensor, ids, own, oth, w_1, 2 * local, fq, fk, qg, kg)
    part_a, part_b = pair_both(queue, part_a, got_a, part_b, got_b, bits[near])
    got_a, got_b = swap_dp(part_a, near), swap_x(part_b)
    branch_own, branch_send, wot = out_proj(queue, (att_0, att_1), w_1, 2 * local)
    middle, normed = middle_norm(queue, branch_own, swap_core(branch_send), tok, gain2, bias2)
    normed_c = swap_core(normed)
    both = pair_last(queue, part_a, got_a, part_b, got_b, bits[near])

    bit = bits[near]
    rest = levels[::-1][1:]
    xs, gs = (normed, normed_c), (cot, cot_c)
    grid = (n_dp, rows, w_up.shape[1] - HALF_COLS)

    def first_step(parts):
        keep_a, send_a, keep_b, send_b = parts
        return keep_a, swap_dp(send_a, near), keep_b.reshape(grid), swap_x(send_b).reshape(grid)

    def second_step(keep_a, send_a, keep_b, send_b):
        return keep_a, swap_x(send_a), keep_b, swap_dp(send_b, near)

    def next_step(keep, send, level):
        return keep, swap_dp(send, level)

    hid, slope, *parts = mlp(queue, xs, gs, both, bit, n_dp)
    d = first_step(parts)
    mlp_own, mlp_send = mlp_out(queue, hid, both, 50)
    *parts, gn_own, gn_send = mlp(queue, xs, gs, both, bit, n_dp, slope)
    u_keep_a, u_send_a, u_keep_b, u_send_b = parts
    x_msg, y_msg, *d = fold_first(queue, *d, u_send_a, u_send_b.reshape(grid), bit, 50)
    x_got, y_got = swap_x(x_msg), swap_dp(y_msg, near)
    grad_mid, branch, sums2, result = middle_back(
        queue, gn_own, swap_core(gn_send), middle, cot, gain2, mlp_own, swap_core(mlp_send)
    )
    branches = (branch, swap_core(branch))
    g, gq, gains_1 = attn_bwd(queue, tensor, ids, q_1, k_1, v_1, qi_1, ki_1, att_1, lse_1, branches, wot, local, fq, fk, qg, kg, 0)
    *d, u_keep_a, u_send_a, u_keep_b, u_send_b = fold_second(
        queue, *d, u_keep_a, u_keep_b.reshape(grid), x_got, y_got, bit, bits[rest[0]]
    )
    u = second_step(u_keep_a, u_send_a, u_keep_b, u_send_b)
    d = next_step(*d, rest[0])
    a_keep, a_send, *gx = proj_grad(queue, g, gq, own, oth, wt_1, bit, n_dp, atts=(att_0, att_1), branch=branches)
    a = next_step(a_keep, a_send, near)
    u = next_step(*fold_joined(queue, *u, bits[rest[0]]), rest[0])
    d = next_step(*fold_dp(queue, *d, bits[rest[1]]), rest[1])
    g, gq, gains_0 = attn_bwd(queue, tensor, ids, q_0, k_0, v_0, qi_0, ki_0, att_0, lse_0, branches, wot, 0, fq, fk, qg, kg, 50)
    a = next_step(*fold_dp(queue, *a, bits[rest[0]]), rest[0])
    u = next_step(*fold_dp(queue, *u, bits[rest[1]]), rest[1])
    for level in rest[2:]:
        d = next_step(*fold_dp(queue, *d, bits[level]), level)
        u = next_step(*fold_dp(queue, *u, bits[level]), level)
    z_keep, z_send, *gx = proj_grad(queue, g, gq, own, oth, wt_0, bit, n_dp, prev=gx)
    z = next_step(z_keep, z_send, near)
    gx_got = swap_core(gx[1])
    gains = gain_rows(queue, gains_0, gains_1, width, 50)
    across, grad_normed = slot_sums(queue, gx[0], gx_got)
    got = swap_x(across)
    grad_d = add_up(queue, *d, F32).reshape(rows, -1)
    sums1 = norm_sums(queue, gx, (tok, tok_c, tok_x, tok_xc))
    small = jnp.concatenate([sums1, sums2, gains])
    small_got = swap_core(small)
    grad_u = add_up(queue, *u, F32).reshape(rows, -1)
    z = next_step(*fold_dp(queue, *z, bits[rest[0]]), rest[0])
    for level in rest[1:]:
        a = next_step(*fold_dp(queue, *a, bits[level]), level)
    small = add_up(queue, small, small_got, F32)
    small_got = swap_x(small)
    grad_tokens = tokens_back(queue, grad_normed, got, tok, gain1, grad_mid)
    small = add_up(queue, small, small_got, F32)
    small_got = swap_dp(small, near)
    for level in rest[1:]:
        z = next_step(*fold_dp(queue, *z, bits[level]), level)
    a_send, lead = sum_x(queue, *a, local)
    a_got = swap_x(a_send)
    for level in rest:
        small = add_up(queue, small, small_got, F32)
        small_got = swap_dp(small, level)
    grad_out, grad_qkv = last_sum(queue, *z, lead, a_got)
    small = add_up(queue, small, small_got, F32)
    return (
        result[None],
        grad_tokens[None],
        small[0],
        small[1],
        grad_qkv,
        small[4, :HD],
        small[5, :HD],
        grad_out,
        small[2],
        small[3],
        grad_u,
        grad_d.T,
    )


def solution(mesh):
    rows = P("dp", "tensor", None)
    wide = P("dp", "tensor")
    tall = P("tensor", "dp")
    qkv = P("dp", None, "tensor")
    in_specs = (rows, P("dp", None), P(), P(), qkv, P(), P(), tall, P(), P(), wide, tall, rows)
    out_specs = (rows, rows, P(), P(), qkv, P(), P(), tall, P(), P(), wide, tall)
    return jax.shard_map(per_device, mesh=mesh, in_specs=in_specs, out_specs=out_specs, check_vma=False)
```
